32 devices in a mesh: blk: 16 (over z, y, core), inner: 2 (over x).
Axes of the slice: x: 2, y: 2, z: 4, core: 2. Of those that a mesh axis runs over, the one named last changes fastest.
Arguments:
- picture_vectors: bfloat16 [12288, 1152], P(('blk', 'inner')), may hold values from -0.29882812 to 0.29882812
- caption_vectors: bfloat16 [12288, 1152], P(('blk', 'inner')), may hold values from -0.29882812 to 0.29882812
- score_scaling: float32 [], replicated, may hold values from 5 to 20
- score_shift: float32 [], replicated, may hold values from -3 to 0
Outputs:
- loss_rows: float32 [12288], P(('blk', 'inner'))
- image_grad: bfloat16 [12288, 1152], P(('blk', 'inner'))
- text_grad: bfloat16 [12288, 1152], P(('blk', 'inner'))
The draws below stay inside these ranges and needn't reach their ends.
All inputs are finite; a program needn't handle non-finite values.
Results may differ from the reference program's by a relative error of at most 0.0061.
Values may be sent and summed in bfloat16 or wider, within the bound.
No kernel may reach another device: no remote copies, remote signals or barrier semaphores. Data moves between devices by JAX's collectives and lax.ppermute only.
A program may use at most 64 MiB of HBM per device.

```python
import math
import jax
import jax.numpy as jnp
from jax import lax

D = 1152
ROWS_DEV = 384
SPAN = 4
PAIRS = 12288


def level_of(key, extent, shards, smallest, largest):
    def one(dim, parts):
        draws = jax.random.uniform(jax.random.fold_in(jax.random.fold_in(key, 6), dim), (parts,), jnp.float32, smallest / len(shards), largest / len(shards))
        return jnp.repeat(jnp.exp(draws), extent[dim] // parts).reshape((-1,) + (1,) * (len(extent) - dim - 1))

    gain = one(*shards[0])
    for cut in shards[1:]:
        gain = gain * one(*cut)
    return gain


def gaussian(rng, extent, scale, limit, cuts=(), held_as=jnp.bfloat16):
    drawn = scale * jax.random.normal(rng, extent, jnp.float32)
    if cuts:
        drawn = drawn * level_of(rng, extent, cuts, -0.22, 0.18)
    return jnp.clip(drawn, -limit, limit).astype(held_as)


def setup_inputs(seed: int = 0) -> dict:
    splits = jax.random.split(jax.random.key(seed), 5)
    return {
        "picture_vectors": gaussian(splits[0], (PAIRS, D), 0.05, 0.29882812, ((0, 32),)),
        "caption_vectors": gaussian(splits[1], (PAIRS, D), 0.05, 0.29882812, ((0, 32),)),
        "score_scaling": jnp.clip(jnp.exp(jax.random.uniform(splits[2], (), jnp.float32, math.log(5.0), math.log(20.0))), 5.0, 20.0),
        "score_shift": jnp.clip(jax.random.uniform(splits[3], (), jnp.float32, -3.0, 0.0), -3.0, 0.0),
    }


def normalize(block):
    values = block.astype(jnp.float32)
    length = jnp.sqrt(lax.optimization_barrier(jnp.sum(values * values, axis=-1, keepdims=True)) + 1e-06)
    return (values / length, length)

def matrix_entries(picture_summed, caption_summed, score_scaling, score_shift, first_round_indicator):
    match_scores = score_scaling * lax.dot_general(picture_summed, caption_summed, (((1,), (1,)), ((), ())), preferred_element_type=jnp.float32) + score_shift
    rows = match_scores.shape[0]
    if first_round_indicator:
        same = jnp.arange(rows)[:, None] == jnp.arange(rows)[None, :]
        match_sign = jnp.where(same, jnp.float32(1.0), jnp.float32(-1.0))
    else:
        match_sign = jnp.float32(-1.0)
    objective_total = lax.optimization_barrier(jnp.sum(jax.nn.softplus(-match_sign * match_scores), axis=1))
    score_multiplier = (-match_sign * jax.nn.sigmoid(-match_sign * match_scores) * score_scaling).astype(jnp.bfloat16)
    return (objective_total, score_multiplier)

def project(unit, grad, length):
    return (grad - unit * lax.optimization_barrier(jnp.sum(unit * grad, axis=-1, keepdims=True))) / length

def reference(picture_vectors, caption_vectors, score_scaling, score_shift):
    rows = ROWS_DEV
    count = PAIRS // rows
    image_blocks = picture_vectors.reshape(count, rows, D)
    text_blocks = caption_vectors.reshape(count, rows, D)

    def one_block(index):
        image_unit, image_length = normalize(image_blocks[index])
        text_unit, text_length = normalize(text_blocks[index])
        picture_summed = image_unit.astype(jnp.bfloat16)
        caption_summed = text_unit.astype(jnp.bfloat16)
        loss_total = jnp.zeros((rows,), jnp.float32)
        grad_image = jnp.zeros((rows, D), jnp.float32)
        grad_text = jnp.zeros((rows, D), jnp.float32)
        for peer_distance in range(SPAN):
            neighbor_caption = normalize(text_blocks[(index - peer_distance) % count])[0].astype(jnp.bfloat16)
            objective_total, score_multiplier = matrix_entries(picture_summed, neighbor_caption, score_scaling, score_shift, peer_distance == 0)
            loss_total = loss_total + objective_total
            grad_image = grad_image + jnp.dot(score_multiplier, neighbor_caption, preferred_element_type=jnp.float32)
            neighbor_picture = normalize(image_blocks[(index + peer_distance) % count])[0].astype(jnp.bfloat16)
            discarded_output, reverse_multiplier = matrix_entries(neighbor_picture, caption_summed, score_scaling, score_shift, peer_distance == 0)
            grad_text = grad_text + lax.dot_general(reverse_multiplier, neighbor_picture, (((0,), (0,)), ((), ())), preferred_element_type=jnp.float32)
        loss_mean = loss_total / (SPAN * rows)
        image_out = project(image_unit, grad_image, image_length).astype(jnp.bfloat16)
        text_out = project(text_unit, grad_text, text_length).astype(jnp.bfloat16)
        return (loss_mean, image_out, text_out)
    loss_rows, image_grad, text_grad = lax.map(one_block, jnp.arange(count, dtype=jnp.int32))
    return (loss_rows.reshape(PAIRS), image_grad.reshape(PAIRS, D), text_grad.reshape(PAIRS, D))
```

```python
import jax
import jax.numpy as jnp
from jax import lax
from jax.experimental import pallas as pl
from jax.experimental.pallas import tpu as pltpu
from jax.sharding import PartitionSpec as P

SPAN = 4
GROUP = 4
AXES = ("blk", "inner")
F32 = jnp.float32
BF16 = jnp.bfloat16
VMEM_LIMIT = 48 * 1024 * 1024

CORE_SWAP = {0: (2, 0), 2: (0, 0), 1: (3, 0), 3: (1, 0)}
X_SWAP = {0: (1, 0), 1: (0, 0), 2: (3, 0), 3: (2, 0)}
GROUP_SHIFT = {0: (2, -1), 1: (3, -1), 2: (0, 1), 3: (1, 1)}


def send(value, moves):
    count = lax.axis_size(AXES)
    groups = count // GROUP
    pairs = [
        (g * GROUP + role, (g + step) % groups * GROUP + to)
        for g in range(groups)
        for role, (to, step) in moves.items()
    ]
    return lax.ppermute(value, AXES, pairs)


def unit_rows(raw):
    values = raw.astype(F32)
    length = jnp.sqrt(jnp.sum(values * values, axis=1, keepdims=True) + 1e-06)
    return values * (1.0 / length), length


def soft_terms(x):
    small = jnp.exp(-jnp.abs(x))
    below = small * (1.0 - small * (0.5 - small * (1.0 / 3.0)))
    log_part = jnp.where(small < 0.015625, below, jnp.log(1.0 + small))
    plus = jnp.maximum(x, 0.0) + log_part
    sigmoid = jnp.where(x >= 0.0, 1.0, small) / (1.0 + small)
    return plus, sigmoid


def dot_nt(a, b):
    return lax.dot_general(a, b, (((1,), (1,)), ((), ())), preferred_element_type=F32)


def dot_nn(a, b):
    return lax.dot_general(a, b, (((1,), (0,)), ((), ())), preferred_element_type=F32)


def dot_tn(a, b):
    return lax.dot_general(a, b, (((0,), (0,)), ((), ())), preferred_element_type=F32)


def lanes_sum(x):
    total = x[:, :128]
    for start in range(128, x.shape[1], 128):
        total = total + x[:, start : start + 128]
    return total


def pair_step(own, raw, scale, shift):
    block = unit_rows(raw)[0].astype(BF16)
    plus, sigmoid = soft_terms(scale * dot_nt(own, block) + shift)
    coef = (sigmoid * scale).astype(BF16)
    return dot_nn(coef, block), lanes_sum(plus)


def project(raw, grad):
    unit, length = unit_rows(raw)
    return ((grad - unit * jnp.sum(unit * grad, axis=1, keepdims=True)) / length).astype(BF16)


def own_kernel(flag, scal, image, text, z_u, z_w, grad_u, grad_w, loss):
    u_is_image = flag[0] == 1
    scale, shift = scal[0], scal[1]
    zi = unit_rows(image[...])[0].astype(BF16)
    zt = unit_rows(text[...])[0].astype(BF16)
    z_u[...] = jnp.where(u_is_image, zi, zt)
    z_w[...] = jnp.where(u_is_image, zt, zi)
    scores = scale * dot_nt(zi, zt) + shift
    rows = lax.broadcasted_iota(jnp.int32, scores.shape, 0)
    columns = lax.broadcasted_iota(jnp.int32, scores.shape, 1)
    sign = jnp.where(rows == columns, F32(-1.0), F32(1.0))
    plus, sigmoid = soft_terms(sign * scores)
    coef = (sign * sigmoid * scale).astype(BF16)
    loss[...] = lanes_sum(plus)
    grad_image = dot_nn(coef, zt)
    grad_text = dot_tn(coef, zi)
    grad_u[...] = jnp.where(u_is_image, grad_image, grad_text)
    grad_w[...] = jnp.where(u_is_image, grad_text, grad_image)


def near_kernel(flag, scal, b1, b2, b3, z_u, z_w, grad_u, grad_w, loss_in, out_u, out_w, loss):
    scale, shift = scal[0], scal[1]
    u_weight = flag[0].astype(F32)
    term1, loss1 = pair_step(z_w[...], b1[...], scale, shift)
    term2, loss2 = pair_step(z_u[...], b2[...], scale, shift)
    term3, loss3 = pair_step(z_w[...], b3[...], scale, shift)
    out_u[...] = grad_u[...] + term2
    out_w[...] = grad_w[...] + term1 + term3
    loss[...] = loss_in[...] + u_weight * loss2 + (1.0 - u_weight) * (loss1 + loss3)


def u_kernel(flag, scal, b4, b5, z_u, grad_u, loss_in, raw_u, out, loss):
    scale, shift = scal[0], scal[1]
    term4, loss4 = pair_step(z_u[...], b4[...], scale, shift)
    term5, loss5 = pair_step(z_u[...], b5[...], scale, shift)
    loss[...] = loss_in[...] + flag[0].astype(F32) * (loss4 + loss5)
    out[...] = project(raw_u[...], grad_u[...] + term4 + term5)


def w_kernel(flag, scal, b6, z_w, grad_w, loss_in, raw_w, done_u, image_grad, text_grad, loss_rows):
    u_is_image = flag[0] == 1
    scale, shift = scal[0], scal[1]
    term, row_loss = pair_step(z_w[...], b6[...], scale, shift)
    total = loss_in[...] + (1.0 - flag[0].astype(F32)) * row_loss
    per_row = jnp.sum(jnp.transpose(total), axis=0, keepdims=True)
    loss_rows[...] = per_row / (SPAN * total.shape[0])
    done_w = project(raw_w[...], grad_w[...] + term)
    image_grad[...] = jnp.where(u_is_image, done_u[...], done_w)
    text_grad[...] = jnp.where(u_is_image, done_w, done_u[...])


def call(kernel, args, outs, products, name):
    smem = pl.BlockSpec(memory_space=pltpu.SMEM)
    vmem = pl.BlockSpec(memory_space=pltpu.VMEM)
    rows, width = args[2].shape
    size = sum(a.size * a.dtype.itemsize for a in list(args) + list(outs))
    return pl.pallas_call(
        kernel,
        out_shape=outs,
        in_specs=[smem, smem] + [vmem] * (len(args) - 2),
        out_specs=[vmem] * len(outs),
        name=name,
        cost_estimate=pl.CostEstimate(
            flops=2 * rows * rows * width * products, bytes_accessed=size, transcendentals=0
        ),
        compiler_params=pltpu.CompilerParams(vmem_limit_bytes=VMEM_LIMIT),
    )(*args)


def local(image, text, score_scaling, score_shift):
    rows, width = image.shape
    role = lax.axis_index(AXES) % GROUP
    u_is_image = role < 2
    flag = u_is_image.astype(jnp.int32).reshape(1)
    scal = jnp.stack([score_scaling, score_shift])
    u = jnp.where(u_is_image, image, text)
    w = jnp.where(u_is_image, text, image)
    outer = (role == 0) | (role == 3)

    slot1 = send(w, CORE_SWAP)
    slot2 = send(u, GROUP_SHIFT)
    slot3 = send(jnp.where(outer, slot1, u), X_SWAP)
    slot4 = send(slot3, GROUP_SHIFT)
    slot5 = send(jnp.where(outer, w, slot2), X_SWAP)
    slot6 = send(slot5, CORE_SWAP)

    block = jax.ShapeDtypeStruct((rows, width), BF16)
    sums = jax.ShapeDtypeStruct((rows, width), F32)
    partial = jax.ShapeDtypeStruct((rows, 128), F32)
    line = jax.ShapeDtypeStruct((1, rows), F32)

    z_u, z_w, grad_u, grad_w, loss = call(
        own_kernel, (flag, scal, image, text), (block, block, sums, sums, partial), 3, "own_pair"
    )
    grad_u, grad_w, loss = call(
        near_kernel,
        (flag, scal, slot1, slot2, slot3, z_u, z_w, grad_u, grad_w, loss),
        (sums, sums, partial),
        6,
        "near_blocks",
    )
    done_u, loss = call(
        u_kernel, (flag, scal, slot4, slot5, z_u, grad_u, loss, u), (block, partial), 4, "finish_u"
    )
    image_grad, text_grad, loss_rows = call(
        w_kernel, (flag, scal, slot6, z_w, grad_w, loss, w, done_u), (block, block, line), 2, "finish_w"
    )
    return loss_rows.reshape(rows), image_grad, text_grad


def solution(mesh):
    in_specs = (P(AXES, None), P(AXES, None), P(), P())
    out_specs = (P(AXES), P(AXES, None), P(AXES, None))
    return jax.shard_map(local, mesh=mesh, in_specs=in_specs, out_specs=out_specs, check_vma=False)
```

```python
import jax
import jax.numpy as jnp
from jax import lax
from jax.experimental import pallas as pl
from jax.experimental.pallas import tpu as pltpu
from jax.sharding import PartitionSpec as P

SPAN = 4
GROUP = 4
AXES = ("blk", "inner")
F32 = jnp.float32
BF16 = jnp.bfloat16
VMEM_LIMIT = 48 * 1024 * 1024

CORE_SWAP = {0: (2, 0), 2: (0, 0), 1: (3, 0), 3: (1, 0)}
X_SWAP = {0: (1, 0), 1: (0, 0), 2: (3, 0), 3: (2, 0)}
IMAGE_BACK = {1: (0, 0), 2: (1, 0)}
TEXT_ON = {1: (2, 0), 2: (3, 0)}
GROUP_SHIFT = {0: (2, -1), 1: (3, -1), 2: (0, 1), 3: (1, 1)}


def send(value, moves):
    count = lax.axis_size(AXES)
    groups = count // GROUP
    pairs = [
        (g * GROUP + role, (g + step) % groups * GROUP + to)
        for g in range(groups)
        for role, (to, step) in moves.items()
    ]
    return lax.ppermute(value, AXES, pairs)


def unit_rows(raw):
    values = raw.astype(F32)
    length = jnp.sqrt(jnp.sum(values * values, axis=1, keepdims=True) + 1e-06)
    return values * (1.0 / length), length


def sigmoid_of(p):
    whole = 1.0 + p
    guess = pl.reciprocal(whole, approx=True)
    guess = guess * (2.0 - whole * guess)
    return p * (guess * (2.0 - whole * guess))


def log1p_of(p):
    below = p * (1.0 - p * (0.5 - p * (1.0 / 3.0)))
    return jnp.where(p < 0.015625, below, jnp.log(1.0 + p))


def softplus_lanes(p):
    total = None
    parts = [p[:, start : start + 128] for start in range(0, p.shape[1], 128)]
    for first in range(0, len(parts), 3):
        joint = parts[first]
        for part in parts[first + 1 : first + 3]:
            joint = joint + part + joint * part
        value = log1p_of(joint)
        total = value if total is None else total + value
    return total


def dot_nt(a, b):
    return lax.dot_general(a, b, (((1,), (1,)), ((), ())), preferred_element_type=F32)


def dot_nn(a, b):
    return lax.dot_general(a, b, (((1,), (0,)), ((), ())), preferred_element_type=F32)


def dot_tn(a, b):
    return lax.dot_general(a, b, (((0,), (0,)), ((), ())), preferred_element_type=F32)


def pair_step(own, raw, scale, shift):
    block = unit_rows(raw)[0].astype(BF16)
    p = jnp.exp(scale * dot_nt(own, block) + shift)
    coef = (sigmoid_of(p) * scale).astype(BF16)
    return dot_nn(coef, block), softplus_lanes(p)


def project(raw, grad):
    unit, length = unit_rows(raw)
    return ((grad - unit * jnp.sum(unit * grad, axis=1, keepdims=True)) / length).astype(BF16)


def own_kernel(flag, scal, image, text, z_u, z_w, grad_u, grad_w, loss):
    u_is_image = flag[0] == 1
    scale, shift = scal[0], scal[1]
    zi = unit_rows(image[...])[0].astype(BF16)
    zt = unit_rows(text[...])[0].astype(BF16)
    z_u[...] = jnp.where(u_is_image, zi, zt)
    z_w[...] = jnp.where(u_is_image, zt, zi)
    scores = scale * dot_nt(zi, zt) + shift
    rows = lax.broadcasted_iota(jnp.int32, scores.shape, 0)
    columns = lax.broadcasted_iota(jnp.int32, scores.shape, 1)
    sign = jnp.where(rows == columns, F32(-1.0), F32(1.0))
    p = jnp.exp(sign * scores)
    coef = (sign * sigmoid_of(p) * scale).astype(BF16)
    loss[...] = softplus_lanes(p)
    grad_image = dot_nn(coef, zt)
    grad_text = dot_tn(coef, zi)
    grad_u[...] = jnp.where(u_is_image, grad_image, grad_text)
    grad_w[...] = jnp.where(u_is_image, grad_text, grad_image)


def first_kernel(flag, scal, b1, z_w, grad_w, loss_in, out_w, loss):
    scale, shift = scal[0], scal[1]
    term, row_loss = pair_step(z_w[...], b1[...], scale, shift)
    out_w[...] = grad_w[...] + term
    loss[...] = loss_in[...] + (1.0 - flag[0].astype(F32)) * row_loss


def near_kernel(flag, scal, b2, b3, z_u, z_w, grad_u, grad_w, loss_in, out_u, out_w, loss):
    scale, shift = scal[0], scal[1]
    u_weight = flag[0].astype(F32)
    term2, loss2 = pair_step(z_u[...], b2[...], scale, shift)
    term3, loss3 = pair_step(z_w[...], b3[...], scale, shift)
    out_u[...] = grad_u[...] + term2
    out_w[...] = grad_w[...] + term3
    loss[...] = loss_in[...] + u_weight * loss2 + (1.0 - u_weight) * loss3


def u_kernel(flag, scal, b4, b5, z_u, grad_u, loss_in, raw_u, out, loss):
    scale, shift = scal[0], scal[1]
    term4, loss4 = pair_step(z_u[...], b4[...], scale, shift)
    term5, loss5 = pair_step(z_u[...], b5[...], scale, shift)
    loss[...] = loss_in[...] + flag[0].astype(F32) * (loss4 + loss5)
    out[...] = project(raw_u[...], grad_u[...] + term4 + term5)


def w_kernel(flag, scal, b6, z_w, grad_w, loss_in, raw_w, done_u, image_grad, text_grad, loss_rows):
    u_is_image = flag[0] == 1
    scale, shift = scal[0], scal[1]
    term, row_loss = pair_step(z_w[...], b6[...], scale, shift)
    total = loss_in[...] + (1.0 - flag[0].astype(F32)) * row_loss
    per_row = jnp.sum(jnp.transpose(total), axis=0, keepdims=True)
    loss_rows[...] = per_row / (SPAN * total.shape[0])
    done_w = project(raw_w[...], grad_w[...] + term)
    image_grad[...] = jnp.where(u_is_image, done_u[...], done_w)
    text_grad[...] = jnp.where(u_is_image, done_w, done_u[...])


def call(kernel, args, outs, products, name):
    smem = pl.BlockSpec(memory_space=pltpu.SMEM)
    vmem = pl.BlockSpec(memory_space=pltpu.VMEM)
    rows, width = args[2].shape
    size = sum(a.size * a.dtype.itemsize for a in list(args) + list(outs))
    return pl.pallas_call(
        kernel,
        out_shape=outs,
        in_specs=[smem, smem] + [vmem] * (len(args) - 2),
        out_specs=[vmem] * len(outs),
        name=name,
        cost_estimate=pl.CostEstimate(
            flops=2 * rows * rows * width * products, bytes_accessed=size, transcendentals=0
        ),
        compiler_params=pltpu.CompilerParams(vmem_limit_bytes=VMEM_LIMIT),
    )(*args)


def local(image, text, score_scaling, score_shift):
    rows, width = image.shape
    role = lax.axis_index(AXES) % GROUP
    u_is_image = role < 2
    flag = u_is_image.astype(jnp.int32).reshape(1)
    scal = jnp.stack([score_scaling, score_shift])
    u = jnp.where(u_is_image, image, text)
    w = jnp.where(u_is_image, text, image)
    outer = (role == 0) | (role == 3)

    block = jax.ShapeDtypeStruct((rows, width), BF16)
    sums = jax.ShapeDtypeStruct((rows, width), F32)
    partial = jax.ShapeDtypeStruct((rows, 128), F32)
    line = jax.ShapeDtypeStruct((1, rows), F32)

    slot1 = send(w, CORE_SWAP)
    slot2 = send(u, GROUP_SHIFT)
    slot3 = jnp.where(u_is_image, send(image, IMAGE_BACK), send(text, TEXT_ON))
    z_u, z_w, grad_u, grad_w, loss = call(
        own_kernel, (flag, scal, image, text), (block, block, sums, sums, partial), 3, "own_pair"
    )
    grad_w, loss = call(
        first_kernel, (flag, scal, slot1, z_w, grad_w, loss), (sums, partial), 2, "first_block"
    )
    w_sent, grad_w, loss = lax.optimization_barrier((w, grad_w, loss))
    slot5 = send(jnp.where(outer, w_sent, slot2), X_SWAP)
    slot4 = send(slot3, GROUP_SHIFT)
    grad_u, grad_w, loss = call(
        near_kernel,
        (flag, scal, slot2, slot3, z_u, z_w, grad_u, grad_w, loss),
        (sums, sums, partial),
        4,
        "near_blocks",
    )
    slot5, grad_u, grad_w, loss = lax.optimization_barrier((slot5, grad_u, grad_w, loss))
    slot6 = send(slot5, CORE_SWAP)
    done_u, loss = call(
        u_kernel, (flag, scal, slot4, slot5, z_u, grad_u, loss, u), (block, partial), 4, "finish_u"
    )
    image_grad, text_grad, loss_rows = call(
        w_kernel, (flag, scal, slot6, z_w, grad_w, loss, w, done_u), (block, block, line), 2, "finish_w"
    )
    return loss_rows.reshape(rows), image_grad, text_grad


def solution(mesh):
    in_specs = (P(AXES, None), P(AXES, None), P(), P())
    out_specs = (P(AXES), P(AXES, None), P(AXES, None))
    return jax.shard_map(local, mesh=mesh, in_specs=in_specs, out_specs=out_specs, check_vma=False)
```

```python
import jax
import jax.numpy as jnp
from jax import lax
from jax.experimental import pallas as pl
from jax.experimental.pallas import tpu as pltpu
from jax.sharding import PartitionSpec as P

SPAN = 4
GROUP = 4
AXES = ("blk", "inner")
F32 = jnp.float32
BF16 = jnp.bfloat16
VMEM_LIMIT = 24 * 1024 * 1024

TEXT_BY_TWO = {0: (2, 0), 1: (3, 0), 2: (0, 1), 3: (1, 1)}
IMAGE_BY_TWO = {0: (2, -1), 1: (3, -1), 2: (0, 0), 3: (1, 0)}
TEXT_X = {0: (0, 0), 1: (2, 0), 2: (3, 0), 3: (1, 0)}
IMAGE_X = {0: (2, 0), 1: (0, 0), 2: (1, 0), 3: (3, 0)}
X_SWAP = {0: (1, 0), 1: (0, 0), 2: (3, 0), 3: (2, 0)}
CORE_SWAP = {0: (2, 0), 1: (3, 0), 2: (0, 0), 3: (1, 0)}
RELAY = {0: (2, -1), 1: (3, -1), 2: (0, 1), 3: (1, 1)}


def send(value, moves):
    count = lax.axis_size(AXES)
    groups = count // GROUP
    pairs = [
        (g * GROUP + role, (g + step) % groups * GROUP + to)
        for g in range(groups)
        for role, (to, step) in moves.items()
    ]
    return lax.ppermute(value, AXES, pairs)


def unit_rows(raw):
    values = raw.astype(F32)
    length = jnp.sqrt(jnp.sum(values * values, axis=1, keepdims=True) + 1e-06)
    return values * (1.0 / length), length


def sigmoid_of(p):
    whole = 1.0 + p
    guess = pl.reciprocal(whole, approx=True)
    guess = guess * (2.0 - whole * guess)
    return p * (guess * (2.0 - whole * guess))


def log1p_of(p):
    below = p * (1.0 - p * (0.5 - p * (1.0 / 3.0)))
    return jnp.where(p < 0.015625, below, jnp.log(1.0 + p))


def softplus_lanes(p):
    total = None
    parts = [p[:, start : start + 128] for start in range(0, p.shape[1], 128)]
    for first in range(0, len(parts), 3):
        joint = parts[first]
        for part in parts[first + 1 : first + 3]:
            joint = joint + part + joint * part
        value = log1p_of(joint)
        total = value if total is None else total + value
    return total


def dot_nt(a, b):
    return lax.dot_general(a, b, (((1,), (1,)), ((), ())), preferred_element_type=F32)


def dot_nn(a, b):
    return lax.dot_general(a, b, (((1,), (0,)), ((), ())), preferred_element_type=F32)


def dot_tn(a, b):
    return lax.dot_general(a, b, (((0,), (0,)), ((), ())), preferred_element_type=F32)


def pair_step(own, blocks, scale, shift, work):
    rows = own.shape[0]
    for place, raw in enumerate(blocks):
        work[place * rows : (place + 1) * rows] = unit_rows(raw)[0].astype(BF16)
    others = work[: len(blocks) * rows]
    p = jnp.exp(scale * dot_nt(own, others) + shift)
    coef = (sigmoid_of(p) * scale).astype(BF16)
    return dot_nn(coef, others), softplus_lanes(p)


def project(raw, grad):
    unit, length = unit_rows(raw)
    return ((grad - unit * jnp.sum(unit * grad, axis=1, keepdims=True)) / length).astype(BF16)


def own_kernel(scal, image, text, z_image, z_text, grad_image, grad_text, loss):
    scale, shift = scal[0], scal[1]
    zi = unit_rows(image[...])[0].astype(BF16)
    zt = unit_rows(text[...])[0].astype(BF16)
    z_image[...] = zi
    z_text[...] = zt
    scores = scale * dot_nt(zi, zt) + shift
    rows = lax.broadcasted_iota(jnp.int32, scores.shape, 0)
    columns = lax.broadcasted_iota(jnp.int32, scores.shape, 1)
    sign = jnp.where(rows == columns, F32(-1.0), F32(1.0))
    p = jnp.exp(sign * scores)
    coef = (sign * sigmoid_of(p) * scale).astype(BF16)
    loss[...] = softplus_lanes(p)
    grad_image[...] = dot_nn(coef, zt)
    grad_text[...] = dot_tn(coef, zi)


def near_kernel(
    scal, flag, text, image, b3, z_image, z_text, grad_image, grad_text, loss_in,
    z_u, z_w, grad_u, grad_w, loss, work,
):
    u_is_image = flag[0] == 1
    u_weight = flag[0].astype(F32)
    scale, shift = scal[0], scal[1]
    z_u[...] = jnp.where(u_is_image, z_image[...], z_text[...])
    z_w[...] = jnp.where(u_is_image, z_text[...], z_image[...])
    for_u = jnp.where(u_is_image, text[...], image[...])
    for_w = jnp.where(u_is_image, image[...], text[...])
    term, row_loss = pair_step(z_u[...], (for_u,), scale, shift, work)
    grad_u[...] = jnp.where(u_is_image, grad_image[...], grad_text[...]) + term
    total = loss_in[...] + u_weight * row_loss
    term, row_loss = pair_step(z_w[...], (for_w, b3[...]), scale, shift, work)
    grad_w[...] = jnp.where(u_is_image, grad_text[...], grad_image[...]) + term
    loss[...] = total + (1.0 - u_weight) * row_loss


def u_kernel(scal, flag, b4, b5, z_u, grad_u, loss_in, image, text, out, loss, work):
    raw = jnp.where(flag[0] == 1, image[...], text[...])
    term, row_loss = pair_step(z_u[...], (b4[...], b5[...]), scal[0], scal[1], work)
    loss[...] = loss_in[...] + flag[0].astype(F32) * row_loss
    out[...] = project(raw, grad_u[...] + term)


def w_kernel(
    scal, flag, b6, z_w, grad_w, loss_in, image, text, done_u, image_grad, text_grad, loss_rows, work
):
    u_is_image = flag[0] == 1
    raw = jnp.where(u_is_image, text[...], image[...])
    term, row_loss = pair_step(z_w[...], (b6[...],), scal[0], scal[1], work)
    total = loss_in[...] + (1.0 - flag[0].astype(F32)) * row_loss
    per_row = jnp.sum(jnp.transpose(total), axis=0, keepdims=True)
    loss_rows[...] = per_row / (SPAN * total.shape[0])
    done_w = project(raw, grad_w[...] + term)
    image_grad[...] = jnp.where(u_is_image, done_u[...], done_w)
    text_grad[...] = jnp.where(u_is_image, done_w, done_u[...])


def call(kernel, scalars, args, outs, products, name, work_rows=0):
    smem = pl.BlockSpec(memory_space=pltpu.SMEM)
    vmem = pl.BlockSpec(memory_space=pltpu.VMEM)
    rows, width = args[0].shape
    size = sum(a.size * a.dtype.itemsize for a in list(args) + list(outs))
    return pl.pallas_call(
        kernel,
        out_shape=outs,
        in_specs=[smem] * len(scalars) + [vmem] * len(args),
        out_specs=[vmem] * len(outs),
        scratch_shapes=[pltpu.VMEM((work_rows, width), BF16)] if work_rows else [],
        name=name,
        cost_estimate=pl.CostEstimate(
            flops=2 * rows * rows * width * products, bytes_accessed=size, transcendentals=0
        ),
        compiler_params=pltpu.CompilerParams(vmem_limit_bytes=VMEM_LIMIT),
    )(*scalars, *args)


def local(image, text, score_scaling, score_shift):
    rows, width = image.shape
    role = lax.axis_index(AXES) % GROUP
    u_is_image = role < 2
    flag = u_is_image.astype(jnp.int32).reshape(1)
    scal = jnp.stack([score_scaling, score_shift])
    block = jax.ShapeDtypeStruct((rows, width), BF16)
    sums = jax.ShapeDtypeStruct((rows, width), F32)
    partial = jax.ShapeDtypeStruct((rows, 128), F32)
    line = jax.ShapeDtypeStruct((1, rows), F32)

    image_x = send(image, IMAGE_X)
    text_x = send(text, TEXT_X)
    text_two = send(text, TEXT_BY_TWO)
    image_two = send(image, IMAGE_BY_TWO)
    z_image, z_text, grad_image, grad_text, loss = call(
        own_kernel, (scal,), (image, text), (block, block, sums, sums, partial), 3, "own_pair"
    )
    text_kept, image_kept, loss = lax.optimization_barrier((text, image, loss))
    slot5 = send(
        jnp.where(
            u_is_image,
            jnp.where(role == 0, text_kept, text_two),
            jnp.where(role == 3, image_kept, image_two),
        ),
        X_SWAP,
    )
    slot3 = jnp.where(u_is_image, image_x, text_x)
    slot4 = send(slot3, RELAY)
    z_u, z_w, grad_u, grad_w, loss = call(
        near_kernel,
        (scal, flag),
        (text_two, image_two, slot3, z_image, z_text, grad_image, grad_text, loss),
        (block, block, sums, sums, partial),
        6,
        "near_blocks",
        2 * rows,
    )
    slot5, loss = lax.optimization_barrier((slot5, loss))
    slot6 = send(slot5, CORE_SWAP)
    done_u, loss = call(
        u_kernel,
        (scal, flag),
        (slot4, slot5, z_u, grad_u, loss, image, text),
        (block, partial),
        4,
        "finish_u",
        2 * rows,
    )
    image_grad, text_grad, loss_rows = call(
        w_kernel,
        (scal, flag),
        (slot6, z_w, grad_w, loss, image, text, done_u),
        (block, block, line),
        2,
        "finish_w",
        rows,
    )
    return loss_rows.reshape(rows), image_grad, text_grad


def solution(mesh):
    in_specs = (P(AXES, None), P(AXES, None), P(), P())
    out_specs = (P(AXES), P(AXES, None), P(AXES, None))
    return jax.shard_map(local, mesh=mesh, in_specs=in_specs, out_specs=out_specs, check_vma=False)
```

```python
import jax
import jax.numpy as jnp
from jax import lax
from jax.experimental import pallas as pl
from jax.experimental.pallas import tpu as pltpu
from jax.sharding import PartitionSpec as P

SPAN = 4
GROUP = 4
AXES = ("blk", "inner")
F32 = jnp.float32
BF16 = jnp.bfloat16
VMEM_LIMIT = 24 * 1024 * 1024

X_SWAP = {0: (1, 0), 1: (0, 0), 2: (3, 0), 3: (2, 0)}
CORE_SWAP = {0: (2, 0), 1: (3, 0), 2: (0, 0), 3: (1, 0)}
GROUP_SHIFT = {0: (2, -1), 1: (3, -1), 2: (0, 1), 3: (1, 1)}


def send(value, moves):
    count = lax.axis_size(AXES)
    groups = count // GROUP
    pairs = [
        (g * GROUP + role, (g + step) % groups * GROUP + to)
        for g in range(groups)
        for role, (to, step) in moves.items()
    ]
    return lax.ppermute(value, AXES, pairs)


def unit_rows(raw):
    values = raw.astype(F32)
    length = jnp.sqrt(jnp.sum(values * values, axis=1, keepdims=True) + 1e-06)
    return values * (1.0 / length), length


def sigmoid_of(p):
    whole = 1.0 + p
    guess = pl.reciprocal(whole, approx=True)
    guess = guess * (2.0 - whole * guess)
    return p * (guess * (2.0 - whole * guess))


def log1p_of(p):
    below = p * (1.0 - p * (0.5 - p * (1.0 / 3.0)))
    return jnp.where(p < 0.015625, below, jnp.log(1.0 + p))


def softplus_lanes(p):
    total = None
    parts = [p[:, start : start + 128] for start in range(0, p.shape[1], 128)]
    for first in range(0, len(parts), 3):
        joint = parts[first]
        for part in parts[first + 1 : first + 3]:
            joint = joint + part + joint * part
        value = log1p_of(joint)
        total = value if total is None else total + value
    return total


def dot_nt(a, b):
    return lax.dot_general(a, b, (((1,), (1,)), ((), ())), preferred_element_type=F32)


def dot_nn(a, b):
    return lax.dot_general(a, b, (((1,), (0,)), ((), ())), preferred_element_type=F32)


def dot_tn(a, b):
    return lax.dot_general(a, b, (((0,), (0,)), ((), ())), preferred_element_type=F32)


def pair_step(own, blocks, scale, shift, work):
    rows = own.shape[0]
    for place, raw in enumerate(blocks):
        work[place * rows : (place + 1) * rows] = unit_rows(raw)[0].astype(BF16)
    others = work[: len(blocks) * rows]
    p = jnp.exp(scale * dot_nt(own, others) + shift)
    coef = (sigmoid_of(p) * scale).astype(BF16)
    return dot_nn(coef, others), softplus_lanes(p)


def project(raw, grad):
    unit, length = unit_rows(raw)
    return ((grad - unit * jnp.sum(unit * grad, axis=1, keepdims=True)) / length).astype(BF16)


def own_kernel(scal, image, text, z_image, z_text, grad_image, grad_text, loss):
    scale, shift = scal[0], scal[1]
    zi = unit_rows(image[...])[0].astype(BF16)
    zt = unit_rows(text[...])[0].astype(BF16)
    z_image[...] = zi
    z_text[...] = zt
    scores = scale * dot_nt(zi, zt) + shift
    rows = lax.broadcasted_iota(jnp.int32, scores.shape, 0)
    columns = lax.broadcasted_iota(jnp.int32, scores.shape, 1)
    sign = jnp.where(rows == columns, F32(-1.0), F32(1.0))
    p = jnp.exp(sign * scores)
    coef = (sign * sigmoid_of(p) * scale).astype(BF16)
    loss[...] = softplus_lanes(p)
    grad_image[...] = dot_nn(coef, zt)
    grad_text[...] = dot_tn(coef, zi)


def near_kernel(
    scal, flag, b1, b2, b3, z_image, z_text, grad_image, grad_text, loss_in,
    z_u, z_w, grad_u, grad_w, loss, work,
):
    u_is_image = flag[0] == 1
    u_weight = flag[0].astype(F32)
    scale, shift = scal[0], scal[1]
    z_u[...] = jnp.where(u_is_image, z_image[...], z_text[...])
    z_w[...] = jnp.where(u_is_image, z_text[...], z_image[...])
    term, row_loss = pair_step(z_u[...], (b2[...],), scale, shift, work)
    grad_u[...] = jnp.where(u_is_image, grad_image[...], grad_text[...]) + term
    total = loss_in[...] + u_weight * row_loss
    term, row_loss = pair_step(z_w[...], (b1[...], b3[...]), scale, shift, work)
    grad_w[...] = jnp.where(u_is_image, grad_text[...], grad_image[...]) + term
    loss[...] = total + (1.0 - u_weight) * row_loss


def u_kernel(scal, flag, b4, b5, z_u, grad_u, loss_in, raw, out, loss, work):
    term, row_loss = pair_step(z_u[...], (b4[...], b5[...]), scal[0], scal[1], work)
    loss[...] = loss_in[...] + flag[0].astype(F32) * row_loss
    out[...] = project(raw[...], grad_u[...] + term)


def w_kernel(
    scal, flag, b6, z_w, grad_w, loss_in, raw, done_u, image_grad, text_grad, loss_rows, work
):
    u_is_image = flag[0] == 1
    term, row_loss = pair_step(z_w[...], (b6[...],), scal[0], scal[1], work)
    total = loss_in[...] + (1.0 - flag[0].astype(F32)) * row_loss
    per_row = jnp.sum(jnp.transpose(total), axis=0, keepdims=True)
    loss_rows[...] = per_row / (SPAN * total.shape[0])
    done_w = project(raw[...], grad_w[...] + term)
    image_grad[...] = jnp.where(u_is_image, done_u[...], done_w)
    text_grad[...] = jnp.where(u_is_image, done_w, done_u[...])


def call(kernel, scalars, args, outs, products, name, work_rows=0):
    smem = pl.BlockSpec(memory_space=pltpu.SMEM)
    vmem = pl.BlockSpec(memory_space=pltpu.VMEM)
    rows, width = args[0].shape
    size = sum(a.size * a.dtype.itemsize for a in list(args) + list(outs))
    return pl.pallas_call(
        kernel,
        out_shape=outs,
        in_specs=[smem] * len(scalars) + [vmem] * len(args),
        out_specs=[vmem] * len(outs),
        scratch_shapes=[pltpu.VMEM((work_rows, width), BF16)] if work_rows else [],
        name=name,
        cost_estimate=pl.CostEstimate(
            flops=2 * rows * rows * width * products, bytes_accessed=size, transcendentals=0
        ),
        compiler_params=pltpu.CompilerParams(vmem_limit_bytes=VMEM_LIMIT),
    )(*scalars, *args)


def local(image, text, score_scaling, score_shift):
    rows, width = image.shape
    role = lax.axis_index(AXES) % GROUP
    u_is_image = role < 2
    flag = u_is_image.astype(jnp.int32).reshape(1)
    scal = jnp.stack([score_scaling, score_shift])
    block = jax.ShapeDtypeStruct((rows, width), BF16)
    sums = jax.ShapeDtypeStruct((rows, width), F32)
    partial = jax.ShapeDtypeStruct((rows, 128), F32)
    line = jax.ShapeDtypeStruct((1, rows), F32)

    u = jnp.where(u_is_image, image, text)
    w = jnp.where(u_is_image, text, image)
    outer = (role == 0) | (role == 3)

    slot1 = send(w, CORE_SWAP)
    slot2 = send(u, GROUP_SHIFT)
    slot3 = send(jnp.where(outer, slot1, u), X_SWAP)
    slot4 = send(slot3, GROUP_SHIFT)
    slot5 = send(jnp.where(outer, w, slot2), X_SWAP)
    slot3, own_image, own_text = lax.optimization_barrier((slot3, image, text))
    z_image, z_text, grad_image, grad_text, loss = call(
        own_kernel, (scal,), (own_image, own_text), (block, block, sums, sums, partial), 3, "own_pair"
    )
    z_u, z_w, grad_u, grad_w, loss = call(
        near_kernel,
        (scal, flag),
        (slot1, slot2, slot3, z_image, z_text, grad_image, grad_text, loss),
        (block, block, sums, sums, partial),
        6,
        "near_blocks",
        2 * rows,
    )
    slot5, loss = lax.optimization_barrier((slot5, loss))
    slot6 = send(slot5, CORE_SWAP)
    done_u, loss = call(
        u_kernel,
        (scal, flag),
        (slot4, slot5, z_u, grad_u, loss, u),
        (block, partial),
        4,
        "finish_u",
        2 * rows,
    )
    image_grad, text_grad, loss_rows = call(
        w_kernel,
        (scal, flag),
        (slot6, z_w, grad_w, loss, w, done_u),
        (block, block, line),
        2,
        "finish_w",
        rows,
    )
    return loss_rows.reshape(rows), image_grad, text_grad


def solution(mesh):
    in_specs = (P(AXES, None), P(AXES, None), P(), P())
    out_specs = (P(AXES), P(AXES, None), P(AXES, None))
    return jax.shard_map(local, mesh=mesh, in_specs=in_specs, out_specs=out_specs, check_vma=False)
```

```python
import jax
import jax.numpy as jnp
from jax import lax
from jax.experimental import pallas as pl
from jax.experimental.pallas import tpu as pltpu
from jax.sharding import PartitionSpec as P

SPAN = 4
GROUP = 4
AXES = ("blk", "inner")
F32 = jnp.float32
BF16 = jnp.bfloat16
VMEM_LIMIT = 16 * 1024 * 1024

X_SWAP = {0: (1, 0), 1: (0, 0), 2: (3, 0), 3: (2, 0)}
CORE_SWAP = {0: (2, 0), 1: (3, 0), 2: (0, 0), 3: (1, 0)}
GROUP_SHIFT = {0: (2, -1), 1: (3, -1), 2: (0, 1), 3: (1, 1)}


def send(value, moves):
    count = lax.axis_size(AXES)
    groups = count // GROUP
    pairs = [
        (g * GROUP + role, (g + step) % groups * GROUP + to)
        for g in range(groups)
        for role, (to, step) in moves.items()
    ]
    return lax.ppermute(value, AXES, pairs)


def unit_rows(raw):
    values = raw.astype(F32)
    length = jnp.sqrt(jnp.sum(values * values, axis=1, keepdims=True) + 1e-06)
    return values * (1.0 / length), length


def sigmoid_of(p):
    whole = 1.0 + p
    guess = pl.reciprocal(whole, approx=True)
    guess = guess * (2.0 - whole * guess)
    return p * (guess * (2.0 - whole * guess))


def log1p_of(p):
    below = p * (1.0 - p * (0.5 - p * (1.0 / 3.0)))
    return jnp.where(p < 0.015625, below, jnp.log(1.0 + p))


def softplus_lanes(p):
    total = None
    parts = [p[:, start : start + 128] for start in range(0, p.shape[1], 128)]
    for first in range(0, len(parts), 3):
        joint = parts[first]
        for part in parts[first + 1 : first + 3]:
            joint = joint + part + joint * part
        value = log1p_of(joint)
        total = value if total is None else total + value
    return total


def dot_nt(a, b):
    return lax.dot_general(a, b, (((1,), (1,)), ((), ())), preferred_element_type=F32)


def dot_nn(a, b):
    return lax.dot_general(a, b, (((1,), (0,)), ((), ())), preferred_element_type=F32)


def dot_tn(a, b):
    return lax.dot_general(a, b, (((0,), (0,)), ((), ())), preferred_element_type=F32)


def pair_step(own, blocks, scale, shift, work):
    rows = own.shape[0]
    for place, raw in enumerate(blocks):
        work[place * rows : (place + 1) * rows] = unit_rows(raw)[0].astype(BF16)
    others = work[: len(blocks) * rows]
    p = jnp.exp(scale * dot_nt(own, others) + shift)
    coef = (sigmoid_of(p) * scale).astype(BF16)
    return dot_nn(coef, others), softplus_lanes(p)


def project(raw, grad):
    unit, length = unit_rows(raw)
    return ((grad - unit * jnp.sum(unit * grad, axis=1, keepdims=True)) / length).astype(BF16)


def near_kernel(scal, flag, image, text, b1, b2, b3, z_u, z_w, grad_u, grad_w, loss, work):
    u_is_image = flag[0] == 1
    u_weight = flag[0].astype(F32)
    scale, shift = scal[0], scal[1]
    zi = unit_rows(image[...])[0].astype(BF16)
    zt = unit_rows(text[...])[0].astype(BF16)
    z_u[...] = jnp.where(u_is_image, zi, zt)
    z_w[...] = jnp.where(u_is_image, zt, zi)
    scores = scale * dot_nt(zi, zt) + shift
    rows = lax.broadcasted_iota(jnp.int32, scores.shape, 0)
    columns = lax.broadcasted_iota(jnp.int32, scores.shape, 1)
    sign = jnp.where(rows == columns, F32(-1.0), F32(1.0))
    p = jnp.exp(sign * scores)
    coef = (sign * sigmoid_of(p) * scale).astype(BF16)
    total = softplus_lanes(p)
    grad_image = dot_nn(coef, zt)
    grad_text = dot_tn(coef, zi)
    grad_u[...] = jnp.where(u_is_image, grad_image, grad_text)
    grad_w[...] = jnp.where(u_is_image, grad_text, grad_image)
    term, row_loss = pair_step(z_u[...], (b2[...],), scale, shift, work)
    grad_u[...] += term
    total = total + u_weight * row_loss
    term, row_loss = pair_step(z_w[...], (b1[...], b3[...]), scale, shift, work)
    grad_w[...] += term
    loss[...] = total + (1.0 - u_weight) * row_loss


def fifth_kernel(scal, flag, b5, z_u, grad_in, loss_in, grad_u, loss, work):
    term, row_loss = pair_step(z_u[...], (b5[...],), scal[0], scal[1], work)
    grad_u[...] = grad_in[...] + term
    loss[...] = loss_in[...] + flag[0].astype(F32) * row_loss


def u_kernel(scal, flag, b4, z_u, grad_u, loss_in, image, text, done_u, loss, work):
    raw = jnp.where(flag[0] == 1, image[...], text[...])
    term, row_loss = pair_step(z_u[...], (b4[...],), scal[0], scal[1], work)
    loss[...] = loss_in[...] + flag[0].astype(F32) * row_loss
    done_u[...] = project(raw, grad_u[...] + term)


def w_kernel(
    scal, flag, b6, z_w, grad_w, loss_in, image, text, done_u, image_grad, text_grad, loss_rows, work
):
    u_is_image = flag[0] == 1
    raw = jnp.where(u_is_image, text[...], image[...])
    term, row_loss = pair_step(z_w[...], (b6[...],), scal[0], scal[1], work)
    total = loss_in[...] + (1.0 - flag[0].astype(F32)) * row_loss
    loss_rows[...] = jnp.sum(jnp.transpose(total), axis=0) / (SPAN * total.shape[0])
    done_w = project(raw, grad_w[...] + term)
    image_grad[...] = jnp.where(u_is_image, done_u[...], done_w)
    text_grad[...] = jnp.where(u_is_image, done_w, done_u[...])


def call(kernel, scalars, args, outs, name, work_rows=0):
    smem = pl.BlockSpec(memory_space=pltpu.SMEM)
    vmem = pl.BlockSpec(memory_space=pltpu.VMEM)
    width = args[0].shape[1]
    return pl.pallas_call(
        kernel,
        out_shape=outs,
        in_specs=[smem] * len(scalars) + [vmem] * len(args),
        out_specs=[vmem] * len(outs),
        scratch_shapes=[pltpu.VMEM((work_rows, width), BF16)] if work_rows else [],
        name=name,
        cost_estimate=pl.CostEstimate(flops=1, bytes_accessed=1, transcendentals=0),
        compiler_params=pltpu.CompilerParams(vmem_limit_bytes=VMEM_LIMIT),
    )(*scalars, *args)


def local(image, text, score_scaling, score_shift):
    rows, width = image.shape
    role = lax.axis_index(AXES) % GROUP
    u_is_image = role < 2
    flag = u_is_image.astype(jnp.int32).reshape(1)
    scal = jnp.stack([score_scaling, score_shift])
    block = jax.ShapeDtypeStruct((rows, width), BF16)
    sums = jax.ShapeDtypeStruct((rows, width), F32)
    partial = jax.ShapeDtypeStruct((rows, 128), F32)
    line = jax.ShapeDtypeStruct((rows,), F32)

    u = jnp.where(u_is_image, image, text)
    w = jnp.where(u_is_image, text, image)
    u, w = lax.optimization_barrier((u, w))
    outer = (role == 0) | (role == 3)

    slot1 = send(w, CORE_SWAP)
    slot2 = send(u, GROUP_SHIFT)
    slot3 = send(jnp.where(outer, slot1, u), X_SWAP)
    slot4 = send(slot3, GROUP_SHIFT)
    slot5 = send(jnp.where(outer, w, slot2), X_SWAP)
    z_u, z_w, grad_u, grad_w, loss = call(
        near_kernel,
        (scal, flag),
        (image, text, slot1, slot2, slot3),
        (block, block, sums, sums, partial),
        "near_blocks",
        2 * rows,
    )
    slot5, loss = lax.optimization_barrier((slot5, loss))
    slot6 = send(slot5, CORE_SWAP)
    grad_u, loss = call(
        fifth_kernel, (scal, flag), (slot5, z_u, grad_u, loss), (sums, partial), "fifth_block", rows
    )
    done_u, loss = call(
        u_kernel,
        (scal, flag),
        (slot4, z_u, grad_u, loss, image, text),
        (block, partial),
        "finish_u",
        rows,
    )
    image_grad, text_grad, loss_rows = call(
        w_kernel,
        (scal, flag),
        (slot6, z_w, grad_w, loss, image, text, done_u),
        (block, block, line),
        "finish_w",
        rows,
    )
    return loss_rows, image_grad, text_grad


def solution(mesh):
    in_specs = (P(AXES, None), P(AXES, None), P(), P())
    out_specs = (P(AXES), P(AXES, None), P(AXES, None))
    return jax.shard_map(local, mesh=mesh, in_specs=in_specs, out_specs=out_specs, check_vma=False)
```

```python
import jax
import jax.numpy as jnp
from jax import lax
from jax.experimental import pallas as pl
from jax.experimental.pallas import tpu as pltpu
from jax.sharding import PartitionSpec as P

SPAN = 4
GROUP = 4
AXES = ("blk", "inner")
F32 = jnp.float32
BF16 = jnp.bfloat16
VMEM_LIMIT = 16 * 1024 * 1024

X_SWAP = {0: (1, 0), 1: (0, 0), 2: (3, 0), 3: (2, 0)}
CORE_SWAP = {0: (2, 0), 1: (3, 0), 2: (0, 0), 3: (1, 0)}
GROUP_SHIFT = {0: (2, -1), 1: (3, -1), 2: (0, 1), 3: (1, 1)}


def send(value, moves):
    count = lax.axis_size(AXES)
    groups = count // GROUP
    pairs = [
        (g * GROUP + role, (g + step) % groups * GROUP + to)
        for g in range(groups)
        for role, (to, step) in moves.items()
    ]
    return lax.ppermute(value, AXES, pairs)


def unit_rows(raw):
    values = raw.astype(F32)
    length = jnp.sqrt(jnp.sum(values * values, axis=1, keepdims=True) + 1e-06)
    return values * (1.0 / length), length


def sigmoid_of(p):
    whole = 1.0 + p
    guess = pl.reciprocal(whole, approx=True)
    guess = guess * (2.0 - whole * guess)
    return p * (guess * (2.0 - whole * guess))


def log1p_of(p):
    below = p * (1.0 - p * (0.5 - p * (1.0 / 3.0)))
    return jnp.where(p < 0.015625, below, jnp.log(1.0 + p))


def softplus_lanes(p):
    total = None
    parts = [p[:, start : start + 128] for start in range(0, p.shape[1], 128)]
    for first in range(0, len(parts), 3):
        joint = parts[first]
        for part in parts[first + 1 : first + 3]:
            joint = joint + part + joint * part
        value = log1p_of(joint)
        total = value if total is None else total + value
    return total


def dot_nt(a, b):
    return lax.dot_general(a, b, (((1,), (1,)), ((), ())), preferred_element_type=F32)


def dot_nn(a, b):
    return lax.dot_general(a, b, (((1,), (0,)), ((), ())), preferred_element_type=F32)


def dot_tn(a, b):
    return lax.dot_general(a, b, (((0,), (0,)), ((), ())), preferred_element_type=F32)


def pair_step(own, blocks, scale, shift, work):
    rows = own.shape[0]
    for place, raw in enumerate(blocks):
        work[place * rows : (place + 1) * rows] = unit_rows(raw)[0].astype(BF16)
    others = work[: len(blocks) * rows]
    p = jnp.exp(scale * dot_nt(own, others) + shift)
    coef = (sigmoid_of(p) * scale).astype(BF16)
    return dot_nn(coef, others), softplus_lanes(p)


def project(raw, grad):
    unit, length = unit_rows(raw)
    return ((grad - unit * jnp.sum(unit * grad, axis=1, keepdims=True)) / length).astype(BF16)


def scalar_pair(scalars):
    return scalars[0:1, 0:1], scalars[1:2, 0:1]


def image_is_u():
    return lax.rem(lax.axis_index("blk"), 2) == 0


def is_outer():
    return lax.rem(lax.axis_index("blk"), 2) == lax.axis_index("inner")


def sort_kernel(image, text, u, w, sems):
    def move(image_to, text_to):
        copies = [
            pltpu.make_async_copy(image, image_to, sems.at[0]),
            pltpu.make_async_copy(text, text_to, sems.at[1]),
        ]
        for copy in copies:
            copy.start()
        for copy in copies:
            copy.wait()

    u_is_image = image_is_u()

    @pl.when(u_is_image)
    def _():
        move(u, w)

    @pl.when(jnp.logical_not(u_is_image))
    def _():
        move(w, u)


def pick_kernel(when_outer, when_inner, picked):
    picked[...] = jnp.where(is_outer(), when_outer[...], when_inner[...])


def near_kernel(scalars, image, text, b1, b2, b3, z_u, z_w, grad_u, grad_w, loss, work):
    u_is_image = image_is_u()
    u_weight = u_is_image.astype(F32)
    scale, shift = scalar_pair(scalars)
    zi = unit_rows(image[...])[0].astype(BF16)
    zt = unit_rows(text[...])[0].astype(BF16)
    z_u[...] = jnp.where(u_is_image, zi, zt)
    z_w[...] = jnp.where(u_is_image, zt, zi)
    scores = scale * dot_nt(zi, zt) + shift
    rows = lax.broadcasted_iota(jnp.int32, scores.shape, 0)
    columns = lax.broadcasted_iota(jnp.int32, scores.shape, 1)
    sign = jnp.where(rows == columns, F32(-1.0), F32(1.0))
    p = jnp.exp(sign * scores)
    coef = (sign * sigmoid_of(p) * scale).astype(BF16)
    total = softplus_lanes(p)
    grad_image = dot_nn(coef, zt)
    grad_text = dot_tn(coef, zi)
    grad_u[...] = jnp.where(u_is_image, grad_image, grad_text)
    grad_w[...] = jnp.where(u_is_image, grad_text, grad_image)
    term, row_loss = pair_step(z_u[...], (b2[...],), scale, shift, work)
    grad_u[...] += term
    total = total + u_weight * row_loss
    term, row_loss = pair_step(z_w[...], (b1[...], b3[...]), scale, shift, work)
    grad_w[...] += term
    loss[...] = total + (1.0 - u_weight) * row_loss


def fifth_kernel(scalars, b5, z_u, grad_in, loss_in, grad_u, loss, work):
    term, row_loss = pair_step(z_u[...], (b5[...],), *scalar_pair(scalars), work)
    grad_u[...] = grad_in[...] + term
    loss[...] = loss_in[...] + image_is_u().astype(F32) * row_loss


def u_kernel(scalars, b4, z_u, grad_u, loss_in, image, text, done_u, loss, work):
    raw = jnp.where(image_is_u(), image[...], text[...])
    term, row_loss = pair_step(z_u[...], (b4[...],), *scalar_pair(scalars), work)
    loss[...] = loss_in[...] + image_is_u().astype(F32) * row_loss
    done_u[...] = project(raw, grad_u[...] + term)


def w_kernel(
    scalars, b6, z_w, grad_w, loss_in, image, text, done_u, image_grad, text_grad, loss_rows, work
):
    u_is_image = image_is_u()
    raw = jnp.where(u_is_image, text[...], image[...])
    term, row_loss = pair_step(z_w[...], (b6[...],), *scalar_pair(scalars), work)
    total = loss_in[...] + (1.0 - image_is_u().astype(F32)) * row_loss
    loss_rows[...] = jnp.sum(jnp.transpose(total), axis=0) / (SPAN * total.shape[0])
    done_w = project(raw, grad_w[...] + term)
    image_grad[...] = jnp.where(u_is_image, done_u[...], done_w)
    text_grad[...] = jnp.where(u_is_image, done_w, done_u[...])


VMEM = pl.BlockSpec(memory_space=pltpu.VMEM)
ANY = pl.BlockSpec(memory_space=pl.ANY)


def call(kernel, in_specs, args, outs, name, scratch=()):
    return pl.pallas_call(
        kernel,
        out_shape=outs,
        in_specs=in_specs,
        out_specs=[VMEM] * len(outs),
        scratch_shapes=list(scratch),
        name=name,
        cost_estimate=pl.CostEstimate(flops=1, bytes_accessed=1, transcendentals=0),
        compiler_params=pltpu.CompilerParams(vmem_limit_bytes=VMEM_LIMIT),
    )(*args)


def local(image, text, score_scaling, score_shift):
    rows, width = image.shape
    block = jax.ShapeDtypeStruct((rows, width), BF16)
    sums = jax.ShapeDtypeStruct((rows, width), F32)
    partial = jax.ShapeDtypeStruct((rows, 128), F32)
    line = jax.ShapeDtypeStruct((rows,), F32)
    def pick(when_outer, when_inner):
        return call(pick_kernel, [VMEM] * 2, (when_outer, when_inner), (block,), "pick")[0]

    def compute(kernel, args, outs, name, places):
        work = pltpu.VMEM((places * rows, width), BF16)
        return call(kernel, [VMEM] * (1 + len(args)), (scalars, *args), outs, name, (work,))

    u, w = call(
        sort_kernel,
        [ANY] * 2,
        [pltpu.with_memory_space_constraint(x, pltpu.HBM) for x in (image, text)],
        (block, block),
        "sort",
        (pltpu.SemaphoreType.DMA((2,)),),
    )
    slot1 = send(w, CORE_SWAP)
    slot2 = send(u, GROUP_SHIFT)
    slot3 = send(pick(slot1, u), X_SWAP)
    slot4 = send(slot3, GROUP_SHIFT)
    slot5 = send(pick(w, slot2), X_SWAP)
    slot3, score_scaling, score_shift = lax.optimization_barrier((slot3, score_scaling, score_shift))
    first = lax.broadcasted_iota(jnp.int32, (8, 128), 0) == 0
    scalars = jnp.where(first, score_scaling, score_shift)
    z_u, z_w, grad_u, grad_w, loss = compute(
        near_kernel,
        (image, text, slot1, slot2, slot3),
        (block, block, sums, sums, partial),
        "near_blocks",
        2,
    )
    slot5, loss = lax.optimization_barrier((slot5, loss))
    slot6 = send(slot5, CORE_SWAP)
    grad_u, loss = compute(fifth_kernel, (slot5, z_u, grad_u, loss), (sums, partial), "fifth_block", 1)
    done_u, loss = compute(
        u_kernel, (slot4, z_u, grad_u, loss, image, text), (block, partial), "finish_u", 1
    )
    image_grad, text_grad, loss_rows = compute(
        w_kernel, (slot6, z_w, grad_w, loss, image, text, done_u), (block, block, line), "finish_w", 1
    )
    return loss_rows, image_grad, text_grad


def solution(mesh):
    in_specs = (P(AXES, None), P(AXES, None), P(), P())
    out_specs = (P(AXES), P(AXES, None), P(AXES, None))
    return jax.shard_map(local, mesh=mesh, in_specs=in_specs, out_specs=out_specs, check_vma=False)
```

```python
import jax
import jax.numpy as jnp
from jax import lax
from jax.experimental import pallas as pl
from jax.experimental.pallas import tpu as pltpu
from jax.sharding import PartitionSpec as P

SPAN = 4
GROUP = 4
AXES = ("blk", "inner")
F32 = jnp.float32
BF16 = jnp.bfloat16
VMEM_LIMIT = 16 * 1024 * 1024

X_SWAP = {0: (1, 0), 1: (0, 0), 2: (3, 0), 3: (2, 0)}
CORE_SWAP = {0: (2, 0), 1: (3, 0), 2: (0, 0), 3: (1, 0)}
GROUP_SHIFT = {0: (2, -1), 1: (3, -1), 2: (0, 1), 3: (1, 1)}


def send(value, moves):
    count = lax.axis_size(AXES)
    groups = count // GROUP
    pairs = [
        (g * GROUP + role, (g + step) % groups * GROUP + to)
        for g in range(groups)
        for role, (to, step) in moves.items()
    ]
    return lax.ppermute(value, AXES, pairs)


def unit_rows(raw):
    values = raw.astype(F32)
    inverse = 1.0 / jnp.sqrt(jnp.sum(values * values, axis=1, keepdims=True) + 1e-06)
    return values * inverse, inverse


def sigmoid_of(p):
    whole = 1.0 + p
    guess = pl.reciprocal(whole, approx=True)
    guess = guess * (2.0 - whole * guess)
    return p * (guess * (2.0 - whole * guess))


def log1p_of(p):
    below = p * (1.0 - p * (0.5 - p * (1.0 / 3.0)))
    return jnp.where(p < 0.015625, below, jnp.log(1.0 + p))


def softplus_lanes(p):
    total = None
    parts = [p[:, start : start + 128] for start in range(0, p.shape[1], 128)]
    for first in range(0, len(parts), 3):
        joint = parts[first]
        for part in parts[first + 1 : first + 3]:
            joint = joint + part + joint * part
        value = log1p_of(joint)
        total = value if total is None else total + value
    return total


def dot_nt(a, b):
    return lax.dot_general(a, b, (((1,), (1,)), ((), ())), preferred_element_type=F32)


def dot_nn(a, b):
    return lax.dot_general(a, b, (((1,), (0,)), ((), ())), preferred_element_type=F32)


def dot_tn(a, b):
    return lax.dot_general(a, b, (((0,), (0,)), ((), ())), preferred_element_type=F32)


def pair_step(own, blocks, scale, shift, work):
    rows = own.shape[0]
    for place, raw in enumerate(blocks):
        work[place * rows : (place + 1) * rows] = unit_rows(raw)[0].astype(BF16)
    return terms(own, work[: len(blocks) * rows], scale, shift)


def terms(own, others, scale, shift):
    p = jnp.exp(scale * dot_nt(own, others) + shift)
    coef = (sigmoid_of(p) * scale).astype(BF16)
    return dot_nn(coef, others), softplus_lanes(p)


def project(unit, inverse, grad):
    return ((grad - unit * jnp.sum(unit * grad, axis=1, keepdims=True)) * inverse).astype(BF16)


def row_parts(rows):
    count = 3 if rows % 48 == 0 else 1
    return [pl.ds(place * (rows // count), rows // count) for place in range(count)]


def scalar_pair(scalars):
    return scalars[0:1, 0:1], scalars[1:2, 0:1]


def image_is_u():
    return lax.rem(lax.axis_index("blk"), 2) == 0


def is_outer():
    return lax.rem(lax.axis_index("blk"), 2) == lax.axis_index("inner")


def sort_kernel(image, text, u, w, sems):
    def move(image_to, text_to):
        copies = [
            pltpu.make_async_copy(image, image_to, sems.at[0]),
            pltpu.make_async_copy(text, text_to, sems.at[1]),
        ]
        for copy in copies:
            copy.start()
        for copy in copies:
            copy.wait()

    u_is_image = image_is_u()

    @pl.when(u_is_image)
    def _():
        move(u, w)

    @pl.when(jnp.logical_not(u_is_image))
    def _():
        move(w, u)


def pick_kernel(when_outer, when_inner, picked, sem):
    @pl.when(is_outer())
    def _():
        pltpu.async_copy(when_outer, picked, sem).wait()

    @pl.when(jnp.logical_not(is_outer()))
    def _():
        pltpu.async_copy(when_inner, picked, sem).wait()


def near_kernel(
    scalars, image, text, b1, b2, b3,
    z_u, z_w, unit_u, unit_w, inverse_u, inverse_w, grad_u, grad_w, loss, work,
):
    u_is_image = image_is_u()
    u_weight = u_is_image.astype(F32)
    scale, shift = scalar_pair(scalars)
    image_unit, image_inverse = unit_rows(image[...])
    text_unit, text_inverse = unit_rows(text[...])
    unit_u[...] = jnp.where(u_is_image, image_unit, text_unit)
    unit_w[...] = jnp.where(u_is_image, text_unit, image_unit)
    inverse_u[...] = jnp.where(u_is_image, image_inverse, text_inverse)
    inverse_w[...] = jnp.where(u_is_image, text_inverse, image_inverse)
    zi = image_unit.astype(BF16)
    zt = text_unit.astype(BF16)
    z_u[...] = jnp.where(u_is_image, zi, zt)
    z_w[...] = jnp.where(u_is_image, zt, zi)
    scores = scale * dot_nt(zi, zt) + shift
    rows = lax.broadcasted_iota(jnp.int32, scores.shape, 0)
    columns = lax.broadcasted_iota(jnp.int32, scores.shape, 1)
    sign = jnp.where(rows == columns, F32(-1.0), F32(1.0))
    p = jnp.exp(sign * scores)
    coef = (sign * sigmoid_of(p) * scale).astype(BF16)
    total = softplus_lanes(p)
    grad_image = dot_nn(coef, zt)
    grad_text = dot_tn(coef, zi)
    grad_u[...] = jnp.where(u_is_image, grad_image, grad_text)
    grad_w[...] = jnp.where(u_is_image, grad_text, grad_image)
    term, row_loss = pair_step(z_u[...], (b2[...],), scale, shift, work)
    grad_u[...] += term
    total = total + u_weight * row_loss
    term, row_loss = pair_step(z_w[...], (b1[...], b3[...]), scale, shift, work)
    grad_w[...] += term
    loss[...] = total + (1.0 - u_weight) * row_loss


def fifth_kernel(scalars, b5, z_u, grad_in, loss_in, grad_u, loss, raw, work, sems):
    copies = []
    for place, part in enumerate(row_parts(raw.shape[0])):
        copy = pltpu.make_async_copy(b5.at[part], raw.at[part], sems.at[place])
        copy.start()
        copies.append((copy, part))
    for copy, part in copies:
        copy.wait()
        work[part] = unit_rows(raw[part])[0].astype(BF16)
    term, row_loss = terms(z_u[...], work[...], *scalar_pair(scalars))
    grad_u[...] = grad_in[...] + term
    loss[...] = loss_in[...] + image_is_u().astype(F32) * row_loss


def u_kernel(scalars, b4, z_u, grad_u, loss_in, unit, inverse, done_u, loss, work):
    term, row_loss = pair_step(z_u[...], (b4[...],), *scalar_pair(scalars), work)
    loss[...] = loss_in[...] + image_is_u().astype(F32) * row_loss
    done_u[...] = project(unit[...], inverse[...], grad_u[...] + term)


def w_kernel(
    scalars, b6, z_w, grad_w, loss_in, unit, inverse, done_u,
    image_grad, text_grad, loss_rows, done_w, work, sems,
):
    u_is_image = image_is_u()
    parts = row_parts(done_w.shape[0])

    def output(action, source, part, to_image, sem):
        @pl.when(to_image)
        def _():
            action(pltpu.make_async_copy(source.at[part], image_grad.at[part], sem))

        @pl.when(jnp.logical_not(to_image))
        def _():
            action(pltpu.make_async_copy(source.at[part], text_grad.at[part], sem))

    whole = pl.ds(0, done_w.shape[0])
    output(lambda copy: copy.start(), done_u, whole, u_is_image, sems.at[0])
    term, row_loss = pair_step(z_w[...], (b6[...],), *scalar_pair(scalars), work)
    for place, part in enumerate(parts):
        start = place * (done_w.shape[0] // len(parts))
        rows = slice(start, start + done_w.shape[0] // len(parts))
        done_w[part] = project(unit[part], inverse[part], grad_w[part] + term[rows])
        output(lambda copy: copy.start(), done_w, part, jnp.logical_not(u_is_image), sems.at[1 + place])
    total = loss_in[...] + (1.0 - u_is_image.astype(F32)) * row_loss
    loss_rows[...] = jnp.sum(jnp.transpose(total), axis=0) / (SPAN * total.shape[0])
    output(lambda copy: copy.wait(), done_u, whole, u_is_image, sems.at[0])
    for place, part in enumerate(parts):
        output(lambda copy: copy.wait(), done_w, part, jnp.logical_not(u_is_image), sems.at[1 + place])


VMEM = pl.BlockSpec(memory_space=pltpu.VMEM)
ANY = pl.BlockSpec(memory_space=pl.ANY)


def call(kernel, in_specs, args, out_specs, outs, name, scratch=()):
    return pl.pallas_call(
        kernel,
        out_shape=outs,
        in_specs=in_specs,
        out_specs=out_specs,
        scratch_shapes=list(scratch),
        name=name,
        cost_estimate=pl.CostEstimate(flops=1, bytes_accessed=1, transcendentals=0),
        compiler_params=pltpu.CompilerParams(vmem_limit_bytes=VMEM_LIMIT),
    )(*args)


def local(image, text, score_scaling, score_shift):
    rows, width = image.shape
    block = jax.ShapeDtypeStruct((rows, width), BF16)
    sums = jax.ShapeDtypeStruct((rows, width), F32)
    column = jax.ShapeDtypeStruct((rows, 1), F32)
    partial = jax.ShapeDtypeStruct((rows, 128), F32)
    line = jax.ShapeDtypeStruct((rows,), F32)
    raw = pltpu.VMEM((rows, width), BF16)
    copies = pltpu.SemaphoreType.DMA((4,))

    def pick(when_outer, when_inner):
        sem = pltpu.SemaphoreType.DMA
        return call(
            pick_kernel, [ANY] * 2, (when_outer, when_inner), [ANY], (block,), "pick", (sem,)
        )[0]

    def compute(kernel, args, outs, name, scratch):
        in_specs = [VMEM] * (1 + len(args))
        return call(kernel, in_specs, (scalars, *args), [VMEM] * len(outs), outs, name, scratch)

    u, w = call(
        sort_kernel,
        [ANY] * 2,
        [pltpu.with_memory_space_constraint(x, pltpu.HBM) for x in (image, text)],
        [VMEM] * 2,
        (block, block),
        "sort",
        (copies,),
    )
    slot1 = send(w, CORE_SWAP)
    slot2 = send(u, GROUP_SHIFT)
    slot3 = send(pick(slot1, u), X_SWAP)
    slot4 = send(slot3, GROUP_SHIFT)
    slot5 = send(pick(w, slot2), X_SWAP)
    slot3, score_scaling, score_shift = lax.optimization_barrier((slot3, score_scaling, score_shift))
    first = lax.broadcasted_iota(jnp.int32, (8, 128), 0) == 0
    scalars = jnp.where(first, score_scaling, score_shift)
    z_u, z_w, unit_u, unit_w, inverse_u, inverse_w, grad_u, grad_w, loss = compute(
        near_kernel,
        (image, text, slot1, slot2, slot3),
        (block, block, sums, sums, column, column, sums, sums, partial),
        "near_blocks",
        (pltpu.VMEM((2 * rows, width), BF16),),
    )
    slot5, loss = lax.optimization_barrier((slot5, loss))
    slot6 = send(slot5, CORE_SWAP)
    grad_u, loss = call(
        fifth_kernel,
        [VMEM, ANY, VMEM, VMEM, VMEM],
        (scalars, slot5, z_u, grad_u, loss),
        [VMEM] * 2,
        (sums, partial),
        "fifth_block",
        (raw, raw, copies),
    )
    done_u, loss = compute(
        u_kernel,
        (slot4, z_u, grad_u, loss, unit_u, inverse_u),
        (block, partial),
        "finish_u",
        (raw,),
    )
    image_grad, text_grad, loss_rows = call(
        w_kernel,
        [VMEM] * 8,
        (scalars, slot6, z_w, grad_w, loss, unit_w, inverse_w, done_u),
        [ANY, ANY, VMEM],
        (block, block, line),
        "finish_w",
        (raw, raw, copies),
    )
    return loss_rows, image_grad, text_grad


def solution(mesh):
    in_specs = (P(AXES, None), P(AXES, None), P(), P())
    out_specs = (P(AXES), P(AXES, None), P(AXES, None))
    return jax.shard_map(local, mesh=mesh, in_specs=in_specs, out_specs=out_specs, check_vma=False)
```

```python
import jax
import jax.numpy as jnp
from jax import lax
from jax.experimental import pallas as pl
from jax.experimental.pallas import tpu as pltpu
from jax.sharding import PartitionSpec as P

SPAN = 4
GROUP = 4
AXES = ("blk", "inner")
F32 = jnp.float32
BF16 = jnp.bfloat16
VMEM_LIMIT = 16 * 1024 * 1024

X_SWAP = {0: (1, 0), 1: (0, 0), 2: (3, 0), 3: (2, 0)}
CORE_SWAP = {0: (2, 0), 1: (3, 0), 2: (0, 0), 3: (1, 0)}
GROUP_SHIFT = {0: (2, -1), 1: (3, -1), 2: (0, 1), 3: (1, 1)}


def send(value, moves):
    count = lax.axis_size(AXES)
    groups = count // GROUP
    pairs = [
        (g * GROUP + role, (g + step) % groups * GROUP + to)
        for g in range(groups)
        for role, (to, step) in moves.items()
    ]
    return lax.ppermute(value, AXES, pairs)


def unit_rows(raw):
    values = raw.astype(F32)
    inverse = 1.0 / jnp.sqrt(jnp.sum(values * values, axis=1, keepdims=True) + 1e-06)
    return values * inverse, inverse


def sigmoid_of(p):
    whole = 1.0 + p
    guess = pl.reciprocal(whole, approx=True)
    guess = guess * (2.0 - whole * guess)
    return p * (guess * (2.0 - whole * guess))


def log1p_of(p):
    below = p * (1.0 - p * (0.5 - p * (1.0 / 3.0)))
    return jnp.where(p < 0.015625, below, jnp.log(1.0 + p))


def softplus_lanes(p):
    total = None
    parts = [p[:, start : start + 128] for start in range(0, p.shape[1], 128)]
    for first in range(0, len(parts), 3):
        joint = parts[first]
        for part in parts[first + 1 : first + 3]:
            joint = joint + part + joint * part
        value = log1p_of(joint)
        total = value if total is None else total + value
    return total


def dot_nt(a, b):
    return lax.dot_general(a, b, (((1,), (1,)), ((), ())), preferred_element_type=F32)


def dot_nn(a, b):
    return lax.dot_general(a, b, (((1,), (0,)), ((), ())), preferred_element_type=F32)


def dot_tn(a, b):
    return lax.dot_general(a, b, (((0,), (0,)), ((), ())), preferred_element_type=F32)


def pair_step(own, blocks, scale, shift, work):
    rows = own.shape[0]
    for place, raw in enumerate(blocks):
        work[place * rows : (place + 1) * rows] = unit_rows(raw)[0].astype(BF16)
    return terms(own, work[: len(blocks) * rows], scale, shift)


def terms(own, others, scale, shift):
    p = jnp.exp(scale * dot_nt(own, others) + shift)
    coef = (sigmoid_of(p) * scale).astype(BF16)
    return dot_nn(coef, others), softplus_lanes(p)


def project(unit, inverse, grad):
    return ((grad - unit * jnp.sum(unit * grad, axis=1, keepdims=True)) * inverse).astype(BF16)


def row_parts(rows):
    count = 3 if rows % 48 == 0 else 1
    return [pl.ds(place * (rows // count), rows // count) for place in range(count)]


def scalar_pair(scalars):
    return scalars[0:1, 0:1], scalars[1:2, 0:1]


def image_is_u():
    return lax.rem(lax.axis_index("blk"), 2) == 0


def is_outer():
    return lax.rem(lax.axis_index("blk"), 2) == lax.axis_index("inner")


def sort_kernel(image, text, u, w, sems):
    def move(image_to, text_to):
        copies = [
            pltpu.make_async_copy(image, image_to, sems.at[0]),
            pltpu.make_async_copy(text, text_to, sems.at[1]),
        ]
        for copy in copies:
            copy.start()
        for copy in copies:
            copy.wait()

    u_is_image = image_is_u()

    @pl.when(u_is_image)
    def _():
        move(u, w)

    @pl.when(jnp.logical_not(u_is_image))
    def _():
        move(w, u)


def pick_kernel(when_outer, when_inner, picked, sem):
    @pl.when(is_outer())
    def _():
        pltpu.async_copy(when_outer, picked, sem).wait()

    @pl.when(jnp.logical_not(is_outer()))
    def _():
        pltpu.async_copy(when_inner, picked, sem).wait()


def near_kernel(
    scalars, image, text, b1, b2, b3,
    z_pair, unit_u, unit_w, inverse_u, inverse_w, grad_u, grad_w, loss, work, z_w,
):
    u_is_image = image_is_u()
    u_weight = u_is_image.astype(F32)
    scale, shift = scalar_pair(scalars)
    image_unit, image_inverse = unit_rows(image[...])
    text_unit, text_inverse = unit_rows(text[...])
    unit_u[...] = jnp.where(u_is_image, image_unit, text_unit)
    unit_w[...] = jnp.where(u_is_image, text_unit, image_unit)
    inverse_u[...] = jnp.where(u_is_image, image_inverse, text_inverse)
    inverse_w[...] = jnp.where(u_is_image, text_inverse, image_inverse)
    zi = image_unit.astype(BF16)
    zt = text_unit.astype(BF16)
    z_u = jnp.where(u_is_image, zi, zt)
    z_pair[: zi.shape[0]] = z_u
    z_w[...] = jnp.where(u_is_image, zt, zi)
    scores = scale * dot_nt(zi, zt) + shift
    rows = lax.broadcasted_iota(jnp.int32, scores.shape, 0)
    columns = lax.broadcasted_iota(jnp.int32, scores.shape, 1)
    sign = jnp.where(rows == columns, F32(-1.0), F32(1.0))
    p = jnp.exp(sign * scores)
    coef = (sign * sigmoid_of(p) * scale).astype(BF16)
    total = softplus_lanes(p)
    grad_image = dot_nn(coef, zt)
    grad_text = dot_tn(coef, zi)
    grad_u[...] = jnp.where(u_is_image, grad_image, grad_text)
    grad_w[...] = jnp.where(u_is_image, grad_text, grad_image)
    term, row_loss = pair_step(z_u, (b2[...],), scale, shift, work)
    grad_u[...] += term
    total = total + u_weight * row_loss
    term, row_loss = pair_step(z_w[...], (b1[...], b3[...]), scale, shift, work)
    z_pair[zi.shape[0] :] = work[: zi.shape[0]]
    grad_w[...] += term
    loss[...] = total + (1.0 - u_weight) * row_loss


def fifth_kernel(scalars, b5, z_pair, grad_in, loss_in, grad_u, loss, for_partner, raw, work, sems):
    copies = []
    rows, width = raw.shape
    for place, part in enumerate(row_parts(rows)):
        copy = pltpu.make_async_copy(b5.at[part], raw.at[part], sems.at[place])
        copy.start()
        copies.append((copy, part))
    for copy, part in copies:
        copy.wait()
        work[part] = unit_rows(raw[part])[0].astype(BF16)
    term, row_loss = terms(z_pair[...], work[...], *scalar_pair(scalars))
    for_partner[:, :width] = term[rows:].astype(BF16)
    for_partner[:, width:] = row_loss[rows:].astype(BF16)
    grad_u[...] = grad_in[...] + term[:rows]
    loss[...] = loss_in[...] + image_is_u().astype(F32) * row_loss[:rows]


def u_kernel(scalars, b4, z_pair, grad_u, loss_in, unit, inverse, done_u, loss, work):
    rows = done_u.shape[0]
    term, row_loss = pair_step(z_pair[:rows], (b4[...],), *scalar_pair(scalars), work)
    loss[...] = loss_in[...] + image_is_u().astype(F32) * row_loss
    done_u[...] = project(unit[...], inverse[...], grad_u[...] + term)


def w_kernel(
    last, grad_w, loss_in, unit, inverse, done_u, image_grad, text_grad, loss_rows, done_w, sems
):
    u_is_image = image_is_u()
    parts = row_parts(done_w.shape[0])

    def output(action, source, part, to_image, sem):
        @pl.when(to_image)
        def _():
            action(pltpu.make_async_copy(source.at[part], image_grad.at[part], sem))

        @pl.when(jnp.logical_not(to_image))
        def _():
            action(pltpu.make_async_copy(source.at[part], text_grad.at[part], sem))

    whole = pl.ds(0, done_w.shape[0])
    output(lambda copy: copy.start(), done_u, whole, u_is_image, sems.at[0])
    width = done_w.shape[1]
    for place, part in enumerate(parts):
        grad = grad_w[part] + last[part, :width].astype(F32)
        done_w[part] = project(unit[part], inverse[part], grad)
        output(lambda copy: copy.start(), done_w, part, jnp.logical_not(u_is_image), sems.at[1 + place])
    total = loss_in[...] + (1.0 - u_is_image.astype(F32)) * last[:, width:].astype(F32)
    loss_rows[...] = jnp.sum(jnp.transpose(total), axis=0) / (SPAN * total.shape[0])
    output(lambda copy: copy.wait(), done_u, whole, u_is_image, sems.at[0])
    for place, part in enumerate(parts):
        output(lambda copy: copy.wait(), done_w, part, jnp.logical_not(u_is_image), sems.at[1 + place])


VMEM = pl.BlockSpec(memory_space=pltpu.VMEM)
ANY = pl.BlockSpec(memory_space=pl.ANY)


def call(kernel, in_specs, args, out_specs, outs, name, scratch=(), flops=1):
    return pl.pallas_call(
        kernel,
        out_shape=outs,
        in_specs=in_specs,
        out_specs=out_specs,
        scratch_shapes=list(scratch),
        name=name,
        cost_estimate=pl.CostEstimate(flops=flops, bytes_accessed=1, transcendentals=0),
        compiler_params=pltpu.CompilerParams(vmem_limit_bytes=VMEM_LIMIT),
    )(*args)


def local(image, text, score_scaling, score_shift):
    rows, width = image.shape
    block = jax.ShapeDtypeStruct((rows, width), BF16)
    pair = jax.ShapeDtypeStruct((2 * rows, width), BF16)
    sums = jax.ShapeDtypeStruct((rows, width), F32)
    column = jax.ShapeDtypeStruct((rows, 1), F32)
    partial = jax.ShapeDtypeStruct((rows, 128), F32)
    line = jax.ShapeDtypeStruct((rows,), F32)
    raw = pltpu.VMEM((rows, width), BF16)
    copies = pltpu.SemaphoreType.DMA((4,))

    def pick(when_outer, when_inner):
        sem = pltpu.SemaphoreType.DMA
        return call(
            pick_kernel, [ANY] * 2, (when_outer, when_inner), [ANY], (block,), "pick", (sem,)
        )[0]

    def compute(kernel, args, outs, name, scratch, flops=1):
        in_specs = [VMEM] * (1 + len(args))
        out_specs = [VMEM] * len(outs)
        return call(kernel, in_specs, (scalars, *args), out_specs, outs, name, scratch, flops)

    u, w = call(
        sort_kernel,
        [ANY] * 2,
        [pltpu.with_memory_space_constraint(x, pltpu.HBM) for x in (image, text)],
        [VMEM] * 2,
        (block, block),
        "sort",
        (copies,),
    )
    slot1 = send(w, CORE_SWAP)
    slot2 = send(u, GROUP_SHIFT)
    slot3 = send(pick(slot1, u), X_SWAP)
    slot4 = send(slot3, GROUP_SHIFT)
    slot5 = send(pick(w, slot2), X_SWAP)
    slot3, score_scaling, score_shift = lax.optimization_barrier((slot3, score_scaling, score_shift))
    first = lax.broadcasted_iota(jnp.int32, (8, 128), 0) == 0
    scalars = jnp.where(first, score_scaling, score_shift)
    z_pair, unit_u, unit_w, inverse_u, inverse_w, grad_u, grad_w, loss = compute(
        near_kernel,
        (image, text, slot1, slot2, slot3),
        (pair, sums, sums, column, column, sums, sums, partial),
        "near_blocks",
        (pltpu.VMEM((2 * rows, width), BF16), raw),
    )
    grad_u, loss, for_partner = call(
        fifth_kernel,
        [VMEM, ANY, VMEM, VMEM, VMEM],
        (scalars, slot5, z_pair, grad_u, loss),
        [VMEM] * 3,
        (sums, partial, jax.ShapeDtypeStruct((rows, width + 128), BF16)),
        "fifth_block",
        (raw, raw, copies),
    )
    last = send(for_partner, CORE_SWAP)
    done_u, loss = compute(
        u_kernel,
        (slot4, z_pair, grad_u, loss, unit_u, inverse_u),
        (block, partial),
        "finish_u",
        (raw,),
        10**10,
    )
    image_grad, text_grad, loss_rows = call(
        w_kernel,
        [VMEM] * 6,
        (last, grad_w, loss, unit_w, inverse_w, done_u),
        [ANY, ANY, VMEM],
        (block, block, line),
        "finish_w",
        (raw, copies),
    )
    return loss_rows, image_grad, text_grad


def solution(mesh):
    in_specs = (P(AXES, None), P(AXES, None), P(), P())
    out_specs = (P(AXES), P(AXES, None), P(AXES, None))
    return jax.shard_map(local, mesh=mesh, in_specs=in_specs, out_specs=out_specs, check_vma=False)
```

```python
import jax
import jax.numpy as jnp
from jax import lax
from jax.experimental import pallas as pl
from jax.experimental.pallas import tpu as pltpu
from jax.sharding import PartitionSpec as P

SPAN = 4
GROUP = 4
AXES = ("blk", "inner")
F32 = jnp.float32
BF16 = jnp.bfloat16
VMEM_LIMIT = 16 * 1024 * 1024

X_SWAP = {0: (1, 0), 1: (0, 0), 2: (3, 0), 3: (2, 0)}
CORE_SWAP = {0: (2, 0), 1: (3, 0), 2: (0, 0), 3: (1, 0)}
GROUP_SHIFT = {0: (2, -1), 1: (3, -1), 2: (0, 1), 3: (1, 1)}


def send(value, moves):
    count = lax.axis_size(AXES)
    groups = count // GROUP
    pairs = [
        (g * GROUP + role, (g + step) % groups * GROUP + to)
        for g in range(groups)
        for role, (to, step) in moves.items()
    ]
    return lax.ppermute(value, AXES, pairs)


def unit_rows(raw):
    values = raw.astype(F32)
    inverse = 1.0 / jnp.sqrt(jnp.sum(values * values, axis=1, keepdims=True) + 1e-06)
    return values * inverse, inverse


def sigmoid_of(p):
    whole = 1.0 + p
    guess = pl.reciprocal(whole, approx=True)
    guess = guess * (2.0 - whole * guess)
    return p * (guess * (2.0 - whole * guess))


def log1p_of(p):
    below = p * (1.0 - p * (0.5 - p * (1.0 / 3.0)))
    return jnp.where(p < 0.015625, below, jnp.log(1.0 + p))


def softplus_lanes(p):
    total = None
    parts = [p[:, start : start + 128] for start in range(0, p.shape[1], 128)]
    for first in range(0, len(parts), 3):
        joint = parts[first]
        for part in parts[first + 1 : first + 3]:
            joint = joint + part + joint * part
        value = log1p_of(joint)
        total = value if total is None else total + value
    return total


def dot_nt(a, b):
    return lax.dot_general(a, b, (((1,), (1,)), ((), ())), preferred_element_type=F32)


def dot_nn(a, b):
    return lax.dot_general(a, b, (((1,), (0,)), ((), ())), preferred_element_type=F32)


def dot_tn(a, b):
    return lax.dot_general(a, b, (((0,), (0,)), ((), ())), preferred_element_type=F32)


def pair_step(own, blocks, scale, shift, work):
    rows = blocks[0].shape[0]
    for place, raw in enumerate(blocks):
        work[place * rows : (place + 1) * rows] = unit_rows(raw)[0].astype(BF16)
    return terms(own, work[: len(blocks) * rows], scale, shift)


def terms(own, others, scale, shift):
    p = jnp.exp(scale * dot_nt(own, others) + shift)
    coef = (sigmoid_of(p) * scale).astype(BF16)
    return dot_nn(coef, others), softplus_lanes(p)


def project(unit, inverse, grad):
    return ((grad - unit * jnp.sum(unit * grad, axis=1, keepdims=True)) * inverse).astype(BF16)


def row_parts(rows):
    count = 3 if rows % 48 == 0 else 1
    return [pl.ds(place * (rows // count), rows // count) for place in range(count)]


def scalar_pair(scalars):
    return scalars[0:1, 0:1], scalars[1:2, 0:1]


def image_is_u():
    return lax.rem(lax.axis_index("blk"), 2) == 0


def is_outer():
    return lax.rem(lax.axis_index("blk"), 2) == lax.axis_index("inner")


def sort_kernel(image, text, u, w, sems):
    def move(image_to, text_to):
        copies = [
            pltpu.make_async_copy(image, image_to, sems.at[0]),
            pltpu.make_async_copy(text, text_to, sems.at[1]),
        ]
        for copy in copies:
            copy.start()
        for copy in copies:
            copy.wait()

    u_is_image = image_is_u()

    @pl.when(u_is_image)
    def _():
        move(u, w)

    @pl.when(jnp.logical_not(u_is_image))
    def _():
        move(w, u)


def pick_kernel(when_outer, when_inner, picked, sem):
    @pl.when(is_outer())
    def _():
        pltpu.async_copy(when_outer, picked, sem).wait()

    @pl.when(jnp.logical_not(is_outer()))
    def _():
        pltpu.async_copy(when_inner, picked, sem).wait()


def near_kernel(
    scalars, image, text, b1, b2, b3,
    z_pair, unit_u, unit_w, inverse_u, inverse_w, grad_u, grad_w, loss, work, z_w,
):
    u_is_image = image_is_u()
    u_weight = u_is_image.astype(F32)
    scale, shift = scalar_pair(scalars)
    image_unit, image_inverse = unit_rows(image[...])
    text_unit, text_inverse = unit_rows(text[...])
    unit_u[...] = jnp.where(u_is_image, image_unit, text_unit)
    unit_w[...] = jnp.where(u_is_image, text_unit, image_unit)
    inverse_u[...] = jnp.where(u_is_image, image_inverse, text_inverse)
    inverse_w[...] = jnp.where(u_is_image, text_inverse, image_inverse)
    zi = image_unit.astype(BF16)
    zt = text_unit.astype(BF16)
    z_u = jnp.where(u_is_image, zi, zt)
    z_pair[: zi.shape[0]] = z_u
    z_w[...] = jnp.where(u_is_image, zt, zi)
    scores = scale * dot_nt(zi, zt) + shift
    rows = lax.broadcasted_iota(jnp.int32, scores.shape, 0)
    columns = lax.broadcasted_iota(jnp.int32, scores.shape, 1)
    sign = jnp.where(rows == columns, F32(-1.0), F32(1.0))
    p = jnp.exp(sign * scores)
    coef = (sign * sigmoid_of(p) * scale).astype(BF16)
    total = softplus_lanes(p)
    grad_image = dot_nn(coef, zt)
    grad_text = dot_tn(coef, zi)
    grad_u[...] = jnp.where(u_is_image, grad_image, grad_text)
    grad_w[...] = jnp.where(u_is_image, grad_text, grad_image)
    term, row_loss = pair_step(z_u, (b2[...],), scale, shift, work)
    grad_u[...] += term
    total = total + u_weight * row_loss
    term, row_loss = pair_step(z_w[...], (b1[...], b3[...]), scale, shift, work)
    z_pair[zi.shape[0] :] = work[: zi.shape[0]]
    grad_w[...] += term
    loss[...] = total + (1.0 - u_weight) * row_loss


def fifth_kernel(scalars, b5, z_pair, grad_in, loss_in, grad_u, loss, for_partner, work):
    rows, width = b5.shape
    term, row_loss = pair_step(z_pair[...], (b5[...],), *scalar_pair(scalars), work)
    for_partner[:, :width] = term[rows:].astype(BF16)
    for_partner[:, width:] = row_loss[rows:].astype(BF16)
    grad_u[...] = grad_in[...] + term[:rows]
    loss[...] = loss_in[...] + image_is_u().astype(F32) * row_loss[:rows]


def u_kernel(scalars, b4, z_pair, grad_u, loss_in, unit, inverse, done_u, loss, work):
    rows = done_u.shape[0]
    term, row_loss = pair_step(z_pair[:rows], (b4[...],), *scalar_pair(scalars), work)
    loss[...] = loss_in[...] + image_is_u().astype(F32) * row_loss
    done_u[...] = project(unit[...], inverse[...], grad_u[...] + term)


def w_kernel(
    last, grad_w, loss_in, unit, inverse, done_u, image_grad, text_grad, loss_rows, done_w, sems
):
    u_is_image = image_is_u()
    parts = row_parts(done_w.shape[0])

    def output(action, source, part, to_image, sem):
        @pl.when(to_image)
        def _():
            action(pltpu.make_async_copy(source.at[part], image_grad.at[part], sem))

        @pl.when(jnp.logical_not(to_image))
        def _():
            action(pltpu.make_async_copy(source.at[part], text_grad.at[part], sem))

    whole = pl.ds(0, done_w.shape[0])
    output(lambda copy: copy.start(), done_u, whole, u_is_image, sems.at[0])
    width = done_w.shape[1]
    for place, part in enumerate(parts):
        grad = grad_w[part] + last[part, :width].astype(F32)
        done_w[part] = project(unit[part], inverse[part], grad)
        output(lambda copy: copy.start(), done_w, part, jnp.logical_not(u_is_image), sems.at[1 + place])
    total = loss_in[...] + (1.0 - u_is_image.astype(F32)) * last[:, width:].astype(F32)
    loss_rows[...] = jnp.sum(jnp.transpose(total), axis=0) / (SPAN * total.shape[0])
    output(lambda copy: copy.wait(), done_u, whole, u_is_image, sems.at[0])
    for place, part in enumerate(parts):
        output(lambda copy: copy.wait(), done_w, part, jnp.logical_not(u_is_image), sems.at[1 + place])


VMEM = pl.BlockSpec(memory_space=pltpu.VMEM)
ANY = pl.BlockSpec(memory_space=pl.ANY)


def call(kernel, in_specs, args, out_specs, outs, name, scratch=(), flops=1):
    return pl.pallas_call(
        kernel,
        out_shape=outs,
        in_specs=in_specs,
        out_specs=out_specs,
        scratch_shapes=list(scratch),
        name=name,
        cost_estimate=pl.CostEstimate(flops=flops, bytes_accessed=1, transcendentals=0),
        compiler_params=pltpu.CompilerParams(vmem_limit_bytes=VMEM_LIMIT),
    )(*args)


def local(image, text, score_scaling, score_shift):
    rows, width = image.shape
    block = jax.ShapeDtypeStruct((rows, width), BF16)
    pair = jax.ShapeDtypeStruct((2 * rows, width), BF16)
    sums = jax.ShapeDtypeStruct((rows, width), F32)
    column = jax.ShapeDtypeStruct((rows, 1), F32)
    partial = jax.ShapeDtypeStruct((rows, 128), F32)
    line = jax.ShapeDtypeStruct((rows,), F32)
    raw = pltpu.VMEM((rows, width), BF16)
    copies = pltpu.SemaphoreType.DMA((4,))
    in_hbm = [pltpu.with_memory_space_constraint(x, pltpu.HBM) for x in (image, text)]

    def pick(when_outer, when_inner):
        sem = pltpu.SemaphoreType.DMA
        return call(
            pick_kernel, [ANY] * 2, (when_outer, when_inner), [ANY], (block,), "pick", (sem,)
        )[0]

    def compute(kernel, args, outs, name, scratch, flops=1):
        in_specs = [VMEM] * (1 + len(args))
        out_specs = [VMEM] * len(outs)
        return call(kernel, in_specs, (scalars, *args), out_specs, outs, name, scratch, flops)

    u, w = call(
        sort_kernel,
        [ANY] * 2,
        in_hbm,
        [VMEM] * 2,
        (block, block),
        "sort",
        (copies,),
    )
    slot1 = send(w, CORE_SWAP)
    slot2 = send(u, GROUP_SHIFT)
    slot3 = send(pick(slot1, u), X_SWAP)
    slot4 = send(slot3, GROUP_SHIFT)
    slot5 = send(pick(w, slot2), X_SWAP)
    slot3, score_scaling, score_shift = lax.optimization_barrier((slot3, score_scaling, score_shift))
    first = lax.broadcasted_iota(jnp.int32, (8, 128), 0) == 0
    scalars = jnp.where(first, score_scaling, score_shift)
    z_pair, unit_u, unit_w, inverse_u, inverse_w, grad_u, grad_w, loss = compute(
        near_kernel,
        (*in_hbm, slot1, slot2, slot3),
        (pair, sums, sums, column, column, sums, sums, partial),
        "near_blocks",
        (pltpu.VMEM((2 * rows, width), BF16), raw),
    )
    grad_u, loss, for_partner = compute(
        fifth_kernel,
        (pltpu.with_memory_space_constraint(slot5, pltpu.VMEM), z_pair, grad_u, loss),
        (sums, partial, jax.ShapeDtypeStruct((rows, width + 128), BF16)),
        "fifth_block",
        (raw,),
    )
    last = send(for_partner, CORE_SWAP)
    done_u, loss = compute(
        u_kernel,
        (pltpu.with_memory_space_constraint(slot4, pltpu.VMEM), z_pair, grad_u, loss, unit_u, inverse_u),
        (block, partial),
        "finish_u",
        (raw,),
        10**10,
    )
    image_grad, text_grad, loss_rows = call(
        w_kernel,
        [VMEM] * 6,
        (last, grad_w, loss, unit_w, inverse_w, done_u),
        [ANY, ANY, VMEM],
        (block, block, line),
        "finish_w",
        (raw, copies),
    )
    return loss_rows, image_grad, text_grad


def solution(mesh):
    in_specs = (P(AXES, None), P(AXES, None), P(), P())
    out_specs = (P(AXES), P(AXES, None), P(AXES, None))
    return jax.shard_map(local, mesh=mesh, in_specs=in_specs, out_specs=out_specs, check_vma=False)
```

```python
import jax
import jax.numpy as jnp
from jax import lax
from jax.experimental import pallas as pl
from jax.experimental.pallas import tpu as pltpu
from jax.sharding import PartitionSpec as P

SPAN = 4
GROUP = 4
AXES = ("blk", "inner")
F32 = jnp.float32
BF16 = jnp.bfloat16
VMEM_LIMIT = 16 * 1024 * 1024

X_SWAP = {0: (1, 0), 1: (0, 0), 2: (3, 0), 3: (2, 0)}
CORE_SWAP = {0: (2, 0), 1: (3, 0), 2: (0, 0), 3: (1, 0)}
GROUP_SHIFT = {0: (2, -1), 1: (3, -1), 2: (0, 1), 3: (1, 1)}


def send(value, moves):
    count = lax.axis_size(AXES)
    groups = count // GROUP
    pairs = [
        (g * GROUP + role, (g + step) % groups * GROUP + to)
        for g in range(groups)
        for role, (to, step) in moves.items()
    ]
    return lax.ppermute(value, AXES, pairs)


def unit_rows(raw):
    values = raw.astype(F32)
    inverse = 1.0 / jnp.sqrt(jnp.sum(values * values, axis=1, keepdims=True) + 1e-06)
    return values * inverse, inverse


def sigmoid_of(p):
    whole = 1.0 + p
    guess = pl.reciprocal(whole, approx=True)
    guess = guess * (2.0 - whole * guess)
    return p * (guess * (2.0 - whole * guess))


def log1p_of(p):
    below = p * (1.0 - p * (0.5 - p * (1.0 / 3.0)))
    return jnp.where(p < 0.015625, below, jnp.log(1.0 + p))


def softplus_lanes(p):
    total = None
    parts = [p[:, start : start + 128] for start in range(0, p.shape[1], 128)]
    for first in range(0, len(parts), 3):
        joint = parts[first]
        for part in parts[first + 1 : first + 3]:
            joint = joint + part + joint * part
        value = log1p_of(joint)
        total = value if total is None else total + value
    return total


def dot_nt(a, b):
    return lax.dot_general(a, b, (((1,), (1,)), ((), ())), preferred_element_type=F32)


def dot_nn(a, b):
    return lax.dot_general(a, b, (((1,), (0,)), ((), ())), preferred_element_type=F32)


def dot_tn(a, b):
    return lax.dot_general(a, b, (((0,), (0,)), ((), ())), preferred_element_type=F32)


def pair_step(own, blocks, scale, shift, work):
    rows = blocks[0].shape[0]
    for place, raw in enumerate(blocks):
        work[place * rows : (place + 1) * rows] = unit_rows(raw)[0].astype(BF16)
    return terms(own, work[: len(blocks) * rows], scale, shift)


def terms(own, others, scale, shift):
    p = jnp.exp(scale * dot_nt(own, others) + shift)
    coef = (sigmoid_of(p) * scale).astype(BF16)
    return dot_nn(coef, others), softplus_lanes(p)


def project(unit, inverse, grad):
    return ((grad - unit * jnp.sum(unit * grad, axis=1, keepdims=True)) * inverse).astype(BF16)


def row_parts(rows):
    count = 3 if rows % 48 == 0 else 1
    return [pl.ds(place * (rows // count), rows // count) for place in range(count)]


def scalar_pair(scalars):
    return scalars[0:1, 0:1], scalars[1:2, 0:1]


def image_is_u():
    return lax.rem(lax.axis_index("blk"), 2) == 0


def is_outer():
    return lax.rem(lax.axis_index("blk"), 2) == lax.axis_index("inner")


def sort_kernel(image, text, u, w, sems):
    def move(image_to, text_to):
        copies = [
            pltpu.make_async_copy(image, image_to, sems.at[0]),
            pltpu.make_async_copy(text, text_to, sems.at[1]),
        ]
        for copy in copies:
            copy.start()
        for copy in copies:
            copy.wait()

    u_is_image = image_is_u()

    @pl.when(u_is_image)
    def _():
        move(u, w)

    @pl.when(jnp.logical_not(u_is_image))
    def _():
        move(w, u)


def pick_kernel(when_outer, when_inner, picked, sem):
    @pl.when(is_outer())
    def _():
        pltpu.async_copy(when_outer, picked, sem).wait()

    @pl.when(jnp.logical_not(is_outer()))
    def _():
        pltpu.async_copy(when_inner, picked, sem).wait()


def near_kernel(
    scalars, image, text, b1, b2, b3,
    z_pair, unit_u, unit_w, inverse_u, inverse_w, grad_u, grad_w, loss, work, z_w,
):
    u_is_image = image_is_u()
    u_weight = u_is_image.astype(F32)
    scale, shift = scalar_pair(scalars)
    image_unit, image_inverse = unit_rows(image[...])
    text_unit, text_inverse = unit_rows(text[...])
    unit_u[...] = jnp.where(u_is_image, image_unit, text_unit)
    unit_w[...] = jnp.where(u_is_image, text_unit, image_unit)
    inverse_u[...] = jnp.where(u_is_image, image_inverse, text_inverse)
    inverse_w[...] = jnp.where(u_is_image, text_inverse, image_inverse)
    zi = image_unit.astype(BF16)
    zt = text_unit.astype(BF16)
    z_u = jnp.where(u_is_image, zi, zt)
    z_pair[: zi.shape[0]] = z_u
    z_w[...] = jnp.where(u_is_image, zt, zi)
    scores = scale * dot_nt(zi, zt) + shift
    rows = lax.broadcasted_iota(jnp.int32, scores.shape, 0)
    columns = lax.broadcasted_iota(jnp.int32, scores.shape, 1)
    sign = jnp.where(rows == columns, F32(-1.0), F32(1.0))
    p = jnp.exp(sign * scores)
    coef = (sign * sigmoid_of(p) * scale).astype(BF16)
    total = softplus_lanes(p)
    grad_image = dot_nn(coef, zt)
    grad_text = dot_tn(coef, zi)
    grad_u[...] = jnp.where(u_is_image, grad_image, grad_text)
    grad_w[...] = jnp.where(u_is_image, grad_text, grad_image)
    term, row_loss = pair_step(z_u, (b2[...],), scale, shift, work)
    grad_u[...] += term
    total = total + u_weight * row_loss
    term, row_loss = pair_step(z_w[...], (b1[...], b3[...]), scale, shift, work)
    z_pair[zi.shape[0] :] = work[: zi.shape[0]]
    grad_w[...] += term
    loss[...] = total + (1.0 - u_weight) * row_loss


def fifth_kernel(scalars, b5, z_pair, grad_in, loss_in, grad_u, loss, for_partner, work):
    rows, width = b5.shape
    term, row_loss = pair_step(z_pair[...], (b5[...],), *scalar_pair(scalars), work)
    for_partner[:, :width] = term[rows:].astype(BF16)
    for_partner[:, width:] = row_loss[rows:].astype(BF16)
    grad_u[...] = grad_in[...] + term[:rows]
    loss[...] = loss_in[...] + image_is_u().astype(F32) * row_loss[:rows]


def u_kernel(scalars, b4, z_pair, grad_u, loss_in, unit, inverse, done_u, loss, work):
    rows = done_u.shape[0]
    term, row_loss = pair_step(z_pair[:rows], (b4[...],), *scalar_pair(scalars), work)
    loss[...] = loss_in[...] + image_is_u().astype(F32) * row_loss
    done_u[...] = project(unit[...], inverse[...], grad_u[...] + term)


def w_kernel(
    last, grad_w, loss_in, unit, inverse, done_u, image_grad, text_grad, loss_rows, done_w, sems
):
    u_is_image = image_is_u()
    parts = row_parts(done_w.shape[0])

    def output(action, source, part, to_image, sem):
        @pl.when(to_image)
        def _():
            action(pltpu.make_async_copy(source.at[part], image_grad.at[part], sem))

        @pl.when(jnp.logical_not(to_image))
        def _():
            action(pltpu.make_async_copy(source.at[part], text_grad.at[part], sem))

    whole = pl.ds(0, done_w.shape[0])
    output(lambda copy: copy.start(), done_u, whole, u_is_image, sems.at[0])
    width = done_w.shape[1]
    for place, part in enumerate(parts):
        grad = grad_w[part] + last[part, :width].astype(F32)
        done_w[part] = project(unit[part], inverse[part], grad)
        output(lambda copy: copy.start(), done_w, part, jnp.logical_not(u_is_image), sems.at[1 + place])
    total = loss_in[...] + (1.0 - u_is_image.astype(F32)) * last[:, width:].astype(F32)
    loss_rows[...] = jnp.sum(jnp.transpose(total), axis=0) / (SPAN * total.shape[0])
    output(lambda copy: copy.wait(), done_u, whole, u_is_image, sems.at[0])
    for place, part in enumerate(parts):
        output(lambda copy: copy.wait(), done_w, part, jnp.logical_not(u_is_image), sems.at[1 + place])


VMEM = pl.BlockSpec(memory_space=pltpu.VMEM)
ANY = pl.BlockSpec(memory_space=pl.ANY)


def call(kernel, in_specs, args, out_specs, outs, name, scratch=(), flops=1):
    return pl.pallas_call(
        kernel,
        out_shape=outs,
        in_specs=in_specs,
        out_specs=out_specs,
        scratch_shapes=list(scratch),
        name=name,
        cost_estimate=pl.CostEstimate(flops=flops, bytes_accessed=1, transcendentals=0),
        compiler_params=pltpu.CompilerParams(vmem_limit_bytes=VMEM_LIMIT),
    )(*args)


def local(image, text, score_scaling, score_shift):
    rows, width = image.shape
    block = jax.ShapeDtypeStruct((rows, width), BF16)
    pair = jax.ShapeDtypeStruct((2 * rows, width), BF16)
    sums = jax.ShapeDtypeStruct((rows, width), F32)
    column = jax.ShapeDtypeStruct((rows, 1), F32)
    partial = jax.ShapeDtypeStruct((rows, 128), F32)
    line = jax.ShapeDtypeStruct((rows,), F32)
    raw = pltpu.VMEM((rows, width), BF16)
    copies = pltpu.SemaphoreType.DMA((4,))

    def in_hbm(*arrays):
        return [pltpu.with_memory_space_constraint(x, pltpu.HBM) for x in arrays]


    def pick(when_outer, when_inner, out):
        sem = pltpu.SemaphoreType.DMA
        return call(
            pick_kernel, [ANY] * 2, (when_outer, when_inner), [ANY], (out,), "pick", (sem,)
        )[0]

    def compute(kernel, args, outs, name, scratch, flops=1):
        in_specs = [VMEM] * (1 + len(args))
        out_specs = [VMEM] * len(outs)
        return call(kernel, in_specs, (scalars, *args), out_specs, outs, name, scratch, flops)

    u, w = call(
        sort_kernel,
        [ANY] * 2,
        in_hbm(image, text),
        [VMEM] * 2,
        (block, block),
        "sort",
        (copies,),
    )
    slot1 = send(w, CORE_SWAP)
    slot2 = send(u, GROUP_SHIFT)
    slot3 = send(pick(slot1, u, block), X_SWAP)
    slot4 = send(slot3, GROUP_SHIFT)
    slot5 = send(pick(w, slot2, pltpu.HBM((rows, width), BF16)), X_SWAP)
    slot3, score_scaling, score_shift = lax.optimization_barrier((slot3, score_scaling, score_shift))
    first = lax.broadcasted_iota(jnp.int32, (8, 128), 0) == 0
    scalars = jnp.where(first, score_scaling, score_shift)
    z_pair, unit_u, unit_w, inverse_u, inverse_w, grad_u, grad_w, loss = compute(
        near_kernel,
        (*in_hbm(image, text), slot1, *in_hbm(slot2, slot3)),
        (pair, sums, sums, column, column, sums, sums, partial),
        "near_blocks",
        (pltpu.VMEM((2 * rows, width), BF16), raw),
    )
    grad_u, loss, for_partner = compute(
        fifth_kernel,
        (pltpu.with_memory_space_constraint(slot5, pltpu.VMEM), z_pair, grad_u, loss),
        (sums, partial, jax.ShapeDtypeStruct((rows, width + 128), BF16)),
        "fifth_block",
        (raw,),
    )
    last = send(for_partner, CORE_SWAP)
    done_u, loss = compute(
        u_kernel,
        (pltpu.with_memory_space_constraint(slot4, pltpu.VMEM), z_pair, grad_u, loss, unit_u, inverse_u),
        (block, partial),
        "finish_u",
        (raw,),
        10**10,
    )
    image_grad, text_grad, loss_rows = call(
        w_kernel,
        [VMEM] * 6,
        (last, grad_w, loss, unit_w, inverse_w, done_u),
        [ANY, ANY, VMEM],
        (block, block, line),
        "finish_w",
        (raw, copies),
    )
    return loss_rows, image_grad, text_grad


def solution(mesh):
    in_specs = (P(AXES, None), P(AXES, None), P(), P())
    out_specs = (P(AXES), P(AXES, None), P(AXES, None))
    return jax.shard_map(local, mesh=mesh, in_specs=in_specs, out_specs=out_specs, check_vma=False)
```

```python
import jax
import jax.numpy as jnp
from jax import lax
from jax.experimental import pallas as pl
from jax.experimental.pallas import tpu as pltpu
from jax.sharding import PartitionSpec as P

SPAN = 4
GROUP = 4
AXES = ("blk", "inner")
F32 = jnp.float32
BF16 = jnp.bfloat16
VMEM_LIMIT = 16 * 1024 * 1024

CYCLE = {0: (2, 0), 1: (0, 0), 2: (3, 0), 3: (1, 0)}
TEXT_BY_TWO = {0: (2, 0), 1: (3, 0), 2: (0, 1), 3: (1, 1)}
IMAGE_BY_TWO = {0: (2, -1), 1: (3, -1), 2: (0, 0), 3: (1, 0)}
X_SWAP = {0: (1, 0), 1: (0, 0), 2: (3, 0), 3: (2, 0)}
CORE_SWAP = {0: (2, 0), 1: (3, 0), 2: (0, 0), 3: (1, 0)}
OUTER_RELAY = {0: (2, -1), 1: (3, 0), 2: (0, 0), 3: (1, 1)}
INNER_RELAY = {0: (2, 0), 1: (3, -1), 2: (0, 1), 3: (1, 0)}


def send(value, moves):
    count = lax.axis_size(AXES)
    groups = count // GROUP
    pairs = [
        (g * GROUP + role, (g + step) % groups * GROUP + to)
        for g in range(groups)
        for role, (to, step) in moves.items()
    ]
    return lax.ppermute(value, AXES, pairs)


def unit_rows(raw):
    values = raw.astype(F32)
    inverse = 1.0 / jnp.sqrt(jnp.sum(values * values, axis=1, keepdims=True) + 1e-06)
    return values * inverse, inverse


def sigmoid_of(p):
    whole = 1.0 + p
    guess = pl.reciprocal(whole, approx=True)
    guess = guess * (2.0 - whole * guess)
    return p * (guess * (2.0 - whole * guess))


def log1p_of(p):
    below = p * (1.0 - p * (0.5 - p * (1.0 / 3.0)))
    return jnp.where(p < 0.015625, below, jnp.log(1.0 + p))


def softplus_lanes(p):
    total = None
    parts = [p[:, start : start + 128] for start in range(0, p.shape[1], 128)]
    for first in range(0, len(parts), 3):
        joint = parts[first]
        for part in parts[first + 1 : first + 3]:
            joint = joint + part + joint * part
        value = log1p_of(joint)
        total = value if total is None else total + value
    return total


def dot_nt(a, b):
    return lax.dot_general(a, b, (((1,), (1,)), ((), ())), preferred_element_type=F32)


def dot_nn(a, b):
    return lax.dot_general(a, b, (((1,), (0,)), ((), ())), preferred_element_type=F32)


def dot_tn(a, b):
    return lax.dot_general(a, b, (((0,), (0,)), ((), ())), preferred_element_type=F32)


def pair_step(own, blocks, scale, shift, work):
    rows = blocks[0].shape[0]
    for place, raw in enumerate(blocks):
        work[place * rows : (place + 1) * rows] = unit_rows(raw)[0].astype(BF16)
    return terms(own, work[: len(blocks) * rows], scale, shift)


def terms(own, others, scale, shift):
    p = jnp.exp(scale * dot_nt(own, others) + shift)
    coef = (sigmoid_of(p) * scale).astype(BF16)
    return dot_nn(coef, others), softplus_lanes(p)


def project(unit, inverse, grad):
    return ((grad - unit * jnp.sum(unit * grad, axis=1, keepdims=True)) * inverse).astype(BF16)


def row_parts(rows):
    count = 3 if rows % 48 == 0 else 1
    return [pl.ds(place * (rows // count), rows // count) for place in range(count)]


def scalar_pair(scalars):
    return scalars[0:1, 0:1], scalars[1:2, 0:1]


def image_is_u():
    return lax.rem(lax.axis_index("blk"), 2) == 0


def is_outer():
    return lax.rem(lax.axis_index("blk"), 2) == lax.axis_index("inner")


def when(condition, then):
    pl.when(condition)(then)


def sort_kernel(image, text, u, w, sems):
    def move(image_to, text_to):
        copies = [
            pltpu.make_async_copy(image, image_to, sems.at[0]),
            pltpu.make_async_copy(text, text_to, sems.at[1]),
        ]
        for copy in copies:
            copy.start()
        for copy in copies:
            copy.wait()

    when(image_is_u(), lambda: move(u, w))
    when(jnp.logical_not(image_is_u()), lambda: move(w, u))


def pick_kernel(outer_u, outer_w, inner_u, inner_w, picked, sem):
    def move(source):
        pltpu.async_copy(source, picked, sem).wait()

    u_is_image, outer = image_is_u(), is_outer()
    inner, w_is_image = jnp.logical_not(outer), jnp.logical_not(u_is_image)
    when(jnp.logical_and(outer, u_is_image), lambda: move(outer_u))
    when(jnp.logical_and(outer, w_is_image), lambda: move(outer_w))
    when(jnp.logical_and(inner, u_is_image), lambda: move(inner_u))
    when(jnp.logical_and(inner, w_is_image), lambda: move(inner_w))


def near_kernel(
    scalars, image, text, image_two, text_two, outer_b3, inner_b3,
    z_pair, unit_u, unit_w, inverse_u, inverse_w, grad_u, grad_w, loss, work, z_w,
):
    u_is_image = image_is_u()
    u_weight = u_is_image.astype(F32)
    scale, shift = scalar_pair(scalars)
    image_unit, image_inverse = unit_rows(image[...])
    text_unit, text_inverse = unit_rows(text[...])
    unit_u[...] = jnp.where(u_is_image, image_unit, text_unit)
    unit_w[...] = jnp.where(u_is_image, text_unit, image_unit)
    inverse_u[...] = jnp.where(u_is_image, image_inverse, text_inverse)
    inverse_w[...] = jnp.where(u_is_image, text_inverse, image_inverse)
    zi = image_unit.astype(BF16)
    zt = text_unit.astype(BF16)
    z_u = jnp.where(u_is_image, zi, zt)
    z_pair[: zi.shape[0]] = z_u
    b1 = jnp.where(u_is_image, image_two[...], text_two[...])
    b2 = jnp.where(u_is_image, text_two[...], image_two[...])
    b3 = jnp.where(is_outer(), outer_b3[...], inner_b3[...])
    z_w[...] = jnp.where(u_is_image, zt, zi)
    scores = scale * dot_nt(zi, zt) + shift
    rows = lax.broadcasted_iota(jnp.int32, scores.shape, 0)
    columns = lax.broadcasted_iota(jnp.int32, scores.shape, 1)
    sign = jnp.where(rows == columns, F32(-1.0), F32(1.0))
    p = jnp.exp(sign * scores)
    coef = (sign * sigmoid_of(p) * scale).astype(BF16)
    total = softplus_lanes(p)
    grad_image = dot_nn(coef, zt)
    grad_text = dot_tn(coef, zi)
    grad_u[...] = jnp.where(u_is_image, grad_image, grad_text)
    grad_w[...] = jnp.where(u_is_image, grad_text, grad_image)
    term, row_loss = pair_step(z_u, (b2,), scale, shift, work)
    grad_u[...] += term
    total = total + u_weight * row_loss
    term, row_loss = pair_step(z_w[...], (b1, b3), scale, shift, work)
    z_pair[zi.shape[0] :] = work[: zi.shape[0]]
    grad_w[...] += term
    loss[...] = total + (1.0 - u_weight) * row_loss


def fifth_kernel(scalars, b5, z_pair, grad_in, loss_in, grad_u, loss, for_partner, work):
    rows, width = b5.shape
    term, row_loss = pair_step(z_pair[...], (b5[...],), *scalar_pair(scalars), work)
    for_partner[:, :width] = term[rows:].astype(BF16)
    for_partner[:, width:] = row_loss[rows:].astype(BF16)
    grad_u[...] = grad_in[...] + term[:rows]
    loss[...] = loss_in[...] + image_is_u().astype(F32) * row_loss[:rows]


def u_kernel(scalars, outer_b4, inner_b4, z_pair, grad_u, loss_in, unit, inverse, done_u, loss, work):
    rows = done_u.shape[0]
    b4 = jnp.where(is_outer(), outer_b4[...], inner_b4[...])
    term, row_loss = pair_step(z_pair[:rows], (b4,), *scalar_pair(scalars), work)
    loss[...] = loss_in[...] + image_is_u().astype(F32) * row_loss
    done_u[...] = project(unit[...], inverse[...], grad_u[...] + term)


def w_kernel(
    last, grad_w, loss_in, unit, inverse, done_u, image_grad, text_grad, loss_rows, done_w, sems
):
    u_is_image = image_is_u()
    parts = row_parts(done_w.shape[0])

    def output(action, source, part, to_image, sem):
        @pl.when(to_image)
        def _():
            action(pltpu.make_async_copy(source.at[part], image_grad.at[part], sem))

        @pl.when(jnp.logical_not(to_image))
        def _():
            action(pltpu.make_async_copy(source.at[part], text_grad.at[part], sem))

    whole = pl.ds(0, done_w.shape[0])
    output(lambda copy: copy.start(), done_u, whole, u_is_image, sems.at[0])
    width = done_w.shape[1]
    for place, part in enumerate(parts):
        grad = grad_w[part] + last[part, :width].astype(F32)
        done_w[part] = project(unit[part], inverse[part], grad)
        output(lambda copy: copy.start(), done_w, part, jnp.logical_not(u_is_image), sems.at[1 + place])
    total = loss_in[...] + (1.0 - u_is_image.astype(F32)) * last[:, width:].astype(F32)
    loss_rows[...] = jnp.sum(jnp.transpose(total), axis=0) / (SPAN * total.shape[0])
    output(lambda copy: copy.wait(), done_u, whole, u_is_image, sems.at[0])
    for place, part in enumerate(parts):
        output(lambda copy: copy.wait(), done_w, part, jnp.logical_not(u_is_image), sems.at[1 + place])


VMEM = pl.BlockSpec(memory_space=pltpu.VMEM)
ANY = pl.BlockSpec(memory_space=pl.ANY)


def call(kernel, in_specs, args, out_specs, outs, name, scratch=(), flops=1):
    return pl.pallas_call(
        kernel,
        out_shape=outs,
        in_specs=in_specs,
        out_specs=out_specs,
        scratch_shapes=list(scratch),
        name=name,
        cost_estimate=pl.CostEstimate(flops=flops, bytes_accessed=1, transcendentals=0),
        compiler_params=pltpu.CompilerParams(vmem_limit_bytes=VMEM_LIMIT),
    )(*args)


def local(image, text, score_scaling, score_shift):
    rows, width = image.shape
    block = jax.ShapeDtypeStruct((rows, width), BF16)
    pair = jax.ShapeDtypeStruct((2 * rows, width), BF16)
    sums = jax.ShapeDtypeStruct((rows, width), F32)
    column = jax.ShapeDtypeStruct((rows, 1), F32)
    partial = jax.ShapeDtypeStruct((rows, 128), F32)
    line = jax.ShapeDtypeStruct((rows,), F32)
    raw = pltpu.VMEM((rows, width), BF16)
    copies = pltpu.SemaphoreType.DMA((4,))

    def in_hbm(*arrays):
        return [pltpu.with_memory_space_constraint(x, pltpu.HBM) for x in arrays]


    def in_vmem(*arrays):
        return [pltpu.with_memory_space_constraint(x, pltpu.VMEM) for x in arrays]

    def compute(kernel, args, outs, name, scratch, flops=1):
        in_specs = [VMEM] * (1 + len(args))
        out_specs = [VMEM] * len(outs)
        return call(kernel, in_specs, (scalars, *args), out_specs, outs, name, scratch, flops)

    text_cycle = send(text, CYCLE)
    image_cycle = send(image, CYCLE)
    text_two = send(text, TEXT_BY_TWO)
    image_two = send(image, IMAGE_BY_TWO)
    slot5 = send(
        call(
            pick_kernel,
            [ANY] * 4,
            (text, image, text_two, image_two),
            [ANY],
            (pltpu.HBM((rows, width), BF16),),
            "pick",
            (pltpu.SemaphoreType.DMA,),
        )[0],
        X_SWAP,
    )
    outer_b3, crossing = call(
        sort_kernel, [ANY] * 2, (image_cycle, text_cycle), [ANY] * 2, (block, block), "sort", (copies,)
    )
    inner_b4 = send(outer_b3, OUTER_RELAY)
    inner_b3 = send(crossing, CORE_SWAP)
    outer_b4 = send(inner_b3, INNER_RELAY)
    first = lax.broadcasted_iota(jnp.int32, (8, 128), 0) == 0
    scalars = jnp.where(first, score_scaling, score_shift)
    z_pair, unit_u, unit_w, inverse_u, inverse_w, grad_u, grad_w, loss = compute(
        near_kernel,
        in_hbm(image, text, image_two, text_two, outer_b3, inner_b3),
        (pair, sums, sums, column, column, sums, sums, partial),
        "near_blocks",
        (pltpu.VMEM((2 * rows, width), BF16), raw),
    )
    grad_u, loss, for_partner = compute(
        fifth_kernel,
        (*in_vmem(slot5), z_pair, grad_u, loss),
        (sums, partial, jax.ShapeDtypeStruct((rows, width + 128), BF16)),
        "fifth_block",
        (raw,),
    )
    last = send(for_partner, CORE_SWAP)
    done_u, loss = compute(
        u_kernel,
        (*in_vmem(outer_b4, inner_b4), z_pair, grad_u, loss, unit_u, inverse_u),
        (block, partial),
        "finish_u",
        (raw,),
        10**10,
    )
    image_grad, text_grad, loss_rows = call(
        w_kernel,
        [VMEM] * 6,
        (last, grad_w, loss, unit_w, inverse_w, done_u),
        [ANY, ANY, VMEM],
        (block, block, line),
        "finish_w",
        (raw, copies),
    )
    return loss_rows, image_grad, text_grad


def solution(mesh):
    in_specs = (P(AXES, None), P(AXES, None), P(), P())
    out_specs = (P(AXES), P(AXES, None), P(AXES, None))
    return jax.shard_map(local, mesh=mesh, in_specs=in_specs, out_specs=out_specs, check_vma=False)
```

```python
import jax
import jax.numpy as jnp
from jax import lax
from jax.experimental import pallas as pl
from jax.experimental.pallas import tpu as pltpu
from jax.sharding import PartitionSpec as P

SPAN = 4
GROUP = 4
AXES = ("blk", "inner")
F32 = jnp.float32
BF16 = jnp.bfloat16
VMEM_LIMIT = 16 * 1024 * 1024

HIDES = 10**10

X_SWAP = {0: (1, 0), 1: (0, 0), 2: (3, 0), 3: (2, 0)}
CORE_SWAP = {0: (2, 0), 1: (3, 0), 2: (0, 0), 3: (1, 0)}
GROUP_SHIFT = {0: (2, -1), 1: (3, -1), 2: (0, 1), 3: (1, 1)}


def send(value, moves):
    count = lax.axis_size(AXES)
    groups = count // GROUP
    pairs = [
        (g * GROUP + role, (g + step) % groups * GROUP + to)
        for g in range(groups)
        for role, (to, step) in moves.items()
    ]
    return lax.ppermute(value, AXES, pairs)


def unit_rows(raw):
    values = raw.astype(F32)
    inverse = 1.0 / jnp.sqrt(jnp.sum(values * values, axis=1, keepdims=True) + 1e-06)
    return values * inverse, inverse


def sigmoid_of(p):
    whole = 1.0 + p
    guess = pl.reciprocal(whole, approx=True)
    guess = guess * (2.0 - whole * guess)
    return p * (guess * (2.0 - whole * guess))


def log1p_of(p):
    below = p * (1.0 - p * (0.5 - p * (1.0 / 3.0)))
    return jnp.where(p < 0.015625, below, jnp.log(1.0 + p))


def softplus_lanes(p):
    if p.shape[1] % 128:
        p = jnp.pad(p, ((0, 0), (0, -p.shape[1] % 128)))
    total = None
    parts = [p[:, start : start + 128] for start in range(0, p.shape[1], 128)]
    for first in range(0, len(parts), 3):
        joint = parts[first]
        for part in parts[first + 1 : first + 3]:
            joint = joint + part + joint * part
        value = log1p_of(joint)
        total = value if total is None else total + value
    return total


def dot_nt(a, b):
    return lax.dot_general(a, b, (((1,), (1,)), ((), ())), preferred_element_type=F32)


def dot_nn(a, b):
    return lax.dot_general(a, b, (((1,), (0,)), ((), ())), preferred_element_type=F32)


def dot_tn(a, b):
    return lax.dot_general(a, b, (((0,), (0,)), ((), ())), preferred_element_type=F32)


def pair_step(own, blocks, scale, shift, work):
    end = 0
    for raw in blocks:
        start, end = end, end + raw.shape[0]
        work[start:end] = unit_rows(raw)[0].astype(BF16)
    return terms(own, work[:end], scale, shift)


def terms(own, others, scale, shift):
    p = jnp.exp(scale * dot_nt(own, others) + shift)
    coef = (sigmoid_of(p) * scale).astype(BF16)
    return dot_nn(coef, others), softplus_lanes(p)


def project(unit, inverse, grad):
    return ((grad - unit * jnp.sum(unit * grad, axis=1, keepdims=True)) * inverse).astype(BF16)


def row_parts(rows):
    count = 3 if rows % 48 == 0 else 1
    return [pl.ds(place * (rows // count), rows // count) for place in range(count)]


def chunk_rows(rows, sixths):
    first = sixths * rows // 6 // 16 * 16
    return first, rows - first


def scalar_pair(scalars):
    return scalars[0:1, 0:1], scalars[1:2, 0:1]


def image_is_u():
    return lax.rem(lax.axis_index("blk"), 2) == 0


def is_outer():
    return lax.rem(lax.axis_index("blk"), 2) == lax.axis_index("inner")


def sort_kernel(image, text, u, w, sems):
    def move(image_to, text_to):
        copies = []
        for source, target in ((image, image_to), (text, text_to)):
            for part in row_parts(image.shape[0]):
                sem = sems.at[len(copies)]
                copies.append(pltpu.make_async_copy(source.at[part], target.at[part], sem))
        for copy in copies:
            copy.start()
        for copy in copies:
            copy.wait()

    u_is_image = image_is_u()

    @pl.when(u_is_image)
    def _():
        move(u, w)

    @pl.when(jnp.logical_not(u_is_image))
    def _():
        move(w, u)


def pick_kernel(when_outer, when_inner, first, second, sems):
    def move(source):
        split = first.shape[0]
        copies = [
            pltpu.make_async_copy(source.at[pl.ds(0, split)], first, sems.at[0]),
            pltpu.make_async_copy(source.at[pl.ds(split, second.shape[0])], second, sems.at[1]),
        ]
        for copy in copies:
            copy.start()
        for copy in copies:
            copy.wait()

    @pl.when(is_outer())
    def _():
        move(when_outer)

    @pl.when(jnp.logical_not(is_outer()))
    def _():
        move(when_inner)


def near_kernel(
    scalars, image, text, b1, b2, b3_first, b3_second,
    z_pair, unit_u, unit_w, inverse_u, inverse_w, grad_u, grad_w, loss, work, z_w,
):
    u_is_image = image_is_u()
    u_weight = u_is_image.astype(F32)
    scale, shift = scalar_pair(scalars)
    image_unit, image_inverse = unit_rows(image[...])
    text_unit, text_inverse = unit_rows(text[...])
    unit_u[...] = jnp.where(u_is_image, image_unit, text_unit)
    unit_w[...] = jnp.where(u_is_image, text_unit, image_unit)
    inverse_u[...] = jnp.where(u_is_image, image_inverse, text_inverse)
    inverse_w[...] = jnp.where(u_is_image, text_inverse, image_inverse)
    zi = image_unit.astype(BF16)
    zt = text_unit.astype(BF16)
    z_u = jnp.where(u_is_image, zi, zt)
    z_pair[: zi.shape[0]] = z_u
    z_w[...] = jnp.where(u_is_image, zt, zi)
    scores = scale * dot_nt(zi, zt) + shift
    rows = lax.broadcasted_iota(jnp.int32, scores.shape, 0)
    columns = lax.broadcasted_iota(jnp.int32, scores.shape, 1)
    sign = jnp.where(rows == columns, F32(-1.0), F32(1.0))
    p = jnp.exp(sign * scores)
    coef = (sign * sigmoid_of(p) * scale).astype(BF16)
    total = softplus_lanes(p)
    grad_image = dot_nn(coef, zt)
    grad_text = dot_tn(coef, zi)
    grad_u[...] = jnp.where(u_is_image, grad_image, grad_text)
    grad_w[...] = jnp.where(u_is_image, grad_text, grad_image)
    term, row_loss = pair_step(z_u, (b2[...],), scale, shift, work)
    grad_u[...] += term
    total = total + u_weight * row_loss
    term, row_loss = pair_step(z_w[...], (b1[...], b3_first[...], b3_second[...]), scale, shift, work)
    z_pair[zi.shape[0] :] = work[: zi.shape[0]]
    grad_w[...] += term
    loss[...] = total + (1.0 - u_weight) * row_loss


def fifth_first_kernel(scalars, b5, z_pair, grad_in, loss_in, grad_u, loss, for_partner, work):
    rows, width = grad_u.shape
    term, row_loss = pair_step(z_pair[...], (b5[...],), *scalar_pair(scalars), work)
    for_partner[:, :width] = term[rows:]
    for_partner[:, width:] = row_loss[rows:]
    grad_u[...] = grad_in[...] + term[:rows]
    loss[...] = loss_in[...] + image_is_u().astype(F32) * row_loss[:rows]


def fourth_first_kernel(scalars, b4, z_pair, grad_in, loss_in, grad_u, loss, work):
    rows = grad_u.shape[0]
    term, row_loss = pair_step(z_pair[:rows], (b4[...],), *scalar_pair(scalars), work)
    grad_u[...] = grad_in[...] + term
    loss[...] = loss_in[...] + image_is_u().astype(F32) * row_loss


def fifth_second_kernel(
    scalars, b5, z_pair, grad_in, loss_in, partner_in, grad_u, loss, for_partner, work
):
    rows, width = grad_u.shape
    term, row_loss = pair_step(z_pair[...], (b5[...],), *scalar_pair(scalars), work)
    for_partner[:, :width] = (partner_in[:, :width] + term[rows:]).astype(BF16)
    for_partner[:, width:] = (partner_in[:, width:] + row_loss[rows:]).astype(BF16)
    grad_u[...] = grad_in[...] + term[:rows]
    loss[...] = loss_in[...] + image_is_u().astype(F32) * row_loss[:rows]


def u_kernel(scalars, b4, z_pair, grad_u, loss_in, unit, inverse, done_u, loss, work):
    rows = done_u.shape[0]
    term, row_loss = pair_step(z_pair[:rows], (b4[...],), *scalar_pair(scalars), work)
    loss[...] = loss_in[...] + image_is_u().astype(F32) * row_loss
    done_u[...] = project(unit[...], inverse[...], grad_u[...] + term)


def w_kernel(
    last, grad_w, loss_in, unit, inverse, done_u, image_grad, text_grad, loss_rows, done_w, sems
):
    u_is_image = image_is_u()
    parts = row_parts(done_w.shape[0])

    def output(action, source, part, to_image, sem):
        @pl.when(to_image)
        def _():
            action(pltpu.make_async_copy(source.at[part], image_grad.at[part], sem))

        @pl.when(jnp.logical_not(to_image))
        def _():
            action(pltpu.make_async_copy(source.at[part], text_grad.at[part], sem))

    whole = pl.ds(0, done_w.shape[0])
    output(lambda copy: copy.start(), done_u, whole, u_is_image, sems.at[0])
    width = done_w.shape[1]
    for place, part in enumerate(parts):
        grad = grad_w[part] + last[part, :width].astype(F32)
        done_w[part] = project(unit[part], inverse[part], grad)
        output(lambda copy: copy.start(), done_w, part, jnp.logical_not(u_is_image), sems.at[1 + place])
    total = loss_in[...] + (1.0 - u_is_image.astype(F32)) * last[:, width:].astype(F32)
    loss_rows[...] = jnp.sum(jnp.transpose(total), axis=0) / (SPAN * total.shape[0])
    output(lambda copy: copy.wait(), done_u, whole, u_is_image, sems.at[0])
    for place, part in enumerate(parts):
        output(lambda copy: copy.wait(), done_w, part, jnp.logical_not(u_is_image), sems.at[1 + place])


VMEM = pl.BlockSpec(memory_space=pltpu.VMEM)
ANY = pl.BlockSpec(memory_space=pl.ANY)


def call(kernel, in_specs, args, out_specs, outs, name, scratch=(), flops=1):
    return pl.pallas_call(
        kernel,
        out_shape=outs,
        in_specs=in_specs,
        out_specs=out_specs,
        scratch_shapes=list(scratch),
        name=name,
        cost_estimate=pl.CostEstimate(flops=flops, bytes_accessed=1, transcendentals=0),
        compiler_params=pltpu.CompilerParams(vmem_limit_bytes=VMEM_LIMIT),
    )(*args)


def local(image, text, score_scaling, score_shift):
    rows, width = image.shape
    block = jax.ShapeDtypeStruct((rows, width), BF16)
    pair = jax.ShapeDtypeStruct((2 * rows, width), BF16)
    sums = jax.ShapeDtypeStruct((rows, width), F32)
    column = jax.ShapeDtypeStruct((rows, 1), F32)
    partial = jax.ShapeDtypeStruct((rows, 128), F32)
    line = jax.ShapeDtypeStruct((rows,), F32)
    raw = pltpu.VMEM((rows, width), BF16)
    copies = pltpu.SemaphoreType.DMA((6,))

    def in_hbm(*arrays):
        return [pltpu.with_memory_space_constraint(x, pltpu.HBM) for x in arrays]


    def pick(when_outer, when_inner, space, sixths):
        outs = [space((size, width), BF16) for size in chunk_rows(rows, sixths)]
        return call(
            pick_kernel, [ANY] * 2, (when_outer, when_inner), [ANY] * 2, outs, "pick", (copies,)
        )

    def in_vmem(*arrays):
        return [pltpu.with_memory_space_constraint(x, pltpu.VMEM) for x in arrays]

    def compute(kernel, args, outs, name, scratch, flops=1):
        in_specs = [VMEM] * (1 + len(args))
        out_specs = [VMEM] * len(outs)
        return call(kernel, in_specs, (scalars, *args), out_specs, outs, name, scratch, flops)

    u, w = call(
        sort_kernel,
        [ANY] * 2,
        in_hbm(image, text),
        [VMEM] * 2,
        (block, block),
        "sort",
        (copies,),
    )
    slot1 = send(w, CORE_SWAP)
    slot2 = send(u, GROUP_SHIFT)
    slot3 = [send(chunk, X_SWAP) for chunk in pick(slot1, u, jax.ShapeDtypeStruct, 3)]
    slot4 = in_vmem(*[send(chunk, GROUP_SHIFT) for chunk in slot3])
    slot5 = in_vmem(*[send(chunk, X_SWAP) for chunk in pick(w, slot2, pltpu.HBM, 4)])
    first = lax.broadcasted_iota(jnp.int32, (8, 128), 0) == 0
    scalars = jnp.where(first, score_scaling, score_shift)
    z_pair, unit_u, unit_w, inverse_u, inverse_w, grad_u, grad_w, loss = compute(
        near_kernel,
        (*in_hbm(image, text), slot1, *in_hbm(slot2, *slot3)),
        (pair, sums, sums, column, column, sums, sums, partial),
        "near_blocks",
        (pltpu.VMEM((2 * rows, width), BF16), raw),
        HIDES // 5,
    )
    both = width + 128
    grad_u, loss, for_partner = compute(
        fifth_first_kernel,
        (slot5[0], z_pair, grad_u, loss),
        (sums, partial, jax.ShapeDtypeStruct((rows, both), F32)),
        "fifth_first",
        (raw,),
    )
    grad_u, loss = compute(
        fourth_first_kernel, (slot4[0], z_pair, grad_u, loss), (sums, partial), "fourth_first", (raw,)
    )
    grad_u, loss, for_partner = compute(
        fifth_second_kernel,
        (slot5[1], z_pair, grad_u, loss, for_partner),
        (sums, partial, jax.ShapeDtypeStruct((rows, both), BF16)),
        "fifth_second",
        (raw,),
    )
    last = send(for_partner, CORE_SWAP)
    done_u, loss = compute(
        u_kernel,
        (slot4[1], z_pair, grad_u, loss, unit_u, inverse_u),
        (block, partial),
        "finish_u",
        (raw,),
        HIDES,
    )
    image_grad, text_grad, loss_rows = call(
        w_kernel,
        [VMEM] * 6,
        (last, grad_w, loss, unit_w, inverse_w, done_u),
        [ANY, ANY, VMEM],
        (block, block, line),
        "finish_w",
        (raw, copies),
    )
    return loss_rows, image_grad, text_grad


def solution(mesh):
    in_specs = (P(AXES, None), P(AXES, None), P(), P())
    out_specs = (P(AXES), P(AXES, None), P(AXES, None))
    return jax.shard_map(local, mesh=mesh, in_specs=in_specs, out_specs=out_specs, check_vma=False)
```

```python
import functools

import jax
import jax.numpy as jnp
from jax import lax
from jax.experimental import pallas as pl
from jax.experimental.pallas import tpu as pltpu
from jax.sharding import PartitionSpec as P

SPAN = 4
GROUP = 4
AXES = ("blk", "inner")
F32 = jnp.float32
BF16 = jnp.bfloat16
VMEM_LIMIT = 16 * 1024 * 1024

X_SWAP = {0: (1, 0), 1: (0, 0), 2: (3, 0), 3: (2, 0)}
CORE_SWAP = {0: (2, 0), 1: (3, 0), 2: (0, 0), 3: (1, 0)}
GROUP_SHIFT = {0: (2, -1), 1: (3, -1), 2: (0, 1), 3: (1, 1)}


def send(value, moves):
    count = lax.axis_size(AXES)
    groups = count // GROUP
    pairs = [
        (g * GROUP + role, (g + step) % groups * GROUP + to)
        for g in range(groups)
        for role, (to, step) in moves.items()
    ]
    return lax.ppermute(value, AXES, pairs)


def unit_rows(raw):
    values = raw.astype(F32)
    inverse = 1.0 / jnp.sqrt(jnp.sum(values * values, axis=1, keepdims=True) + 1e-06)
    return values * inverse, inverse


def sigmoid_of(p):
    whole = 1.0 + p
    guess = pl.reciprocal(whole, approx=True)
    guess = guess * (2.0 - whole * guess)
    return p * (guess * (2.0 - whole * guess))


def log1p_of(p):
    below = p * (1.0 - p * (0.5 - p * (1.0 / 3.0)))
    return jnp.where(p < 0.015625, below, jnp.log(1.0 + p))


def softplus_lanes(p):
    total = None
    parts = [p[:, start : start + 128] for start in range(0, p.shape[1], 128)]
    for first in range(0, len(parts), 3):
        joint = parts[first]
        for part in parts[first + 1 : first + 3]:
            joint = joint + part + joint * part
        value = log1p_of(joint)
        total = value if total is None else total + value
    return total


def dot_nt(a, b):
    return lax.dot_general(a, b, (((1,), (1,)), ((), ())), preferred_element_type=F32)


def dot_nn(a, b):
    return lax.dot_general(a, b, (((1,), (0,)), ((), ())), preferred_element_type=F32)


def dot_tn(a, b):
    return lax.dot_general(a, b, (((0,), (0,)), ((), ())), preferred_element_type=F32)


def pair_step(own, blocks, scale, shift, work):
    rows = blocks[0].shape[0]
    for place, raw in enumerate(blocks):
        work[place * rows : (place + 1) * rows] = unit_rows(raw)[0].astype(BF16)
    return terms(own, work[: len(blocks) * rows], scale, shift)


def terms(own, others, scale, shift):
    half = own.shape[0] // 2
    scores = [dot_nt(own[:half], others), dot_nt(own[half:], others)]
    products, losses = [], []
    for score in scores:
        p = jnp.exp(scale * score + shift)
        coef = (sigmoid_of(p) * scale).astype(BF16)
        products.append(dot_nn(coef, others))
        losses.append(softplus_lanes(p))
    return jnp.concatenate(products), jnp.concatenate(losses)


def project(unit, inverse, grad):
    return ((grad - unit * jnp.sum(unit * grad, axis=1, keepdims=True)) * inverse).astype(BF16)


def row_parts(rows, wanted):
    count = wanted if rows % (16 * wanted) == 0 else 1
    return [pl.ds(place * (rows // count), rows // count) for place in range(count)]


def scalar_pair(scalars):
    return scalars[0:1, 0:1], scalars[1:2, 0:1]


def image_is_u():
    return lax.rem(lax.axis_index("blk"), 2) == 0


def is_outer():
    return lax.rem(lax.axis_index("blk"), 2) == lax.axis_index("inner")


def own_kernel(image_core, image, text, block, sems):
    def move(source):
        copies = []
        for place, part in enumerate(row_parts(block.shape[0], 3)):
            copies.append(pltpu.make_async_copy(source.at[part], block.at[part], sems.at[place]))
        for copy in copies:
            copy.start()
        for copy in copies:
            copy.wait()

    wants_image = lax.rem(lax.axis_index("blk"), 2) == image_core

    @pl.when(wants_image)
    def _():
        move(image)

    @pl.when(jnp.logical_not(wants_image))
    def _():
        move(text)


def pick_kernel(when_outer, when_inner, picked, sem):
    @pl.when(is_outer())
    def _():
        pltpu.async_copy(when_outer, picked, sem).wait()

    @pl.when(jnp.logical_not(is_outer()))
    def _():
        pltpu.async_copy(when_inner, picked, sem).wait()


def near_kernel(
    scalars, image, text, b1, b2, b3,
    z_pair, unit_u, unit_w, inverse_u, inverse_w, grad_u, grad_w, loss, work, z_w,
):
    u_is_image = image_is_u()
    u_weight = u_is_image.astype(F32)
    scale, shift = scalar_pair(scalars)
    image_unit, image_inverse = unit_rows(image[...])
    text_unit, text_inverse = unit_rows(text[...])
    unit_u[...] = jnp.where(u_is_image, image_unit, text_unit)
    unit_w[...] = jnp.where(u_is_image, text_unit, image_unit)
    inverse_u[...] = jnp.where(u_is_image, image_inverse, text_inverse)
    inverse_w[...] = jnp.where(u_is_image, text_inverse, image_inverse)
    zi = image_unit.astype(BF16)
    zt = text_unit.astype(BF16)
    z_u = jnp.where(u_is_image, zi, zt)
    z_pair[: zi.shape[0]] = z_u
    z_w[...] = jnp.where(u_is_image, zt, zi)
    scores = scale * dot_nt(zi, zt) + shift
    rows = lax.broadcasted_iota(jnp.int32, scores.shape, 0)
    columns = lax.broadcasted_iota(jnp.int32, scores.shape, 1)
    sign = jnp.where(rows == columns, F32(-1.0), F32(1.0))
    p = jnp.exp(sign * scores)
    coef = (sign * sigmoid_of(p) * scale).astype(BF16)
    total = softplus_lanes(p)
    grad_image = dot_nn(coef, zt)
    grad_text = dot_tn(coef, zi)
    grad_u[...] = jnp.where(u_is_image, grad_image, grad_text)
    grad_w[...] = jnp.where(u_is_image, grad_text, grad_image)
    term, row_loss = pair_step(z_u, (b2[...],), scale, shift, work)
    grad_u[...] += term
    total = total + u_weight * row_loss
    term, row_loss = pair_step(z_w[...], (b1[...], b3[...]), scale, shift, work)
    z_pair[zi.shape[0] :] = work[: zi.shape[0]]
    grad_w[...] += term
    loss[...] = total + (1.0 - u_weight) * row_loss


def fifth_kernel(scalars, b5, z_pair, grad_in, loss_in, grad_u, loss, for_partner, work):
    rows, width = b5.shape
    term, row_loss = pair_step(z_pair[...], (b5[...],), *scalar_pair(scalars), work)
    for_partner[:, :width] = term[rows:].astype(BF16)
    for_partner[:, width:] = row_loss[rows:].astype(BF16)
    grad_u[...] = grad_in[...] + term[:rows]
    loss[...] = loss_in[...] + image_is_u().astype(F32) * row_loss[:rows]


def u_kernel(scalars, b4, z_pair, grad_u, loss_in, unit, inverse, done_u, loss, work):
    rows = done_u.shape[0]
    term, row_loss = pair_step(z_pair[:rows], (b4[...],), *scalar_pair(scalars), work)
    loss[...] = loss_in[...] + image_is_u().astype(F32) * row_loss
    done_u[...] = project(unit[...], inverse[...], grad_u[...] + term)


def w_kernel(
    last, grad_w, loss_in, unit, inverse, done_u, image_grad, text_grad, loss_rows, done_w, sems
):
    u_is_image = image_is_u()
    parts = row_parts(done_w.shape[0], 6)

    def output(action, source, part, to_image, sem):
        @pl.when(to_image)
        def _():
            action(pltpu.make_async_copy(source.at[part], image_grad.at[part], sem))

        @pl.when(jnp.logical_not(to_image))
        def _():
            action(pltpu.make_async_copy(source.at[part], text_grad.at[part], sem))

    whole = pl.ds(0, done_w.shape[0])
    output(lambda copy: copy.start(), done_u, whole, u_is_image, sems.at[0])
    width = done_w.shape[1]
    for place, part in enumerate(parts):
        grad = grad_w[part] + last[part, :width].astype(F32)
        done_w[part] = project(unit[part], inverse[part], grad)
        output(lambda copy: copy.start(), done_w, part, jnp.logical_not(u_is_image), sems.at[1 + place])
    total = loss_in[...] + (1.0 - u_is_image.astype(F32)) * last[:, width:].astype(F32)
    loss_rows[...] = jnp.sum(jnp.transpose(total), axis=0) / (SPAN * total.shape[0])
    output(lambda copy: copy.wait(), done_u, whole, u_is_image, sems.at[0])
    for place, part in enumerate(parts):
        output(lambda copy: copy.wait(), done_w, part, jnp.logical_not(u_is_image), sems.at[1 + place])


VMEM = pl.BlockSpec(memory_space=pltpu.VMEM)
ANY = pl.BlockSpec(memory_space=pl.ANY)


def call(kernel, in_specs, args, out_specs, outs, name, scratch=(), flops=1):
    return pl.pallas_call(
        kernel,
        out_shape=outs,
        in_specs=in_specs,
        out_specs=out_specs,
        scratch_shapes=list(scratch),
        name=name,
        cost_estimate=pl.CostEstimate(flops=flops, bytes_accessed=1, transcendentals=0),
        compiler_params=pltpu.CompilerParams(vmem_limit_bytes=VMEM_LIMIT),
    )(*args)


def local(image, text, score_scaling, score_shift):
    rows, width = image.shape
    block = jax.ShapeDtypeStruct((rows, width), BF16)
    pair = jax.ShapeDtypeStruct((2 * rows, width), BF16)
    sums = jax.ShapeDtypeStruct((rows, width), F32)
    column = jax.ShapeDtypeStruct((rows, 1), F32)
    partial = jax.ShapeDtypeStruct((rows, 128), F32)
    line = jax.ShapeDtypeStruct((rows,), F32)
    raw = pltpu.VMEM((rows, width), BF16)
    copies = pltpu.SemaphoreType.DMA((7,))

    def in_hbm(*arrays):
        return [pltpu.with_memory_space_constraint(x, pltpu.HBM) for x in arrays]


    def pick(when_outer, when_inner, out):
        sem = pltpu.SemaphoreType.DMA
        return call(
            pick_kernel, [ANY] * 2, (when_outer, when_inner), [ANY], (out,), "pick", (sem,)
        )[0]

    def compute(kernel, args, outs, name, scratch, flops=1):
        in_specs = [VMEM] * (1 + len(args))
        out_specs = [VMEM] * len(outs)
        return call(kernel, in_specs, (scalars, *args), out_specs, outs, name, scratch, flops)

    def own(image_core):
        kernel = functools.partial(own_kernel, image_core)
        return call(kernel, [ANY] * 2, in_hbm(image, text), [VMEM], (block,), "own", (copies,))[0]

    w = own(1)
    slot1 = send(w, CORE_SWAP)
    u = own(0)
    slot2 = send(u, GROUP_SHIFT)
    slot3 = send(pick(slot1, u, block), X_SWAP)
    slot4 = send(slot3, GROUP_SHIFT)
    slot5 = send(pick(w, slot2, pltpu.HBM((rows, width), BF16)), X_SWAP)
    slot3, score_scaling, score_shift = lax.optimization_barrier((slot3, score_scaling, score_shift))
    first = lax.broadcasted_iota(jnp.int32, (8, 128), 0) == 0
    scalars = jnp.where(first, score_scaling, score_shift)
    z_pair, unit_u, unit_w, inverse_u, inverse_w, grad_u, grad_w, loss = compute(
        near_kernel,
        (*in_hbm(image, text), slot1, *in_hbm(slot2, slot3)),
        (pair, sums, sums, column, column, sums, sums, partial),
        "near_blocks",
        (pltpu.VMEM((2 * rows, width), BF16), raw),
    )
    grad_u, loss, for_partner = compute(
        fifth_kernel,
        (pltpu.with_memory_space_constraint(slot5, pltpu.VMEM), z_pair, grad_u, loss),
        (sums, partial, jax.ShapeDtypeStruct((rows, width + 128), BF16)),
        "fifth_block",
        (raw,),
    )
    last = send(for_partner, CORE_SWAP)
    done_u, loss = compute(
        u_kernel,
        (pltpu.with_memory_space_constraint(slot4, pltpu.VMEM), z_pair, grad_u, loss, unit_u, inverse_u),
        (block, partial),
        "finish_u",
        (raw,),
        10**10,
    )
    image_grad, text_grad, loss_rows = call(
        w_kernel,
        [VMEM] * 6,
        (last, grad_w, loss, unit_w, inverse_w, done_u),
        [ANY, ANY, VMEM],
        (block, block, line),
        "finish_w",
        (raw, copies),
    )
    return loss_rows, image_grad, text_grad


def solution(mesh):
    in_specs = (P(AXES, None), P(AXES, None), P(), P())
    out_specs = (P(AXES), P(AXES, None), P(AXES, None))
    return jax.shard_map(local, mesh=mesh, in_specs=in_specs, out_specs=out_specs, check_vma=False)
```

```python
import jax
import jax.numpy as jnp
from jax import lax
from jax.experimental import pallas as pl
from jax.experimental.pallas import tpu as pltpu
from jax.sharding import PartitionSpec as P

SPAN = 4
GROUP = 4
AXES = ("blk", "inner")
F32 = jnp.float32
BF16 = jnp.bfloat16
VMEM_LIMIT = 28 * 1024 * 1024

X_SWAP = {0: (1, 0), 1: (0, 0), 2: (3, 0), 3: (2, 0)}
CORE_SWAP = {0: (2, 0), 1: (3, 0), 2: (0, 0), 3: (1, 0)}
GROUP_SHIFT = {0: (2, -1), 1: (3, -1), 2: (0, 1), 3: (1, 1)}


def send(value, moves):
    count = lax.axis_size(AXES)
    groups = count // GROUP
    pairs = [
        (g * GROUP + role, (g + step) % groups * GROUP + to)
        for g in range(groups)
        for role, (to, step) in moves.items()
    ]
    return lax.ppermute(value, AXES, pairs)


def unit_rows(raw):
    values = raw.astype(F32)
    inverse = 1.0 / jnp.sqrt(jnp.sum(values * values, axis=1, keepdims=True) + 1e-06)
    return values * inverse, inverse


def sigmoid_of(p):
    whole = 1.0 + p
    guess = pl.reciprocal(whole, approx=True)
    guess = guess * (2.0 - whole * guess)
    return p * (guess * (2.0 - whole * guess))


def log1p_of(p):
    below = p * (1.0 - p * (0.5 - p * (1.0 / 3.0)))
    return jnp.where(p < 0.015625, below, jnp.log(1.0 + p))


def softplus_lanes(p):
    total = None
    parts = [p[:, start : start + 128] for start in range(0, p.shape[1], 128)]
    for first in range(0, len(parts), 3):
        joint = parts[first]
        for part in parts[first + 1 : first + 3]:
            joint = joint + part + joint * part
        value = log1p_of(joint)
        total = value if total is None else total + value
    return total


def dot_nt(a, b):
    return lax.dot_general(a, b, (((1,), (1,)), ((), ())), preferred_element_type=F32)


def dot_nn(a, b):
    return lax.dot_general(a, b, (((1,), (0,)), ((), ())), preferred_element_type=F32)


def dot_tn(a, b):
    return lax.dot_general(a, b, (((0,), (0,)), ((), ())), preferred_element_type=F32)


def pair_step(own, blocks, scale, shift, work):
    rows = blocks[0].shape[0]
    for place, raw in enumerate(blocks):
        work[place * rows : (place + 1) * rows] = unit_rows(raw)[0].astype(BF16)
    return terms(own, work[: len(blocks) * rows], scale, shift)


def terms(own, others, scale, shift):
    half = own.shape[0] // 2
    scores = [dot_nt(own[:half], others), dot_nt(own[half:], others)]
    products, losses = [], []
    for score in scores:
        p = jnp.exp(scale * score + shift)
        coef = (sigmoid_of(p) * scale).astype(BF16)
        products.append(dot_nn(coef, others))
        losses.append(softplus_lanes(p))
    return jnp.concatenate(products), jnp.concatenate(losses)


def project(unit, inverse, grad):
    return (grad - unit * jnp.sum(unit * grad, axis=1, keepdims=True)) * inverse


def row_parts(rows, wanted):
    count = wanted if rows % (16 * wanted) == 0 else 1
    return [pl.ds(place * (rows // count), rows // count) for place in range(count)]


def scalar_pair(scalars):
    return scalars[0:1, 0:1], scalars[1:2, 0:1]


def image_is_u():
    return lax.rem(lax.axis_index("blk"), 2) == 0


def is_outer():
    return lax.rem(lax.axis_index("blk"), 2) == lax.axis_index("inner")


def sort_kernel(image, text, u, w, sems):
    def move(image_to, text_to):
        copies = []
        for source, target in ((image, image_to), (text, text_to)):
            for part in row_parts(image.shape[0], 3):
                sem = sems.at[len(copies)]
                copies.append(pltpu.make_async_copy(source.at[part], target.at[part], sem))
        for copy in copies:
            copy.start()
        for copy in copies:
            copy.wait()

    u_is_image = image_is_u()

    @pl.when(u_is_image)
    def _():
        move(u, w)

    @pl.when(jnp.logical_not(u_is_image))
    def _():
        move(w, u)


def pick_kernel(when_outer, when_inner, picked, sem):
    @pl.when(is_outer())
    def _():
        pltpu.async_copy(when_outer, picked, sem).wait()

    @pl.when(jnp.logical_not(is_outer()))
    def _():
        pltpu.async_copy(when_inner, picked, sem).wait()


def near_kernel(
    scalars, image, text, b1, b2, b3,
    z_pair, unit_u, unit_other, inverse_u, inverse_other, grad_u, part_w, loss, work, z_w, grad_w, unit_w,
):
    u_is_image = image_is_u()
    u_weight = u_is_image.astype(F32)
    scale, shift = scalar_pair(scalars)
    image_unit, image_inverse = unit_rows(image[...])
    text_unit, text_inverse = unit_rows(text[...])
    unit_u[...] = jnp.where(u_is_image, image_unit, text_unit)
    unit_w[...] = jnp.where(u_is_image, text_unit, image_unit)
    inverse_u[...] = jnp.where(u_is_image, image_inverse, text_inverse)
    inverse_w = jnp.where(u_is_image, text_inverse, image_inverse)
    unit_other[...], inverse_other[...] = unit_rows(b1[...])
    zi = image_unit.astype(BF16)
    zt = text_unit.astype(BF16)
    z_u = jnp.where(u_is_image, zi, zt)
    z_pair[: zi.shape[0]] = z_u
    z_w[...] = jnp.where(u_is_image, zt, zi)
    scores = scale * dot_nt(zi, zt) + shift
    rows = lax.broadcasted_iota(jnp.int32, scores.shape, 0)
    columns = lax.broadcasted_iota(jnp.int32, scores.shape, 1)
    sign = jnp.where(rows == columns, F32(-1.0), F32(1.0))
    p = jnp.exp(sign * scores)
    coef = (sign * sigmoid_of(p) * scale).astype(BF16)
    total = softplus_lanes(p)
    grad_image = dot_nn(coef, zt)
    grad_text = dot_tn(coef, zi)
    grad_u[...] = jnp.where(u_is_image, grad_image, grad_text)
    grad_w[...] = jnp.where(u_is_image, grad_text, grad_image)
    term, row_loss = pair_step(z_u, (b2[...],), scale, shift, work)
    grad_u[...] += term
    total = total + u_weight * row_loss
    term, row_loss = pair_step(z_w[...], (b1[...], b3[...]), scale, shift, work)
    z_pair[zi.shape[0] :] = work[: zi.shape[0]]
    part_w[...] = project(unit_w[...], inverse_w, grad_w[...] + term)
    loss[...] = total + (1.0 - u_weight) * row_loss


def fifth_kernel(
    scalars, b5, z_pair, unit_other, inverse_other, grad_in, loss_in, grad_u, loss, for_partner, work
):
    rows, width = b5.shape
    term, row_loss = pair_step(z_pair[...], (b5[...],), *scalar_pair(scalars), work)
    for_partner[:, :width] = project(unit_other[...], inverse_other[...], term[rows:]).astype(BF16)
    for_partner[:, width:] = row_loss[rows:].astype(BF16)
    grad_u[...] = grad_in[...] + term[:rows]
    loss[...] = loss_in[...] + image_is_u().astype(F32) * row_loss[:rows]


def u_kernel(scalars, b4, z_pair, grad_u, loss_in, unit, inverse, done_u, loss, work):
    rows = done_u.shape[0]
    term, row_loss = pair_step(z_pair[:rows], (b4[...],), *scalar_pair(scalars), work)
    loss[...] = loss_in[...] + image_is_u().astype(F32) * row_loss
    done_u[...] = project(unit[...], inverse[...], grad_u[...] + term).astype(BF16)


def w_kernel(
    last, part_w, loss_in, done_u, image_grad, text_grad, loss_rows, done_w, sems
):
    u_is_image = image_is_u()
    parts = row_parts(done_w.shape[0], 6)

    def output(action, source, part, to_image, sem):
        @pl.when(to_image)
        def _():
            action(pltpu.make_async_copy(source.at[part], image_grad.at[part], sem))

        @pl.when(jnp.logical_not(to_image))
        def _():
            action(pltpu.make_async_copy(source.at[part], text_grad.at[part], sem))

    whole = pl.ds(0, done_w.shape[0])
    output(lambda copy: copy.start(), done_u, whole, u_is_image, sems.at[0])
    width = done_w.shape[1]
    for place, part in enumerate(parts):
        done_w[part] = (part_w[part] + last[part, :width].astype(F32)).astype(BF16)
        output(lambda copy: copy.start(), done_w, part, jnp.logical_not(u_is_image), sems.at[1 + place])
    total = loss_in[...] + (1.0 - u_is_image.astype(F32)) * last[:, width:].astype(F32)
    loss_rows[...] = jnp.sum(jnp.transpose(total), axis=0) / (SPAN * total.shape[0])
    output(lambda copy: copy.wait(), done_u, whole, u_is_image, sems.at[0])
    for place, part in enumerate(parts):
        output(lambda copy: copy.wait(), done_w, part, jnp.logical_not(u_is_image), sems.at[1 + place])


VMEM = pl.BlockSpec(memory_space=pltpu.VMEM)
ANY = pl.BlockSpec(memory_space=pl.ANY)


def call(kernel, in_specs, args, out_specs, outs, name, scratch=(), flops=1):
    return pl.pallas_call(
        kernel,
        out_shape=outs,
        in_specs=in_specs,
        out_specs=out_specs,
        scratch_shapes=list(scratch),
        name=name,
        cost_estimate=pl.CostEstimate(flops=flops, bytes_accessed=1, transcendentals=0),
        compiler_params=pltpu.CompilerParams(vmem_limit_bytes=VMEM_LIMIT),
    )(*args)


def local(image, text, score_scaling, score_shift):
    rows, width = image.shape
    block = jax.ShapeDtypeStruct((rows, width), BF16)
    pair = jax.ShapeDtypeStruct((2 * rows, width), BF16)
    sums = jax.ShapeDtypeStruct((rows, width), F32)
    column = jax.ShapeDtypeStruct((rows, 1), F32)
    partial = jax.ShapeDtypeStruct((rows, 128), F32)
    line = jax.ShapeDtypeStruct((rows,), F32)
    raw = pltpu.VMEM((rows, width), BF16)
    copies = pltpu.SemaphoreType.DMA((7,))

    def in_hbm(*arrays):
        return [pltpu.with_memory_space_constraint(x, pltpu.HBM) for x in arrays]


    def pick(when_outer, when_inner, out):
        sem = pltpu.SemaphoreType.DMA
        return call(
            pick_kernel, [ANY] * 2, (when_outer, when_inner), [ANY], (out,), "pick", (sem,)
        )[0]

    def compute(kernel, args, outs, name, scratch, flops=1):
        in_specs = [VMEM] * (1 + len(args))
        out_specs = [VMEM] * len(outs)
        return call(kernel, in_specs, (scalars, *args), out_specs, outs, name, scratch, flops)

    u, w = call(
        sort_kernel, [ANY] * 2, in_hbm(image, text), [VMEM] * 2, (block, block), "sort", (copies,)
    )
    slot1 = send(w, CORE_SWAP)
    slot2 = send(u, GROUP_SHIFT)
    slot3 = send(pick(slot1, u, block), X_SWAP)
    slot4 = send(slot3, GROUP_SHIFT)
    slot5 = send(pick(w, slot2, pltpu.HBM((rows, width), BF16)), X_SWAP)
    slot3, score_scaling, score_shift = lax.optimization_barrier((slot3, score_scaling, score_shift))
    first = lax.broadcasted_iota(jnp.int32, (8, 128), 0) == 0
    scalars = jnp.where(first, score_scaling, score_shift)
    z_pair, unit_u, unit_other, inverse_u, inverse_other, grad_u, part_w, loss = compute(
        near_kernel,
        (*in_hbm(image, text), slot1, *in_hbm(slot2, slot3)),
        (pair, sums, sums, column, column, sums, sums, partial),
        "near_blocks",
        (pltpu.VMEM((2 * rows, width), BF16), raw) + (pltpu.VMEM((rows, width), F32),) * 2,
    )
    grad_u, loss, for_partner = compute(
        fifth_kernel,
        (pltpu.with_memory_space_constraint(slot5, pltpu.VMEM), z_pair, unit_other, inverse_other, grad_u, loss),
        (sums, partial, jax.ShapeDtypeStruct((rows, width + 128), BF16)),
        "fifth_block",
        (raw,),
    )
    last = send(for_partner, CORE_SWAP)
    done_u, loss = compute(
        u_kernel,
        (pltpu.with_memory_space_constraint(slot4, pltpu.VMEM), z_pair, grad_u, loss, unit_u, inverse_u),
        (block, partial),
        "finish_u",
        (raw,),
        10**10,
    )
    image_grad, text_grad, loss_rows = call(
        w_kernel,
        [VMEM] * 4,
        (last, part_w, loss, done_u),
        [ANY, ANY, VMEM],
        (block, block, line),
        "finish_w",
        (raw, copies),
    )
    return loss_rows, image_grad, text_grad


def solution(mesh):
    in_specs = (P(AXES, None), P(AXES, None), P(), P())
    out_specs = (P(AXES), P(AXES, None), P(AXES, None))
    return jax.shard_map(local, mesh=mesh, in_specs=in_specs, out_specs=out_specs, check_vma=False)
```

```python
import jax
import jax.numpy as jnp
from jax import lax
from jax.experimental import pallas as pl
from jax.experimental.pallas import tpu as pltpu
from jax.sharding import PartitionSpec as P

SPAN = 4
GROUP = 4
AXES = ("blk", "inner")
F32 = jnp.float32
BF16 = jnp.bfloat16
VMEM_LIMIT = 28 * 1024 * 1024

X_SWAP = {0: (1, 0), 1: (0, 0), 2: (3, 0), 3: (2, 0)}
CORE_SWAP = {0: (2, 0), 1: (3, 0), 2: (0, 0), 3: (1, 0)}
GROUP_SHIFT = {0: (2, -1), 1: (3, -1), 2: (0, 1), 3: (1, 1)}


def send(value, moves):
    count = lax.axis_size(AXES)
    groups = count // GROUP
    pairs = [
        (g * GROUP + role, (g + step) % groups * GROUP + to)
        for g in range(groups)
        for role, (to, step) in moves.items()
    ]
    return lax.ppermute(value, AXES, pairs)


def unit_rows(raw):
    values = raw.astype(F32)
    inverse = 1.0 / jnp.sqrt(jnp.sum(values * values, axis=1, keepdims=True) + 1e-06)
    return values * inverse, inverse


def sigmoid_of(p):
    whole = 1.0 + p
    guess = pl.reciprocal(whole, approx=True)
    guess = guess * (2.0 - whole * guess)
    return p * (guess * (2.0 - whole * guess))


def log1p_of(p):
    below = p * (1.0 - p * (0.5 - p * (1.0 / 3.0)))
    return jnp.where(p < 0.015625, below, jnp.log(1.0 + p))


def softplus_lanes(p):
    total = None
    parts = [p[:, start : start + 128] for start in range(0, p.shape[1], 128)]
    for first in range(0, len(parts), 3):
        joint = parts[first]
        for part in parts[first + 1 : first + 3]:
            joint = joint + part + joint * part
        value = log1p_of(joint)
        total = value if total is None else total + value
    return total


def dot_nt(a, b):
    return lax.dot_general(a, b, (((1,), (1,)), ((), ())), preferred_element_type=F32)


def dot_nn(a, b):
    return lax.dot_general(a, b, (((1,), (0,)), ((), ())), preferred_element_type=F32)


def dot_tn(a, b):
    return lax.dot_general(a, b, (((0,), (0,)), ((), ())), preferred_element_type=F32)


def pair_step(own, blocks, scale, shift, work):
    rows = blocks[0].shape[0]
    for place, raw in enumerate(blocks):
        work[place * rows : (place + 1) * rows] = unit_rows(raw)[0].astype(BF16)
    return terms(own, work[: len(blocks) * rows], scale, shift)


def terms(own, others, scale, shift):
    half = own.shape[0] // 2
    scores = [dot_nt(own[:half], others), dot_nt(own[half:], others)]
    products, losses = [], []
    for score in scores:
        p = jnp.exp(scale * score + shift)
        coef = (sigmoid_of(p) * scale).astype(BF16)
        products.append(dot_nn(coef, others))
        losses.append(softplus_lanes(p))
    return jnp.concatenate(products), jnp.concatenate(losses)


def project(unit, inverse, grad):
    return (grad - unit * jnp.sum(unit * grad, axis=1, keepdims=True)) * inverse


def row_parts(rows, wanted):
    count = wanted if rows % (16 * wanted) == 0 else 1
    return [pl.ds(place * (rows // count), rows // count) for place in range(count)]


def scalar_pair(scalars):
    return scalars[0:1, 0:1], scalars[1:2, 0:1]


def image_is_u():
    return lax.rem(lax.axis_index("blk"), 2) == 0


def is_outer():
    return lax.rem(lax.axis_index("blk"), 2) == lax.axis_index("inner")


def sort_kernel(image, text, u, w, sems):
    def move(image_to, text_to):
        copies = []
        for source, target in ((image, image_to), (text, text_to)):
            for part in row_parts(image.shape[0], 3):
                sem = sems.at[len(copies)]
                copies.append(pltpu.make_async_copy(source.at[part], target.at[part], sem))
        for copy in copies:
            copy.start()
        for copy in copies:
            copy.wait()

    u_is_image = image_is_u()

    @pl.when(u_is_image)
    def _():
        move(u, w)

    @pl.when(jnp.logical_not(u_is_image))
    def _():
        move(w, u)


def pick_kernel(when_outer, when_inner, picked, sem):
    @pl.when(is_outer())
    def _():
        pltpu.async_copy(when_outer, picked, sem).wait()

    @pl.when(jnp.logical_not(is_outer()))
    def _():
        pltpu.async_copy(when_inner, picked, sem).wait()


def other_kernel(both, block, sem):
    pltpu.async_copy(both.at[1 - lax.axis_index("inner")], block, sem).wait()


def near_kernel(
    scalars, image, text, b1, b2, b3,
    z_pair, unit_u, unit_other, inverse_u, inverse_other, grad_u, part_w, loss, work, z_w, grad_w, unit_w,
):
    u_is_image = image_is_u()
    u_weight = u_is_image.astype(F32)
    scale, shift = scalar_pair(scalars)
    image_unit, image_inverse = unit_rows(image[...])
    text_unit, text_inverse = unit_rows(text[...])
    unit_u[...] = jnp.where(u_is_image, image_unit, text_unit)
    unit_w[...] = jnp.where(u_is_image, text_unit, image_unit)
    inverse_u[...] = jnp.where(u_is_image, image_inverse, text_inverse)
    inverse_w = jnp.where(u_is_image, text_inverse, image_inverse)
    unit_other[...], inverse_other[...] = unit_rows(b1[...])
    zi = image_unit.astype(BF16)
    zt = text_unit.astype(BF16)
    z_u = jnp.where(u_is_image, zi, zt)
    z_pair[: zi.shape[0]] = z_u
    z_w[...] = jnp.where(u_is_image, zt, zi)
    scores = scale * dot_nt(zi, zt) + shift
    rows = lax.broadcasted_iota(jnp.int32, scores.shape, 0)
    columns = lax.broadcasted_iota(jnp.int32, scores.shape, 1)
    sign = jnp.where(rows == columns, F32(-1.0), F32(1.0))
    p = jnp.exp(sign * scores)
    coef = (sign * sigmoid_of(p) * scale).astype(BF16)
    total = softplus_lanes(p)
    grad_image = dot_nn(coef, zt)
    grad_text = dot_tn(coef, zi)
    grad_u[...] = jnp.where(u_is_image, grad_image, grad_text)
    grad_w[...] = jnp.where(u_is_image, grad_text, grad_image)
    term, row_loss = pair_step(z_u, (b2[...],), scale, shift, work)
    grad_u[...] += term
    total = total + u_weight * row_loss
    term, row_loss = pair_step(z_w[...], (b1[...], b3[...]), scale, shift, work)
    z_pair[zi.shape[0] :] = work[: zi.shape[0]]
    part_w[...] = project(unit_w[...], inverse_w, grad_w[...] + term)
    loss[...] = total + (1.0 - u_weight) * row_loss


def fifth_kernel(
    scalars, b5, z_pair, unit_other, inverse_other, grad_in, loss_in, grad_u, loss, for_partner, work
):
    rows, width = b5.shape
    term, row_loss = pair_step(z_pair[...], (b5[...],), *scalar_pair(scalars), work)
    for_partner[:, :width] = project(unit_other[...], inverse_other[...], term[rows:]).astype(BF16)
    for_partner[:, width:] = row_loss[rows:].astype(BF16)
    grad_u[...] = grad_in[...] + term[:rows]
    loss[...] = loss_in[...] + image_is_u().astype(F32) * row_loss[:rows]


def u_kernel(scalars, b4, z_pair, grad_u, loss_in, unit, inverse, done_u, loss, work):
    rows = done_u.shape[0]
    term, row_loss = pair_step(z_pair[:rows], (b4[...],), *scalar_pair(scalars), work)
    loss[...] = loss_in[...] + image_is_u().astype(F32) * row_loss
    done_u[...] = project(unit[...], inverse[...], grad_u[...] + term).astype(BF16)


def w_kernel(
    last, part_w, loss_in, done_u, image_grad, text_grad, loss_rows, done_w, sems
):
    u_is_image = image_is_u()
    parts = row_parts(done_w.shape[0], 6)

    def output(action, source, part, to_image, sem):
        @pl.when(to_image)
        def _():
            action(pltpu.make_async_copy(source.at[part], image_grad.at[part], sem))

        @pl.when(jnp.logical_not(to_image))
        def _():
            action(pltpu.make_async_copy(source.at[part], text_grad.at[part], sem))

    whole = pl.ds(0, done_w.shape[0])
    output(lambda copy: copy.start(), done_u, whole, u_is_image, sems.at[0])
    width = done_w.shape[1]
    for place, part in enumerate(parts):
        done_w[part] = (part_w[part] + last[part, :width].astype(F32)).astype(BF16)
        output(lambda copy: copy.start(), done_w, part, jnp.logical_not(u_is_image), sems.at[1 + place])
    total = loss_in[...] + (1.0 - u_is_image.astype(F32)) * last[:, width:].astype(F32)
    loss_rows[...] = jnp.sum(jnp.transpose(total), axis=0) / (SPAN * total.shape[0])
    output(lambda copy: copy.wait(), done_u, whole, u_is_image, sems.at[0])
    for place, part in enumerate(parts):
        output(lambda copy: copy.wait(), done_w, part, jnp.logical_not(u_is_image), sems.at[1 + place])


VMEM = pl.BlockSpec(memory_space=pltpu.VMEM)
ANY = pl.BlockSpec(memory_space=pl.ANY)


def call(kernel, in_specs, args, out_specs, outs, name, scratch=(), flops=1):
    return pl.pallas_call(
        kernel,
        out_shape=outs,
        in_specs=in_specs,
        out_specs=out_specs,
        scratch_shapes=list(scratch),
        name=name,
        cost_estimate=pl.CostEstimate(flops=flops, bytes_accessed=1, transcendentals=0),
        compiler_params=pltpu.CompilerParams(vmem_limit_bytes=VMEM_LIMIT),
    )(*args)


def local(image, text, score_scaling, score_shift):
    rows, width = image.shape
    block = jax.ShapeDtypeStruct((rows, width), BF16)
    pair = jax.ShapeDtypeStruct((2 * rows, width), BF16)
    sums = jax.ShapeDtypeStruct((rows, width), F32)
    column = jax.ShapeDtypeStruct((rows, 1), F32)
    partial = jax.ShapeDtypeStruct((rows, 128), F32)
    line = jax.ShapeDtypeStruct((rows,), F32)
    raw = pltpu.VMEM((rows, width), BF16)
    copies = pltpu.SemaphoreType.DMA((7,))

    def in_hbm(*arrays):
        return [pltpu.with_memory_space_constraint(x, pltpu.HBM) for x in arrays]


    def pick(when_outer, when_inner, out):
        sem = pltpu.SemaphoreType.DMA
        return call(
            pick_kernel, [ANY] * 2, (when_outer, when_inner), [ANY], (out,), "pick", (sem,)
        )[0]

    def across_x(both):
        sem = pltpu.SemaphoreType.DMA
        return call(other_kernel, [ANY], in_hbm(both), [ANY], (block,), "other", (sem,))[0]

    def compute(kernel, args, outs, name, scratch, flops=1):
        in_specs = [VMEM] * (1 + len(args))
        out_specs = [VMEM] * len(outs)
        return call(kernel, in_specs, (scalars, *args), out_specs, outs, name, scratch, flops)

    u, w = call(
        sort_kernel, [ANY] * 2, in_hbm(image, text), [VMEM] * 2, (block, block), "sort", (copies,)
    )
    slot1 = send(w, CORE_SWAP)
    slot2 = send(u, GROUP_SHIFT)
    slot3 = across_x(lax.all_gather(pick(slot1, u, block), "inner"))
    slot4 = send(slot3, GROUP_SHIFT)
    both5 = lax.all_gather(pick(w, slot2, pltpu.HBM((rows, width), BF16)), "inner")
    slot3, score_scaling, score_shift = lax.optimization_barrier((slot3, score_scaling, score_shift))
    first = lax.broadcasted_iota(jnp.int32, (8, 128), 0) == 0
    scalars = jnp.where(first, score_scaling, score_shift)
    z_pair, unit_u, unit_other, inverse_u, inverse_other, grad_u, part_w, loss = compute(
        near_kernel,
        (*in_hbm(image, text), slot1, *in_hbm(slot2, slot3)),
        (pair, sums, sums, column, column, sums, sums, partial),
        "near_blocks",
        (pltpu.VMEM((2 * rows, width), BF16), raw) + (pltpu.VMEM((rows, width), F32),) * 2,
    )
    both5, loss = lax.optimization_barrier((both5, loss))
    slot5 = across_x(both5)
    grad_u, loss, for_partner = compute(
        fifth_kernel,
        (pltpu.with_memory_space_constraint(slot5, pltpu.VMEM), z_pair, unit_other, inverse_other, grad_u, loss),
        (sums, partial, jax.ShapeDtypeStruct((rows, width + 128), BF16)),
        "fifth_block",
        (raw,),
    )
    last = send(for_partner, CORE_SWAP)
    done_u, loss = compute(
        u_kernel,
        (pltpu.with_memory_space_constraint(slot4, pltpu.VMEM), z_pair, grad_u, loss, unit_u, inverse_u),
        (block, partial),
        "finish_u",
        (raw,),
        10**10,
    )
    image_grad, text_grad, loss_rows = call(
        w_kernel,
        [VMEM] * 4,
        (last, part_w, loss, done_u),
        [ANY, ANY, VMEM],
        (block, block, line),
        "finish_w",
        (raw, copies),
    )
    return loss_rows, image_grad, text_grad


def solution(mesh):
    in_specs = (P(AXES, None), P(AXES, None), P(), P())
    out_specs = (P(AXES), P(AXES, None), P(AXES, None))
    return jax.shard_map(local, mesh=mesh, in_specs=in_specs, out_specs=out_specs, check_vma=False)
```

```python
import jax
import jax.numpy as jnp
from jax import lax
from jax.experimental import pallas as pl
from jax.experimental.pallas import tpu as pltpu
from jax.sharding import PartitionSpec as P

SPAN = 4
GROUP = 4
AXES = ("blk", "inner")
F32 = jnp.float32
BF16 = jnp.bfloat16
VMEM_LIMIT = 28 * 1024 * 1024

X_SWAP = {0: (1, 0), 1: (0, 0), 2: (3, 0), 3: (2, 0)}
CORE_SWAP = {0: (2, 0), 1: (3, 0), 2: (0, 0), 3: (1, 0)}
GROUP_SHIFT = {0: (2, -1), 1: (3, -1), 2: (0, 1), 3: (1, 1)}


def send(value, moves):
    count = lax.axis_size(AXES)
    groups = count // GROUP
    pairs = [
        (g * GROUP + role, (g + step) % groups * GROUP + to)
        for g in range(groups)
        for role, (to, step) in moves.items()
    ]
    return lax.ppermute(value, AXES, pairs)


def unit_rows(raw):
    values = raw.astype(F32)
    inverse = 1.0 / jnp.sqrt(jnp.sum(values * values, axis=1, keepdims=True) + 1e-06)
    return values * inverse, inverse


def sigmoid_of(p):
    whole = 1.0 + p
    guess = pl.reciprocal(whole, approx=True)
    guess = guess * (2.0 - whole * guess)
    return p * (guess * (2.0 - whole * guess))


def log1p_of(p):
    below = p * (1.0 - p * (0.5 - p * (1.0 / 3.0)))
    return jnp.where(p < 0.015625, below, jnp.log(1.0 + p))


def softplus_lanes(p):
    total = None
    parts = [p[:, start : start + 128] for start in range(0, p.shape[1], 128)]
    for first in range(0, len(parts), 3):
        joint = parts[first]
        for part in parts[first + 1 : first + 3]:
            joint = joint + part + joint * part
        value = log1p_of(joint)
        total = value if total is None else total + value
    return total


def dot_nt(a, b):
    return lax.dot_general(a, b, (((1,), (1,)), ((), ())), preferred_element_type=F32)


def dot_nn(a, b):
    return lax.dot_general(a, b, (((1,), (0,)), ((), ())), preferred_element_type=F32)


def dot_tn(a, b):
    return lax.dot_general(a, b, (((0,), (0,)), ((), ())), preferred_element_type=F32)


def pair_step(own, blocks, scale, shift, work):
    rows = blocks[0].shape[0]
    for place, raw in enumerate(blocks):
        work[place * rows : (place + 1) * rows] = unit_rows(raw)[0].astype(BF16)
    return terms(own, work[: len(blocks) * rows], scale, shift)


def terms(own, others, scale, shift):
    half = own.shape[0] // 2
    scores = [dot_nt(own[:half], others), dot_nt(own[half:], others)]
    products, losses = [], []
    for score in scores:
        p = jnp.exp(scale * score + shift)
        coef = (sigmoid_of(p) * scale).astype(BF16)
        products.append(dot_nn(coef, others))
        losses.append(softplus_lanes(p))
    return jnp.concatenate(products), jnp.concatenate(losses)


def project(unit, inverse, grad):
    return (grad - unit * jnp.sum(unit * grad, axis=1, keepdims=True)) * inverse


def row_parts(rows, wanted):
    count = wanted if rows % (16 * wanted) == 0 else 1
    return [pl.ds(place * (rows // count), rows // count) for place in range(count)]


def scalar_pair(scalars):
    return scalars[0:1, 0:1], scalars[1:2, 0:1]


def image_is_u():
    return lax.rem(lax.axis_index("blk"), 2) == 0


def is_outer():
    return lax.rem(lax.axis_index("blk"), 2) == lax.axis_index("inner")


def sort_kernel(image, text, u, w, sems):
    def move(image_to, text_to):
        copies = []
        for source, target in ((image, image_to), (text, text_to)):
            for part in row_parts(image.shape[0], 3):
                sem = sems.at[len(copies)]
                copies.append(pltpu.make_async_copy(source.at[part], target.at[part], sem))
        for copy in copies:
            copy.start()
        for copy in copies:
            copy.wait()

    u_is_image = image_is_u()

    @pl.when(u_is_image)
    def _():
        move(u, w)

    @pl.when(jnp.logical_not(u_is_image))
    def _():
        move(w, u)


def pick_kernel(when_outer, when_inner, picked, sem):
    @pl.when(is_outer())
    def _():
        pltpu.async_copy(when_outer, picked, sem).wait()

    @pl.when(jnp.logical_not(is_outer()))
    def _():
        pltpu.async_copy(when_inner, picked, sem).wait()


def near_kernel(
    scalars, image, text, b1, b2, b3,
    z_pair, unit_u, unit_other, inverse_u, inverse_other, grad_u, part_w, loss, work, z_w, grad_w, unit_w,
):
    u_is_image = image_is_u()
    u_weight = u_is_image.astype(F32)
    scale, shift = scalar_pair(scalars)
    image_unit, image_inverse = unit_rows(image[...])
    text_unit, text_inverse = unit_rows(text[...])
    unit_u[...] = jnp.where(u_is_image, image_unit, text_unit)
    unit_w[...] = jnp.where(u_is_image, text_unit, image_unit)
    inverse_u[...] = jnp.where(u_is_image, image_inverse, text_inverse)
    inverse_w = jnp.where(u_is_image, text_inverse, image_inverse)
    unit_other[...], inverse_other[...] = unit_rows(b1[...])
    zi = image_unit.astype(BF16)
    zt = text_unit.astype(BF16)
    z_u = jnp.where(u_is_image, zi, zt)
    z_pair[: zi.shape[0]] = z_u
    z_w[...] = jnp.where(u_is_image, zt, zi)
    scores = scale * dot_nt(zi, zt) + shift
    rows = lax.broadcasted_iota(jnp.int32, scores.shape, 0)
    columns = lax.broadcasted_iota(jnp.int32, scores.shape, 1)
    sign = jnp.where(rows == columns, F32(-1.0), F32(1.0))
    p = jnp.exp(sign * scores)
    coef = (sign * sigmoid_of(p) * scale).astype(BF16)
    total = softplus_lanes(p)
    grad_image = dot_nn(coef, zt)
    grad_text = dot_tn(coef, zi)
    grad_u[...] = jnp.where(u_is_image, grad_image, grad_text)
    grad_w[...] = jnp.where(u_is_image, grad_text, grad_image)
    term, row_loss = pair_step(z_u, (b2[...],), scale, shift, work)
    grad_u[...] += term
    total = total + u_weight * row_loss
    term, row_loss = pair_step(z_w[...], (b1[...], b3[...]), scale, shift, work)
    z_pair[zi.shape[0] :] = work[: zi.shape[0]]
    part_w[...] = project(unit_w[...], inverse_w, grad_w[...] + term)
    loss[...] = total + (1.0 - u_weight) * row_loss


def fifth_kernel(
    scalars, b5, z_pair, unit_other, inverse_other, grad_in, loss_in, grad_u, loss, for_partner, work
):
    rows, width = b5.shape
    term, row_loss = pair_step(z_pair[...], (b5[...],), *scalar_pair(scalars), work)
    for_partner[:, :width] = project(unit_other[...], inverse_other[...], term[rows:]).astype(BF16)
    for_partner[:, width:] = row_loss[rows:].astype(BF16)
    grad_u[...] = grad_in[...] + term[:rows]
    loss[...] = loss_in[...] + image_is_u().astype(F32) * row_loss[:rows]


def u_kernel(scalars, b4, z_pair, grad_u, loss_in, unit, inverse, done_u, loss, work):
    rows = done_u.shape[0]
    term, row_loss = pair_step(z_pair[:rows], (b4[...],), *scalar_pair(scalars), work)
    loss[...] = loss_in[...] + image_is_u().astype(F32) * row_loss
    done_u[...] = project(unit[...], inverse[...], grad_u[...] + term).astype(BF16)


def w_kernel(
    last, part_w, loss_in, done_u, image_grad, text_grad, loss_rows, done_w, sems
):
    u_is_image = image_is_u()
    parts = row_parts(done_w.shape[0], 6)

    def output(action, source, part, to_image, sem):
        @pl.when(to_image)
        def _():
            action(pltpu.make_async_copy(source.at[part], image_grad.at[part], sem))

        @pl.when(jnp.logical_not(to_image))
        def _():
            action(pltpu.make_async_copy(source.at[part], text_grad.at[part], sem))

    whole = pl.ds(0, done_w.shape[0])
    output(lambda copy: copy.start(), done_u, whole, u_is_image, sems.at[0])
    width = done_w.shape[1]
    for place, part in enumerate(parts):
        done_w[part] = (part_w[part] + last[part, :width].astype(F32)).astype(BF16)
        output(lambda copy: copy.start(), done_w, part, jnp.logical_not(u_is_image), sems.at[1 + place])
    total = loss_in[...] + (1.0 - u_is_image.astype(F32)) * last[:, width:].astype(F32)
    loss_rows[...] = jnp.sum(jnp.transpose(total), axis=0) / (SPAN * total.shape[0])
    output(lambda copy: copy.wait(), done_u, whole, u_is_image, sems.at[0])
    for place, part in enumerate(parts):
        output(lambda copy: copy.wait(), done_w, part, jnp.logical_not(u_is_image), sems.at[1 + place])


VMEM = pl.BlockSpec(memory_space=pltpu.VMEM)
ANY = pl.BlockSpec(memory_space=pl.ANY)


def call(kernel, in_specs, args, out_specs, outs, name, scratch=(), flops=1):
    return pl.pallas_call(
        kernel,
        out_shape=outs,
        in_specs=in_specs,
        out_specs=out_specs,
        scratch_shapes=list(scratch),
        name=name,
        cost_estimate=pl.CostEstimate(flops=flops, bytes_accessed=1, transcendentals=0),
        compiler_params=pltpu.CompilerParams(vmem_limit_bytes=VMEM_LIMIT),
    )(*args)


def local(image, text, score_scaling, score_shift):
    rows, width = image.shape
    block = jax.ShapeDtypeStruct((rows, width), BF16)
    pair = jax.ShapeDtypeStruct((2 * rows, width), BF16)
    sums = jax.ShapeDtypeStruct((rows, width), F32)
    column = jax.ShapeDtypeStruct((rows, 1), F32)
    partial = jax.ShapeDtypeStruct((rows, 128), F32)
    line = jax.ShapeDtypeStruct((rows,), F32)
    raw = pltpu.VMEM((rows, width), BF16)
    copies = pltpu.SemaphoreType.DMA((7,))

    def in_hbm(*arrays):
        return [pltpu.with_memory_space_constraint(x, pltpu.HBM) for x in arrays]


    def pick(when_outer, when_inner, out):
        sem = pltpu.SemaphoreType.DMA
        return call(
            pick_kernel, [ANY] * 2, (when_outer, when_inner), [ANY], (out,), "pick", (sem,)
        )[0]

    def compute(kernel, args, outs, name, scratch, flops=1):
        in_specs = [VMEM] * (1 + len(args))
        out_specs = [VMEM] * len(outs)
        return call(kernel, in_specs, (scalars, *args), out_specs, outs, name, scratch, flops)

    u, w = call(
        sort_kernel, [ANY] * 2, in_hbm(image, text), [VMEM] * 2, (block, block), "sort", (copies,)
    )
    slot1 = send(w, CORE_SWAP)
    slot2 = send(u, GROUP_SHIFT)
    slot3 = send(pick(slot1, u, block), X_SWAP)
    slot4 = send(slot3, GROUP_SHIFT)
    slot5 = send(pick(w, slot2, pltpu.HBM((rows, width), BF16)), X_SWAP)
    slot3, score_scaling, score_shift = lax.optimization_barrier((slot3, score_scaling, score_shift))
    first = lax.broadcasted_iota(jnp.int32, (8, 128), 0) == 0
    scalars = jnp.where(first, score_scaling, score_shift)
    z_pair, unit_u, unit_other, inverse_u, inverse_other, grad_u, part_w, loss = compute(
        near_kernel,
        (*in_hbm(image, text, slot1, slot2), slot3),
        (pair, sums, sums, column, column, sums, sums, partial),
        "near_blocks",
        (pltpu.VMEM((2 * rows, width), BF16), raw) + (pltpu.VMEM((rows, width), F32),) * 2,
    )
    grad_u, loss, for_partner = compute(
        fifth_kernel,
        (pltpu.with_memory_space_constraint(slot5, pltpu.VMEM), z_pair, unit_other, inverse_other, grad_u, loss),
        (sums, partial, jax.ShapeDtypeStruct((rows, width + 128), BF16)),
        "fifth_block",
        (raw,),
    )
    last = send(for_partner, CORE_SWAP)
    done_u, loss = compute(
        u_kernel,
        (pltpu.with_memory_space_constraint(slot4, pltpu.VMEM), z_pair, grad_u, loss, unit_u, inverse_u),
        (block, partial),
        "finish_u",
        (raw,),
        10**10,
    )
    image_grad, text_grad, loss_rows = call(
        w_kernel,
        [VMEM] * 4,
        (last, part_w, loss, done_u),
        [ANY, ANY, VMEM],
        (block, block, line),
        "finish_w",
        (raw, copies),
    )
    return loss_rows, image_grad, text_grad


def solution(mesh):
    in_specs = (P(AXES, None), P(AXES, None), P(), P())
    out_specs = (P(AXES), P(AXES, None), P(AXES, None))
    return jax.shard_map(local, mesh=mesh, in_specs=in_specs, out_specs=out_specs, check_vma=False)
```

```python
import jax
import jax.numpy as jnp
from jax import lax
from jax.experimental import pallas as pl
from jax.experimental.pallas import tpu as pltpu
from jax.sharding import PartitionSpec as P

SPAN = 4
GROUP = 4
AXES = ("blk", "inner")
F32 = jnp.float32
BF16 = jnp.bfloat16
VMEM_LIMIT = 28 * 1024 * 1024

X_SWAP = {0: (1, 0), 1: (0, 0), 2: (3, 0), 3: (2, 0)}
CORE_SWAP = {0: (2, 0), 1: (3, 0), 2: (0, 0), 3: (1, 0)}
GROUP_SHIFT = {0: (2, -1), 1: (3, -1), 2: (0, 1), 3: (1, 1)}


def send(value, moves):
    count = lax.axis_size(AXES)
    groups = count // GROUP
    pairs = [
        (g * GROUP + role, (g + step) % groups * GROUP + to)
        for g in range(groups)
        for role, (to, step) in moves.items()
    ]
    return lax.ppermute(value, AXES, pairs)


def unit_rows(raw):
    values = raw.astype(F32)
    inverse = 1.0 / jnp.sqrt(jnp.sum(values * values, axis=1, keepdims=True) + 1e-06)
    return values * inverse, inverse


def sigmoid_of(p):
    whole = 1.0 + p
    guess = pl.reciprocal(whole, approx=True)
    guess = guess * (2.0 - whole * guess)
    return p * (guess * (2.0 - whole * guess))


def log1p_of(p):
    below = p * (1.0 - p * (0.5 - p * (1.0 / 3.0)))
    return jnp.where(p < 0.015625, below, jnp.log(1.0 + p))


def softplus_lanes(p):
    total = None
    parts = [p[:, start : start + 128] for start in range(0, p.shape[1], 128)]
    for first in range(0, len(parts), 3):
        joint = parts[first]
        for part in parts[first + 1 : first + 3]:
            joint = joint + part + joint * part
        value = log1p_of(joint)
        total = value if total is None else total + value
    return total


def dot_nt(a, b):
    return lax.dot_general(a, b, (((1,), (1,)), ((), ())), preferred_element_type=F32)


def dot_nn(a, b):
    return lax.dot_general(a, b, (((1,), (0,)), ((), ())), preferred_element_type=F32)


def dot_tn(a, b):
    return lax.dot_general(a, b, (((0,), (0,)), ((), ())), preferred_element_type=F32)


def pair_step(own, blocks, scale, shift, work):
    rows = blocks[0].shape[0]
    for place, raw in enumerate(blocks):
        work[place * rows : (place + 1) * rows] = unit_rows(raw)[0].astype(BF16)
    return terms(own, work[: len(blocks) * rows], scale, shift)


def terms(own, others, scale, shift):
    half = own.shape[0] // 2
    scores = [dot_nt(own[:half], others), dot_nt(own[half:], others)]
    products, losses = [], []
    for score in scores:
        p = jnp.exp(scale * score + shift)
        coef = (sigmoid_of(p) * scale).astype(BF16)
        products.append(dot_nn(coef, others))
        losses.append(softplus_lanes(p))
    return jnp.concatenate(products), jnp.concatenate(losses)


def project(unit, inverse, grad):
    return (grad - unit * jnp.sum(unit * grad, axis=1, keepdims=True)) * inverse


def row_parts(rows, wanted):
    count = wanted if rows % (16 * wanted) == 0 else 1
    return [pl.ds(place * (rows // count), rows // count) for place in range(count)]


def scalar_pair(scalars):
    return scalars[0:1, 0:1], scalars[1:2, 0:1]


def image_is_u():
    return lax.rem(lax.axis_index("blk"), 2) == 0


def is_outer():
    return lax.rem(lax.axis_index("blk"), 2) == lax.axis_index("inner")


def sort_kernel(image, text, u, w, sems):
    def move(image_to, text_to):
        copies = []
        for source, target in ((image, image_to), (text, text_to)):
            for part in row_parts(image.shape[0], 3):
                sem = sems.at[len(copies)]
                copies.append(pltpu.make_async_copy(source.at[part], target.at[part], sem))
        for copy in copies:
            copy.start()
        for copy in copies:
            copy.wait()

    u_is_image = image_is_u()

    @pl.when(u_is_image)
    def _():
        move(u, w)

    @pl.when(jnp.logical_not(u_is_image))
    def _():
        move(w, u)


def pick_kernel(when_outer, when_inner, picked, sem):
    @pl.when(is_outer())
    def _():
        pltpu.async_copy(when_outer, picked, sem).wait()

    @pl.when(jnp.logical_not(is_outer()))
    def _():
        pltpu.async_copy(when_inner, picked, sem).wait()


def near_kernel(
    scalars, image, text, b1, b2, b3,
    z_pair, unit_u, unit_other, inverse_u, inverse_other, grad_u, part_w, loss, work, z_w, grad_w, unit_w,
):
    u_is_image = image_is_u()
    u_weight = u_is_image.astype(F32)
    scale, shift = scalar_pair(scalars)
    image_unit, image_inverse = unit_rows(image[...])
    text_unit, text_inverse = unit_rows(text[...])
    unit_u[...] = jnp.where(u_is_image, image_unit, text_unit)
    unit_w[...] = jnp.where(u_is_image, text_unit, image_unit)
    inverse_u[...] = jnp.where(u_is_image, image_inverse, text_inverse)
    inverse_w = jnp.where(u_is_image, text_inverse, image_inverse)
    unit_other[...], inverse_other[...] = unit_rows(b1[...])
    zi = image_unit.astype(BF16)
    zt = text_unit.astype(BF16)
    z_u = jnp.where(u_is_image, zi, zt)
    z_pair[: zi.shape[0]] = z_u
    z_w[...] = jnp.where(u_is_image, zt, zi)
    scores = scale * dot_nt(zi, zt) + shift
    rows = lax.broadcasted_iota(jnp.int32, scores.shape, 0)
    columns = lax.broadcasted_iota(jnp.int32, scores.shape, 1)
    sign = jnp.where(rows == columns, F32(-1.0), F32(1.0))
    p = jnp.exp(sign * scores)
    coef = (sign * sigmoid_of(p) * scale).astype(BF16)
    total = softplus_lanes(p)
    grad_image = dot_nn(coef, zt)
    grad_text = dot_tn(coef, zi)
    grad_u[...] = jnp.where(u_is_image, grad_image, grad_text)
    grad_w[...] = jnp.where(u_is_image, grad_text, grad_image)
    term, row_loss = pair_step(z_u, (b2[...],), scale, shift, work)
    grad_u[...] += term
    total = total + u_weight * row_loss
    term, row_loss = pair_step(z_w[...], (b1[...], b3[...]), scale, shift, work)
    z_pair[zi.shape[0] :] = work[: zi.shape[0]]
    part_w[...] = project(unit_w[...], inverse_w, grad_w[...] + term)
    loss[...] = total + (1.0 - u_weight) * row_loss


def fifth_kernel(
    scalars, b5, z_pair, unit_other, inverse_other, grad_in, loss_in, grad_u, loss, for_partner, work
):
    rows, width = b5.shape
    term, row_loss = pair_step(z_pair[...], (b5[...],), *scalar_pair(scalars), work)
    for_partner[:, :width] = project(unit_other[...], inverse_other[...], term[rows:]).astype(BF16)
    for_partner[:, width:] = row_loss[rows:].astype(BF16)
    grad_u[...] = grad_in[...] + term[:rows]
    loss[...] = loss_in[...] + image_is_u().astype(F32) * row_loss[:rows]


def u_kernel(scalars, b4, z_pair, grad_u, loss_in, unit, inverse, done_u, loss, work):
    rows = done_u.shape[0]
    term, row_loss = pair_step(z_pair[:rows], (b4[...],), *scalar_pair(scalars), work)
    loss[...] = loss_in[...] + image_is_u().astype(F32) * row_loss
    done_u[...] = project(unit[...], inverse[...], grad_u[...] + term).astype(BF16)


def w_kernel(
    last, part_w, loss_in, done_u, image_grad, text_grad, loss_rows, done_w, sems
):
    u_is_image = image_is_u()
    parts = row_parts(done_w.shape[0], 6)

    def output(action, source, part, to_image, sem):
        @pl.when(to_image)
        def _():
            action(pltpu.make_async_copy(source.at[part], image_grad.at[part], sem))

        @pl.when(jnp.logical_not(to_image))
        def _():
            action(pltpu.make_async_copy(source.at[part], text_grad.at[part], sem))

    whole = pl.ds(0, done_w.shape[0])
    output(lambda copy: copy.start(), done_u, whole, u_is_image, sems.at[0])
    width = done_w.shape[1]
    for place, part in enumerate(parts):
        done_w[part] = (part_w[part] + last[part, :width].astype(F32)).astype(BF16)
        output(lambda copy: copy.start(), done_w, part, jnp.logical_not(u_is_image), sems.at[1 + place])
    total = loss_in[...] + (1.0 - u_is_image.astype(F32)) * last[:, width:].astype(F32)
    loss_rows[...] = jnp.sum(jnp.transpose(total), axis=0) / (SPAN * total.shape[0])
    output(lambda copy: copy.wait(), done_u, whole, u_is_image, sems.at[0])
    for place, part in enumerate(parts):
        output(lambda copy: copy.wait(), done_w, part, jnp.logical_not(u_is_image), sems.at[1 + place])


VMEM = pl.BlockSpec(memory_space=pltpu.VMEM)
ANY = pl.BlockSpec(memory_space=pl.ANY)


def call(kernel, in_specs, args, out_specs, outs, name, scratch=(), flops=1):
    return pl.pallas_call(
        kernel,
        out_shape=outs,
        in_specs=in_specs,
        out_specs=out_specs,
        scratch_shapes=list(scratch),
        name=name,
        cost_estimate=pl.CostEstimate(flops=flops, bytes_accessed=1, transcendentals=0),
        compiler_params=pltpu.CompilerParams(vmem_limit_bytes=VMEM_LIMIT),
    )(*args)


def local(image, text, score_scaling, score_shift):
    rows, width = image.shape
    block = jax.ShapeDtypeStruct((rows, width), BF16)
    pair = jax.ShapeDtypeStruct((2 * rows, width), BF16)
    sums = jax.ShapeDtypeStruct((rows, width), F32)
    column = jax.ShapeDtypeStruct((rows, 1), F32)
    partial = jax.ShapeDtypeStruct((rows, 128), F32)
    line = jax.ShapeDtypeStruct((rows,), F32)
    raw = pltpu.VMEM((rows, width), BF16)
    copies = pltpu.SemaphoreType.DMA((7,))

    def in_hbm(*arrays):
        return [pltpu.with_memory_space_constraint(x, pltpu.HBM) for x in arrays]


    def pick(when_outer, when_inner, out):
        sem = pltpu.SemaphoreType.DMA
        return call(
            pick_kernel, [ANY] * 2, (when_outer, when_inner), [ANY], (out,), "pick", (sem,)
        )[0]

    def compute(kernel, args, outs, name, scratch, flops=1):
        in_specs = [VMEM] * (1 + len(args))
        out_specs = [VMEM] * len(outs)
        return call(kernel, in_specs, (scalars, *args), out_specs, outs, name, scratch, flops)

    u, w = call(
        sort_kernel, [ANY] * 2, in_hbm(image, text), [VMEM] * 2, (block, block), "sort", (copies,)
    )
    slot1 = send(w, CORE_SWAP)
    slot2 = send(u, GROUP_SHIFT)
    slot3 = send(pick(slot1, u, block), X_SWAP)
    slot4 = send(slot3, GROUP_SHIFT)
    slot5 = send(pick(w, slot2, block), X_SWAP)
    slot3, score_scaling, score_shift = lax.optimization_barrier((slot3, score_scaling, score_shift))
    first = lax.broadcasted_iota(jnp.int32, (8, 128), 0) == 0
    scalars = jnp.where(first, score_scaling, score_shift)
    z_pair, unit_u, unit_other, inverse_u, inverse_other, grad_u, part_w, loss = compute(
        near_kernel,
        (*in_hbm(image, text, slot1, slot2), slot3),
        (pair, sums, sums, column, column, sums, sums, partial),
        "near_blocks",
        (pltpu.VMEM((2 * rows, width), BF16), raw) + (pltpu.VMEM((rows, width), F32),) * 2,
    )
    grad_u, loss, for_partner = compute(
        fifth_kernel,
        (pltpu.with_memory_space_constraint(slot5, pltpu.VMEM), z_pair, unit_other, inverse_other, grad_u, loss),
        (sums, partial, jax.ShapeDtypeStruct((rows, width + 128), BF16)),
        "fifth_block",
        (raw,),
    )
    last = send(for_partner, CORE_SWAP)
    done_u, loss = compute(
        u_kernel,
        (pltpu.with_memory_space_constraint(slot4, pltpu.VMEM), z_pair, grad_u, loss, unit_u, inverse_u),
        (block, partial),
        "finish_u",
        (raw,),
        10**10,
    )
    image_grad, text_grad, loss_rows = call(
        w_kernel,
        [VMEM] * 4,
        (last, part_w, loss, done_u),
        [ANY, ANY, VMEM],
        (block, block, line),
        "finish_w",
        (raw, copies),
    )
    return loss_rows, image_grad, text_grad


def solution(mesh):
    in_specs = (P(AXES, None), P(AXES, None), P(), P())
    out_specs = (P(AXES), P(AXES, None), P(AXES, None))
    return jax.shard_map(local, mesh=mesh, in_specs=in_specs, out_specs=out_specs, check_vma=False)
```

```python
import jax
import jax.numpy as jnp
from jax import lax
from jax.experimental import pallas as pl
from jax.experimental.pallas import tpu as pltpu
from jax.sharding import PartitionSpec as P

SPAN = 4
GROUP = 4
AXES = ("blk", "inner")
F32 = jnp.float32
BF16 = jnp.bfloat16
VMEM_LIMIT = 28 * 1024 * 1024

X_SWAP = {0: (1, 0), 1: (0, 0), 2: (3, 0), 3: (2, 0)}
CORE_SWAP = {0: (2, 0), 1: (3, 0), 2: (0, 0), 3: (1, 0)}
GROUP_SHIFT = {0: (2, -1), 1: (3, -1), 2: (0, 1), 3: (1, 1)}


def send(value, moves):
    count = lax.axis_size(AXES)
    groups = count // GROUP
    pairs = [
        (g * GROUP + role, (g + step) % groups * GROUP + to)
        for g in range(groups)
        for role, (to, step) in moves.items()
    ]
    return lax.ppermute(value, AXES, pairs)


def unit_rows(raw):
    values = raw.astype(F32)
    inverse = 1.0 / jnp.sqrt(jnp.sum(values * values, axis=1, keepdims=True) + 1e-06)
    return values * inverse, inverse


def sigmoid_of(p):
    whole = 1.0 + p
    guess = pl.reciprocal(whole, approx=True)
    guess = guess * (2.0 - whole * guess)
    return p * (guess * (2.0 - whole * guess))


def log1p_of(p):
    below = p * (1.0 - p * (0.5 - p * (1.0 / 3.0)))
    return jnp.where(p < 0.015625, below, jnp.log(1.0 + p))


def softplus_lanes(p):
    total = None
    parts = [p[:, start : start + 128] for start in range(0, p.shape[1], 128)]
    for first in range(0, len(parts), 3):
        joint = parts[first]
        for part in parts[first + 1 : first + 3]:
            joint = joint + part + joint * part
        value = log1p_of(joint)
        total = value if total is None else total + value
    return total


def dot_nt(a, b):
    return lax.dot_general(a, b, (((1,), (1,)), ((), ())), preferred_element_type=F32)


def dot_nn(a, b):
    return lax.dot_general(a, b, (((1,), (0,)), ((), ())), preferred_element_type=F32)


def dot_tn(a, b):
    return lax.dot_general(a, b, (((0,), (0,)), ((), ())), preferred_element_type=F32)


def pair_step(own, blocks, scale, shift, work):
    rows = blocks[0].shape[0]
    for place, raw in enumerate(blocks):
        work[place * rows : (place + 1) * rows] = unit_rows(raw)[0].astype(BF16)
    return terms(own, work[: len(blocks) * rows], scale, shift)


def terms(own, others, scale, shift):
    half = own.shape[0] // 2
    scores = [dot_nt(own[:half], others), dot_nt(own[half:], others)]
    products, losses = [], []
    for score in scores:
        p = jnp.exp(scale * score + shift)
        coef = (sigmoid_of(p) * scale).astype(BF16)
        products.append(dot_nn(coef, others))
        losses.append(softplus_lanes(p))
    return jnp.concatenate(products), jnp.concatenate(losses)


def raw_terms(own, raw, scale, shift):
    values = raw.astype(F32)
    inverse = 1.0 / jnp.sqrt(jnp.sum(values * values, axis=1, keepdims=True) + 1e-06)
    factor = scale * jnp.transpose(jnp.broadcast_to(inverse, (raw.shape[0], 128)))[:1]
    half = own.shape[0] // 2
    scores = [dot_nt(own[:half], raw), dot_nt(own[half:], raw)]
    products, losses = [], []
    for score in scores:
        p = jnp.exp(factor * score + shift)
        products.append(dot_nn((sigmoid_of(p) * factor).astype(BF16), raw))
        losses.append(softplus_lanes(p))
    return jnp.concatenate(products), jnp.concatenate(losses)


def project(unit, inverse, grad):
    return (grad - unit * jnp.sum(unit * grad, axis=1, keepdims=True)) * inverse


def row_parts(rows, wanted):
    count = wanted if rows % (16 * wanted) == 0 else 1
    return [pl.ds(place * (rows // count), rows // count) for place in range(count)]


def scalar_pair(scalars):
    return scalars[0:1, 0:1], scalars[1:2, 0:1]


def image_is_u():
    return lax.rem(lax.axis_index("blk"), 2) == 0


def is_outer():
    return lax.rem(lax.axis_index("blk"), 2) == lax.axis_index("inner")


def sort_kernel(image, text, u, w, sems):
    def move(image_to, text_to):
        copies = []
        for source, target in ((image, image_to), (text, text_to)):
            for part in row_parts(image.shape[0], 3):
                sem = sems.at[len(copies)]
                copies.append(pltpu.make_async_copy(source.at[part], target.at[part], sem))
        for copy in copies:
            copy.start()
        for copy in copies:
            copy.wait()

    u_is_image = image_is_u()

    @pl.when(u_is_image)
    def _():
        move(u, w)

    @pl.when(jnp.logical_not(u_is_image))
    def _():
        move(w, u)


def pick_kernel(when_outer, when_inner, picked, sem):
    @pl.when(is_outer())
    def _():
        pltpu.async_copy(when_outer, picked, sem).wait()

    @pl.when(jnp.logical_not(is_outer()))
    def _():
        pltpu.async_copy(when_inner, picked, sem).wait()


def near_kernel(
    scalars, image, text, b1, b2, b3,
    z_pair, unit_u, unit_other, inverse_u, inverse_other, grad_u, part_w, loss, work, z_w, grad_w, unit_w,
):
    u_is_image = image_is_u()
    u_weight = u_is_image.astype(F32)
    scale, shift = scalar_pair(scalars)
    image_unit, image_inverse = unit_rows(image[...])
    text_unit, text_inverse = unit_rows(text[...])
    unit_u[...] = jnp.where(u_is_image, image_unit, text_unit)
    unit_w[...] = jnp.where(u_is_image, text_unit, image_unit)
    inverse_u[...] = jnp.where(u_is_image, image_inverse, text_inverse)
    inverse_w = jnp.where(u_is_image, text_inverse, image_inverse)
    unit_other[...], inverse_other[...] = unit_rows(b1[...])
    zi = image_unit.astype(BF16)
    zt = text_unit.astype(BF16)
    z_u = jnp.where(u_is_image, zi, zt)
    z_pair[: zi.shape[0]] = z_u
    z_w[...] = jnp.where(u_is_image, zt, zi)
    scores = scale * dot_nt(zi, zt) + shift
    rows = lax.broadcasted_iota(jnp.int32, scores.shape, 0)
    columns = lax.broadcasted_iota(jnp.int32, scores.shape, 1)
    sign = jnp.where(rows == columns, F32(-1.0), F32(1.0))
    p = jnp.exp(sign * scores)
    coef = (sign * sigmoid_of(p) * scale).astype(BF16)
    total = softplus_lanes(p)
    grad_image = dot_nn(coef, zt)
    grad_text = dot_tn(coef, zi)
    grad_u[...] = jnp.where(u_is_image, grad_image, grad_text)
    grad_w[...] = jnp.where(u_is_image, grad_text, grad_image)
    term, row_loss = pair_step(z_u, (b2[...],), scale, shift, work)
    grad_u[...] += term
    total = total + u_weight * row_loss
    term, row_loss = pair_step(z_w[...], (b1[...], b3[...]), scale, shift, work)
    z_pair[zi.shape[0] :] = work[: zi.shape[0]]
    part_w[...] = project(unit_w[...], inverse_w, grad_w[...] + term)
    loss[...] = total + (1.0 - u_weight) * row_loss


def fifth_kernel(
    scalars, b5, z_pair, unit_other, inverse_other, grad_in, loss_in, grad_u, loss, for_partner
):
    rows, width = b5.shape
    term, row_loss = raw_terms(z_pair[...], b5[...], *scalar_pair(scalars))
    for_partner[:, :width] = project(unit_other[...], inverse_other[...], term[rows:]).astype(BF16)
    for_partner[:, width:] = row_loss[rows:].astype(BF16)
    grad_u[...] = grad_in[...] + term[:rows]
    loss[...] = loss_in[...] + image_is_u().astype(F32) * row_loss[:rows]


def u_kernel(scalars, b4, z_pair, grad_u, loss_in, unit, inverse, done_u, loss):
    rows = done_u.shape[0]
    term, row_loss = raw_terms(z_pair[:rows], b4[...], *scalar_pair(scalars))
    loss[...] = loss_in[...] + image_is_u().astype(F32) * row_loss
    done_u[...] = project(unit[...], inverse[...], grad_u[...] + term).astype(BF16)


def w_kernel(
    last, part_w, loss_in, done_u, image_grad, text_grad, loss_rows, done_w, sems
):
    u_is_image = image_is_u()
    parts = row_parts(done_w.shape[0], 6)

    def output(action, source, part, to_image, sem):
        @pl.when(to_image)
        def _():
            action(pltpu.make_async_copy(source.at[part], image_grad.at[part], sem))

        @pl.when(jnp.logical_not(to_image))
        def _():
            action(pltpu.make_async_copy(source.at[part], text_grad.at[part], sem))

    whole = pl.ds(0, done_w.shape[0])
    output(lambda copy: copy.start(), done_u, whole, u_is_image, sems.at[0])
    width = done_w.shape[1]
    for place, part in enumerate(parts):
        done_w[part] = (part_w[part] + last[part, :width].astype(F32)).astype(BF16)
        output(lambda copy: copy.start(), done_w, part, jnp.logical_not(u_is_image), sems.at[1 + place])
    total = loss_in[...] + (1.0 - u_is_image.astype(F32)) * last[:, width:].astype(F32)
    loss_rows[...] = jnp.sum(jnp.transpose(total), axis=0) / (SPAN * total.shape[0])
    output(lambda copy: copy.wait(), done_u, whole, u_is_image, sems.at[0])
    for place, part in enumerate(parts):
        output(lambda copy: copy.wait(), done_w, part, jnp.logical_not(u_is_image), sems.at[1 + place])


VMEM = pl.BlockSpec(memory_space=pltpu.VMEM)
ANY = pl.BlockSpec(memory_space=pl.ANY)


def call(kernel, in_specs, args, out_specs, outs, name, scratch=(), flops=1):
    return pl.pallas_call(
        kernel,
        out_shape=outs,
        in_specs=in_specs,
        out_specs=out_specs,
        scratch_shapes=list(scratch),
        name=name,
        cost_estimate=pl.CostEstimate(flops=flops, bytes_accessed=1, transcendentals=0),
        compiler_params=pltpu.CompilerParams(vmem_limit_bytes=VMEM_LIMIT),
    )(*args)


def local(image, text, score_scaling, score_shift):
    rows, width = image.shape
    block = jax.ShapeDtypeStruct((rows, width), BF16)
    pair = jax.ShapeDtypeStruct((2 * rows, width), BF16)
    sums = jax.ShapeDtypeStruct((rows, width), F32)
    column = jax.ShapeDtypeStruct((rows, 1), F32)
    partial = jax.ShapeDtypeStruct((rows, 128), F32)
    line = jax.ShapeDtypeStruct((rows,), F32)
    raw = pltpu.VMEM((rows, width), BF16)
    copies = pltpu.SemaphoreType.DMA((7,))

    def in_hbm(*arrays):
        return [pltpu.with_memory_space_constraint(x, pltpu.HBM) for x in arrays]


    def pick(when_outer, when_inner, out):
        sem = pltpu.SemaphoreType.DMA
        return call(
            pick_kernel, [ANY] * 2, (when_outer, when_inner), [ANY], (out,), "pick", (sem,)
        )[0]

    def compute(kernel, args, outs, name, scratch, flops=1):
        in_specs = [VMEM] * (1 + len(args))
        out_specs = [VMEM] * len(outs)
        return call(kernel, in_specs, (scalars, *args), out_specs, outs, name, scratch, flops)

    u, w = call(
        sort_kernel, [ANY] * 2, in_hbm(image, text), [VMEM] * 2, (block, block), "sort", (copies,)
    )
    slot1 = send(w, CORE_SWAP)
    slot2 = send(u, GROUP_SHIFT)
    slot3 = send(pick(slot1, u, block), X_SWAP)
    slot4 = send(slot3, GROUP_SHIFT)
    slot5 = send(pick(w, slot2, pltpu.HBM((rows, width), BF16)), X_SWAP)
    slot3, score_scaling, score_shift = lax.optimization_barrier((slot3, score_scaling, score_shift))
    first = lax.broadcasted_iota(jnp.int32, (8, 128), 0) == 0
    scalars = jnp.where(first, score_scaling, score_shift)
    z_pair, unit_u, unit_other, inverse_u, inverse_other, grad_u, part_w, loss = compute(
        near_kernel,
        (*in_hbm(image, text, slot1, slot2), slot3),
        (pair, sums, sums, column, column, sums, sums, partial),
        "near_blocks",
        (pltpu.VMEM((2 * rows, width), BF16), raw) + (pltpu.VMEM((rows, width), F32),) * 2,
    )
    grad_u, loss, for_partner = compute(
        fifth_kernel,
        (pltpu.with_memory_space_constraint(slot5, pltpu.VMEM), z_pair, unit_other, inverse_other, grad_u, loss),
        (sums, partial, jax.ShapeDtypeStruct((rows, width + 128), BF16)),
        "fifth_block",
        (),
    )
    last = send(for_partner, CORE_SWAP)
    done_u, loss = compute(
        u_kernel,
        (pltpu.with_memory_space_constraint(slot4, pltpu.VMEM), z_pair, grad_u, loss, unit_u, inverse_u),
        (block, partial),
        "finish_u",
        (),
        10**10,
    )
    image_grad, text_grad, loss_rows = call(
        w_kernel,
        [VMEM] * 4,
        (last, part_w, loss, done_u),
        [ANY, ANY, VMEM],
        (block, block, line),
        "finish_w",
        (raw, copies),
    )
    return loss_rows, image_grad, text_grad


def solution(mesh):
    in_specs = (P(AXES, None), P(AXES, None), P(), P())
    out_specs = (P(AXES), P(AXES, None), P(AXES, None))
    return jax.shard_map(local, mesh=mesh, in_specs=in_specs, out_specs=out_specs, check_vma=False)
```

```python
import jax
import jax.numpy as jnp
from jax import lax
from jax.experimental import pallas as pl
from jax.experimental.pallas import tpu as pltpu
from jax.sharding import PartitionSpec as P

SPAN = 4
GROUP = 4
AXES = ("blk", "inner")
F32 = jnp.float32
BF16 = jnp.bfloat16
VMEM_LIMIT = 28 * 1024 * 1024

X_SWAP = {0: (1, 0), 1: (0, 0), 2: (3, 0), 3: (2, 0)}
CORE_SWAP = {0: (2, 0), 1: (3, 0), 2: (0, 0), 3: (1, 0)}
GROUP_SHIFT = {0: (2, -1), 1: (3, -1), 2: (0, 1), 3: (1, 1)}


def send(value, moves):
    count = lax.axis_size(AXES)
    groups = count // GROUP
    pairs = [
        (g * GROUP + role, (g + step) % groups * GROUP + to)
        for g in range(groups)
        for role, (to, step) in moves.items()
    ]
    return lax.ppermute(value, AXES, pairs)


def unit_rows(raw):
    values = raw.astype(F32)
    inverse = 1.0 / jnp.sqrt(jnp.sum(values * values, axis=1, keepdims=True) + 1e-06)
    return values * inverse, inverse


def sigmoid_of(p):
    whole = 1.0 + p
    guess = pl.reciprocal(whole, approx=True)
    guess = guess * (2.0 - whole * guess)
    return p * (guess * (2.0 - whole * guess))


def log1p_of(p):
    below = p * (1.0 - p * (0.5 - p * (1.0 / 3.0)))
    return jnp.where(p < 0.015625, below, jnp.log(1.0 + p))


def softplus_lanes(p):
    total = None
    parts = [p[:, start : start + 128] for start in range(0, p.shape[1], 128)]
    for first in range(0, len(parts), 3):
        joint = parts[first]
        for part in parts[first + 1 : first + 3]:
            joint = joint + part + joint * part
        value = log1p_of(joint)
        total = value if total is None else total + value
    return total


def dot_nt(a, b):
    return lax.dot_general(a, b, (((1,), (1,)), ((), ())), preferred_element_type=F32)


def dot_nn(a, b):
    return lax.dot_general(a, b, (((1,), (0,)), ((), ())), preferred_element_type=F32)


def dot_tn(a, b):
    return lax.dot_general(a, b, (((0,), (0,)), ((), ())), preferred_element_type=F32)


def pair_step(own, blocks, scale, shift, work):
    rows = blocks[0].shape[0]
    for place, raw in enumerate(blocks):
        work[place * rows : (place + 1) * rows] = unit_rows(raw)[0].astype(BF16)
    return terms(own, work[: len(blocks) * rows], scale, shift)


def terms(own, others, scale, shift):
    half = own.shape[0] // 2
    scores = [dot_nt(own[:half], others), dot_nt(own[half:], others)]
    products, losses = [], []
    for score in scores:
        p = jnp.exp(scale * score + shift)
        coef = (sigmoid_of(p) * scale).astype(BF16)
        products.append(dot_nn(coef, others))
        losses.append(softplus_lanes(p))
    return jnp.concatenate(products), jnp.concatenate(losses)


def raw_terms(own, raw, scale, shift):
    values = raw.astype(F32)
    inverse = 1.0 / jnp.sqrt(jnp.sum(values * values, axis=1, keepdims=True) + 1e-06)
    factor = scale * jnp.transpose(jnp.broadcast_to(inverse, (raw.shape[0], 128)))[:1]
    size = raw.shape[0] // 2
    chunks = [slice(start, start + size) for start in range(0, own.shape[0], size)]
    score = dot_nt(own[chunks[0]], raw)
    for place, chunk in enumerate(chunks):
        p = jnp.exp(factor * score + shift)
        if place + 1 < len(chunks):
            score = dot_nt(own[chunks[place + 1]], raw)
        yield chunk, dot_nn((sigmoid_of(p) * factor).astype(BF16), raw), softplus_lanes(p)


def project(unit, inverse, grad):
    return (grad - unit * jnp.sum(unit * grad, axis=1, keepdims=True)) * inverse


def row_parts(rows, wanted):
    count = wanted if rows % (16 * wanted) == 0 else 1
    return [pl.ds(place * (rows // count), rows // count) for place in range(count)]


def scalar_pair(scalars):
    return scalars[0:1, 0:1], scalars[1:2, 0:1]


def image_is_u():
    return lax.rem(lax.axis_index("blk"), 2) == 0


def is_outer():
    return lax.rem(lax.axis_index("blk"), 2) == lax.axis_index("inner")


def sort_kernel(image, text, u, w, sems):
    def move(image_to, text_to):
        copies = []
        for source, target in ((image, image_to), (text, text_to)):
            for part in row_parts(image.shape[0], 3):
                sem = sems.at[len(copies)]
                copies.append(pltpu.make_async_copy(source.at[part], target.at[part], sem))
        for copy in copies:
            copy.start()
        for copy in copies:
            copy.wait()

    u_is_image = image_is_u()

    @pl.when(u_is_image)
    def _():
        move(u, w)

    @pl.when(jnp.logical_not(u_is_image))
    def _():
        move(w, u)


def pick_kernel(when_outer, when_inner, picked, sem):
    @pl.when(is_outer())
    def _():
        pltpu.async_copy(when_outer, picked, sem).wait()

    @pl.when(jnp.logical_not(is_outer()))
    def _():
        pltpu.async_copy(when_inner, picked, sem).wait()


def near_kernel(
    scalars, image, text, b1, b2, b3,
    z_pair, unit_u, unit_other, inverse_u, inverse_other, grad_u, part_w, loss, work, z_w, grad_w, unit_w,
):
    u_is_image = image_is_u()
    u_weight = u_is_image.astype(F32)
    scale, shift = scalar_pair(scalars)
    image_unit, image_inverse = unit_rows(image[...])
    text_unit, text_inverse = unit_rows(text[...])
    unit_u[...] = jnp.where(u_is_image, image_unit, text_unit)
    unit_w[...] = jnp.where(u_is_image, text_unit, image_unit)
    inverse_u[...] = jnp.where(u_is_image, image_inverse, text_inverse)
    inverse_w = jnp.where(u_is_image, text_inverse, image_inverse)
    unit_other[...], inverse_other[...] = unit_rows(b1[...])
    zi = image_unit.astype(BF16)
    zt = text_unit.astype(BF16)
    z_u = jnp.where(u_is_image, zi, zt)
    z_pair[: zi.shape[0]] = z_u
    z_w[...] = jnp.where(u_is_image, zt, zi)
    scores = scale * dot_nt(zi, zt) + shift
    rows = lax.broadcasted_iota(jnp.int32, scores.shape, 0)
    columns = lax.broadcasted_iota(jnp.int32, scores.shape, 1)
    sign = jnp.where(rows == columns, F32(-1.0), F32(1.0))
    p = jnp.exp(sign * scores)
    coef = (sign * sigmoid_of(p) * scale).astype(BF16)
    total = softplus_lanes(p)
    grad_image = dot_nn(coef, zt)
    grad_text = dot_tn(coef, zi)
    grad_u[...] = jnp.where(u_is_image, grad_image, grad_text)
    grad_w[...] = jnp.where(u_is_image, grad_text, grad_image)
    term, row_loss = pair_step(z_u, (b2[...],), scale, shift, work)
    grad_u[...] += term
    total = total + u_weight * row_loss
    term, row_loss = pair_step(z_w[...], (b1[...], b3[...]), scale, shift, work)
    z_pair[zi.shape[0] :] = work[: zi.shape[0]]
    part_w[...] = project(unit_w[...], inverse_w, grad_w[...] + term)
    loss[...] = total + (1.0 - u_weight) * row_loss


def fifth_kernel(
    scalars, b5, z_pair, unit_other, inverse_other, grad_in, loss_in, grad_u, loss, for_partner
):
    rows, width = b5.shape
    weight = image_is_u().astype(F32)
    for chunk, term, row_loss in raw_terms(z_pair, b5[...], *scalar_pair(scalars)):
        if chunk.start < rows:
            grad_u[chunk] = grad_in[chunk] + term
            loss[chunk] = loss_in[chunk] + weight * row_loss
        else:
            part = slice(chunk.start - rows, chunk.stop - rows)
            projected = project(unit_other[part], inverse_other[part], term)
            for_partner[part, :width] = projected.astype(BF16)
            for_partner[part, width:] = row_loss.astype(BF16)


def u_kernel(scalars, b4, z_pair, grad_u, loss_in, unit, inverse, done_u, loss):
    weight = image_is_u().astype(F32)
    own = z_pair.at[pl.ds(0, done_u.shape[0])]
    for chunk, term, row_loss in raw_terms(own, b4[...], *scalar_pair(scalars)):
        loss[chunk] = loss_in[chunk] + weight * row_loss
        done_u[chunk] = project(unit[chunk], inverse[chunk], grad_u[chunk] + term).astype(BF16)


def w_kernel(
    last, part_w, loss_in, done_u, image_grad, text_grad, loss_rows, done_w, sems
):
    u_is_image = image_is_u()
    parts = row_parts(done_w.shape[0], 6)

    def output(action, source, part, to_image, sem):
        @pl.when(to_image)
        def _():
            action(pltpu.make_async_copy(source.at[part], image_grad.at[part], sem))

        @pl.when(jnp.logical_not(to_image))
        def _():
            action(pltpu.make_async_copy(source.at[part], text_grad.at[part], sem))

    whole = pl.ds(0, done_w.shape[0])
    output(lambda copy: copy.start(), done_u, whole, u_is_image, sems.at[0])
    width = done_w.shape[1]
    for place, part in enumerate(parts):
        done_w[part] = (part_w[part] + last[part, :width].astype(F32)).astype(BF16)
        output(lambda copy: copy.start(), done_w, part, jnp.logical_not(u_is_image), sems.at[1 + place])
    total = loss_in[...] + (1.0 - u_is_image.astype(F32)) * last[:, width:].astype(F32)
    loss_rows[...] = jnp.sum(jnp.transpose(total), axis=0) / (SPAN * total.shape[0])
    output(lambda copy: copy.wait(), done_u, whole, u_is_image, sems.at[0])
    for place, part in enumerate(parts):
        output(lambda copy: copy.wait(), done_w, part, jnp.logical_not(u_is_image), sems.at[1 + place])


VMEM = pl.BlockSpec(memory_space=pltpu.VMEM)
ANY = pl.BlockSpec(memory_space=pl.ANY)


def call(kernel, in_specs, args, out_specs, outs, name, scratch=(), flops=1):
    return pl.pallas_call(
        kernel,
        out_shape=outs,
        in_specs=in_specs,
        out_specs=out_specs,
        scratch_shapes=list(scratch),
        name=name,
        cost_estimate=pl.CostEstimate(flops=flops, bytes_accessed=1, transcendentals=0),
        compiler_params=pltpu.CompilerParams(vmem_limit_bytes=VMEM_LIMIT),
    )(*args)


def local(image, text, score_scaling, score_shift):
    rows, width = image.shape
    block = jax.ShapeDtypeStruct((rows, width), BF16)
    pair = jax.ShapeDtypeStruct((2 * rows, width), BF16)
    sums = jax.ShapeDtypeStruct((rows, width), F32)
    column = jax.ShapeDtypeStruct((rows, 1), F32)
    partial = jax.ShapeDtypeStruct((rows, 128), F32)
    line = jax.ShapeDtypeStruct((rows,), F32)
    raw = pltpu.VMEM((rows, width), BF16)
    copies = pltpu.SemaphoreType.DMA((7,))

    def in_hbm(*arrays):
        return [pltpu.with_memory_space_constraint(x, pltpu.HBM) for x in arrays]


    def pick(when_outer, when_inner, out):
        sem = pltpu.SemaphoreType.DMA
        return call(
            pick_kernel, [ANY] * 2, (when_outer, when_inner), [ANY], (out,), "pick", (sem,)
        )[0]

    def compute(kernel, args, outs, name, scratch, flops=1):
        in_specs = [VMEM] * (1 + len(args))
        out_specs = [VMEM] * len(outs)
        return call(kernel, in_specs, (scalars, *args), out_specs, outs, name, scratch, flops)

    u, w = call(
        sort_kernel, [ANY] * 2, in_hbm(image, text), [VMEM] * 2, (block, block), "sort", (copies,)
    )
    slot1 = send(w, CORE_SWAP)
    slot2 = send(u, GROUP_SHIFT)
    slot3 = send(pick(slot1, u, block), X_SWAP)
    slot4 = send(slot3, GROUP_SHIFT)
    slot5 = send(pick(w, slot2, pltpu.HBM((rows, width), BF16)), X_SWAP)
    slot3, score_scaling, score_shift = lax.optimization_barrier((slot3, score_scaling, score_shift))
    first = lax.broadcasted_iota(jnp.int32, (8, 128), 0) == 0
    scalars = jnp.where(first, score_scaling, score_shift)
    z_pair, unit_u, unit_other, inverse_u, inverse_other, grad_u, part_w, loss = compute(
        near_kernel,
        (*in_hbm(image, text, slot1, slot2), slot3),
        (pair, sums, sums, column, column, sums, sums, partial),
        "near_blocks",
        (pltpu.VMEM((2 * rows, width), BF16), raw) + (pltpu.VMEM((rows, width), F32),) * 2,
    )
    grad_u, loss, for_partner = compute(
        fifth_kernel,
        (pltpu.with_memory_space_constraint(slot5, pltpu.VMEM), z_pair, unit_other, inverse_other, grad_u, loss),
        (sums, partial, jax.ShapeDtypeStruct((rows, width + 128), BF16)),
        "fifth_block",
        (),
    )
    last = send(for_partner, CORE_SWAP)
    done_u, loss = compute(
        u_kernel,
        (pltpu.with_memory_space_constraint(slot4, pltpu.VMEM), z_pair, grad_u, loss, unit_u, inverse_u),
        (block, partial),
        "finish_u",
        (),
        10**10,
    )
    image_grad, text_grad, loss_rows = call(
        w_kernel,
        [VMEM] * 4,
        (last, part_w, loss, done_u),
        [ANY, ANY, VMEM],
        (block, block, line),
        "finish_w",
        (raw, copies),
    )
    return loss_rows, image_grad, text_grad


def solution(mesh):
    in_specs = (P(AXES, None), P(AXES, None), P(), P())
    out_specs = (P(AXES), P(AXES, None), P(AXES, None))
    return jax.shard_map(local, mesh=mesh, in_specs=in_specs, out_specs=out_specs, check_vma=False)
```

```python
import jax
import jax.numpy as jnp
from jax import lax
from jax.experimental import pallas as pl
from jax.experimental.pallas import tpu as pltpu
from jax.sharding import PartitionSpec as P

SPAN = 4
GROUP = 4
AXES = ("blk", "inner")
F32 = jnp.float32
BF16 = jnp.bfloat16
VMEM_LIMIT = 28 * 1024 * 1024

X_SWAP = {0: (1, 0), 1: (0, 0), 2: (3, 0), 3: (2, 0)}
CORE_SWAP = {0: (2, 0), 1: (3, 0), 2: (0, 0), 3: (1, 0)}
GROUP_SHIFT = {0: (2, -1), 1: (3, -1), 2: (0, 1), 3: (1, 1)}


def send(value, moves):
    count = lax.axis_size(AXES)
    groups = count // GROUP
    pairs = [
        (g * GROUP + role, (g + step) % groups * GROUP + to)
        for g in range(groups)
        for role, (to, step) in moves.items()
    ]
    return lax.ppermute(value, AXES, pairs)


def unit_rows(raw):
    values = raw.astype(F32)
    inverse = 1.0 / jnp.sqrt(jnp.sum(values * values, axis=1, keepdims=True) + 1e-06)
    return values * inverse, inverse


def sigmoid_of(p):
    whole = 1.0 + p
    guess = pl.reciprocal(whole, approx=True)
    guess = guess * (2.0 - whole * guess)
    return p * (guess * (2.0 - whole * guess))


def log1p_of(p):
    below = p * (1.0 - p * (0.5 - p * (1.0 / 3.0)))
    return jnp.where(p < 0.015625, below, jnp.log(1.0 + p))


def softplus_lanes(p):
    total = None
    parts = [p[:, start : start + 128] for start in range(0, p.shape[1], 128)]
    for first in range(0, len(parts), 3):
        joint = parts[first]
        for part in parts[first + 1 : first + 3]:
            joint = joint + part + joint * part
        value = log1p_of(joint)
        total = value if total is None else total + value
    return total


def dot_nt(a, b):
    return lax.dot_general(a, b, (((1,), (1,)), ((), ())), preferred_element_type=F32)


def dot_nn(a, b):
    return lax.dot_general(a, b, (((1,), (0,)), ((), ())), preferred_element_type=F32)


def dot_tn(a, b):
    return lax.dot_general(a, b, (((0,), (0,)), ((), ())), preferred_element_type=F32)


def pair_step(own, blocks, scale, shift, work):
    rows = blocks[0].shape[0]
    for place, raw in enumerate(blocks):
        work[place * rows : (place + 1) * rows] = unit_rows(raw)[0].astype(BF16)
    return terms(own, work[: len(blocks) * rows], scale, shift)


def terms(own, others, scale, shift):
    half = own.shape[0] // 2
    scores = [dot_nt(own[:half], others), dot_nt(own[half:], others)]
    products, losses = [], []
    for score in scores:
        p = jnp.exp(scale * score + shift)
        coef = (sigmoid_of(p) * scale).astype(BF16)
        products.append(dot_nn(coef, others))
        losses.append(softplus_lanes(p))
    return jnp.concatenate(products), jnp.concatenate(losses)


def raw_terms(own, raw, scale, shift):
    values = raw.astype(F32)
    inverse = 1.0 / jnp.sqrt(jnp.sum(values * values, axis=1, keepdims=True) + 1e-06)
    factor = scale * jnp.transpose(jnp.broadcast_to(inverse, (raw.shape[0], 128)))[:1]
    size = raw.shape[0] // (3 if raw.shape[0] % 48 == 0 else 1)
    chunks = [slice(start, start + size) for start in range(0, own.shape[0], size)]
    score = dot_nt(own[chunks[0]], raw)
    for place, chunk in enumerate(chunks):
        p = jnp.exp(factor * score + shift)
        if place + 1 < len(chunks):
            score = dot_nt(own[chunks[place + 1]], raw)
        yield chunk, dot_nn((sigmoid_of(p) * factor).astype(BF16), raw), softplus_lanes(p)


def project(unit, inverse, grad):
    return (grad - unit * jnp.sum(unit * grad, axis=1, keepdims=True)) * inverse


def row_parts(rows, wanted):
    count = wanted if rows % (16 * wanted) == 0 else 1
    return [pl.ds(place * (rows // count), rows // count) for place in range(count)]


def scalar_pair(scalars):
    return scalars[0:1, 0:1], scalars[1:2, 0:1]


def image_is_u():
    return lax.rem(lax.axis_index("blk"), 2) == 0


def is_outer():
    return lax.rem(lax.axis_index("blk"), 2) == lax.axis_index("inner")


def sort_kernel(image, text, u, w, sems):
    def move(image_to, text_to):
        copies = []
        for source, target in ((image, image_to), (text, text_to)):
            for part in row_parts(image.shape[0], 3):
                sem = sems.at[len(copies)]
                copies.append(pltpu.make_async_copy(source.at[part], target.at[part], sem))
        for copy in copies:
            copy.start()
        for copy in copies:
            copy.wait()

    u_is_image = image_is_u()

    @pl.when(u_is_image)
    def _():
        move(u, w)

    @pl.when(jnp.logical_not(u_is_image))
    def _():
        move(w, u)


def pick_kernel(when_outer, when_inner, picked, sem):
    @pl.when(is_outer())
    def _():
        pltpu.async_copy(when_outer, picked, sem).wait()

    @pl.when(jnp.logical_not(is_outer()))
    def _():
        pltpu.async_copy(when_inner, picked, sem).wait()


def near_kernel(
    scalars, image, text, b1, b2, b3,
    z_pair, unit_u, unit_other, inverse_u, inverse_other, grad_u, part_w, loss, work, z_w, grad_w, unit_w,
):
    u_is_image = image_is_u()
    u_weight = u_is_image.astype(F32)
    scale, shift = scalar_pair(scalars)
    image_unit, image_inverse = unit_rows(image[...])
    text_unit, text_inverse = unit_rows(text[...])
    unit_u[...] = jnp.where(u_is_image, image_unit, text_unit)
    unit_w[...] = jnp.where(u_is_image, text_unit, image_unit)
    inverse_u[...] = jnp.where(u_is_image, image_inverse, text_inverse)
    inverse_w = jnp.where(u_is_image, text_inverse, image_inverse)
    unit_other[...], inverse_other[...] = unit_rows(b1[...])
    zi = image_unit.astype(BF16)
    zt = text_unit.astype(BF16)
    z_u = jnp.where(u_is_image, zi, zt)
    z_pair[: zi.shape[0]] = z_u
    z_w[...] = jnp.where(u_is_image, zt, zi)
    scores = scale * dot_nt(zi, zt) + shift
    rows = lax.broadcasted_iota(jnp.int32, scores.shape, 0)
    columns = lax.broadcasted_iota(jnp.int32, scores.shape, 1)
    sign = jnp.where(rows == columns, F32(-1.0), F32(1.0))
    p = jnp.exp(sign * scores)
    coef = (sign * sigmoid_of(p) * scale).astype(BF16)
    total = softplus_lanes(p)
    grad_image = dot_nn(coef, zt)
    grad_text = dot_tn(coef, zi)
    grad_u[...] = jnp.where(u_is_image, grad_image, grad_text)
    grad_w[...] = jnp.where(u_is_image, grad_text, grad_image)
    term, row_loss = pair_step(z_u, (b2[...],), scale, shift, work)
    grad_u[...] += term
    total = total + u_weight * row_loss
    term, row_loss = pair_step(z_w[...], (b1[...], b3[...]), scale, shift, work)
    z_pair[zi.shape[0] :] = work[: zi.shape[0]]
    part_w[...] = project(unit_w[...], inverse_w, grad_w[...] + term)
    loss[...] = total + (1.0 - u_weight) * row_loss


def fifth_kernel(
    scalars, b5, z_pair, unit_other, inverse_other, grad_in, loss_in, grad_u, loss, for_partner
):
    rows, width = b5.shape
    weight = image_is_u().astype(F32)
    for chunk, term, row_loss in raw_terms(z_pair, b5[...], *scalar_pair(scalars)):
        if chunk.start < rows:
            grad_u[chunk] = grad_in[chunk] + term
            loss[chunk] = loss_in[chunk] + weight * row_loss
        else:
            part = slice(chunk.start - rows, chunk.stop - rows)
            projected = project(unit_other[part], inverse_other[part], term)
            for_partner[part, :width] = projected.astype(BF16)
            for_partner[part, width:] = row_loss.astype(BF16)


def u_kernel(scalars, b4, z_pair, grad_u, loss_in, unit, inverse, done_u, loss):
    weight = image_is_u().astype(F32)
    own = z_pair.at[pl.ds(0, done_u.shape[0])]
    for chunk, term, row_loss in raw_terms(own, b4[...], *scalar_pair(scalars)):
        loss[chunk] = loss_in[chunk] + weight * row_loss
        done_u[chunk] = project(unit[chunk], inverse[chunk], grad_u[chunk] + term).astype(BF16)


def w_kernel(
    last, part_w, loss_in, done_u, image_grad, text_grad, loss_rows, done_w, sems
):
    u_is_image = image_is_u()
    parts = row_parts(done_w.shape[0], 6)

    def output(action, source, part, to_image, sem):
        @pl.when(to_image)
        def _():
            action(pltpu.make_async_copy(source.at[part], image_grad.at[part], sem))

        @pl.when(jnp.logical_not(to_image))
        def _():
            action(pltpu.make_async_copy(source.at[part], text_grad.at[part], sem))

    thirds = row_parts(done_w.shape[0], 3)
    for place, part in enumerate(thirds):
        output(lambda copy: copy.start(), done_u, part, u_is_image, sems.at[place])
    width = done_w.shape[1]
    for place, part in enumerate(parts):
        done_w[part] = (part_w[part] + last[part, :width].astype(F32)).astype(BF16)
        output(lambda copy: copy.start(), done_w, part, jnp.logical_not(u_is_image), sems.at[3 + place])
    total = loss_in[...] + (1.0 - u_is_image.astype(F32)) * last[:, width:].astype(F32)
    loss_rows[...] = jnp.sum(jnp.transpose(total), axis=0) / (SPAN * total.shape[0])
    for place, part in enumerate(thirds):
        output(lambda copy: copy.wait(), done_u, part, u_is_image, sems.at[place])
    for place, part in enumerate(parts):
        output(lambda copy: copy.wait(), done_w, part, jnp.logical_not(u_is_image), sems.at[3 + place])


VMEM = pl.BlockSpec(memory_space=pltpu.VMEM)
ANY = pl.BlockSpec(memory_space=pl.ANY)


def call(kernel, in_specs, args, out_specs, outs, name, scratch=(), flops=1):
    return pl.pallas_call(
        kernel,
        out_shape=outs,
        in_specs=in_specs,
        out_specs=out_specs,
        scratch_shapes=list(scratch),
        name=name,
        cost_estimate=pl.CostEstimate(flops=flops, bytes_accessed=1, transcendentals=0),
        compiler_params=pltpu.CompilerParams(vmem_limit_bytes=VMEM_LIMIT),
    )(*args)


def local(image, text, score_scaling, score_shift):
    rows, width = image.shape
    block = jax.ShapeDtypeStruct((rows, width), BF16)
    pair = jax.ShapeDtypeStruct((2 * rows, width), BF16)
    sums = jax.ShapeDtypeStruct((rows, width), F32)
    column = jax.ShapeDtypeStruct((rows, 1), F32)
    partial = jax.ShapeDtypeStruct((rows, 128), F32)
    line = jax.ShapeDtypeStruct((rows,), F32)
    raw = pltpu.VMEM((rows, width), BF16)
    copies = pltpu.SemaphoreType.DMA((9,))

    def in_hbm(*arrays):
        return [pltpu.with_memory_space_constraint(x, pltpu.HBM) for x in arrays]


    def pick(when_outer, when_inner, out):
        sem = pltpu.SemaphoreType.DMA
        return call(
            pick_kernel, [ANY] * 2, (when_outer, when_inner), [ANY], (out,), "pick", (sem,)
        )[0]

    def compute(kernel, args, outs, name, scratch, flops=1):
        in_specs = [VMEM] * (1 + len(args))
        out_specs = [VMEM] * len(outs)
        return call(kernel, in_specs, (scalars, *args), out_specs, outs, name, scratch, flops)

    u, w = call(
        sort_kernel, [ANY] * 2, in_hbm(image, text), [VMEM] * 2, (block, block), "sort", (copies,)
    )
    slot1 = send(w, CORE_SWAP)
    slot2 = send(u, GROUP_SHIFT)
    slot3 = send(pick(slot1, u, block), X_SWAP)
    slot4 = send(slot3, GROUP_SHIFT)
    slot5 = send(pick(w, slot2, pltpu.HBM((rows, width), BF16)), X_SWAP)
    slot3, score_scaling, score_shift = lax.optimization_barrier((slot3, score_scaling, score_shift))
    first = lax.broadcasted_iota(jnp.int32, (8, 128), 0) == 0
    scalars = jnp.where(first, score_scaling, score_shift)
    z_pair, unit_u, unit_other, inverse_u, inverse_other, grad_u, part_w, loss = compute(
        near_kernel,
        (*in_hbm(image, text, slot1, slot2), slot3),
        (pair, sums, sums, column, column, sums, sums, partial),
        "near_blocks",
        (pltpu.VMEM((2 * rows, width), BF16), raw) + (pltpu.VMEM((rows, width), F32),) * 2,
    )
    grad_u, loss, for_partner = compute(
        fifth_kernel,
        (pltpu.with_memory_space_constraint(slot5, pltpu.VMEM), z_pair, unit_other, inverse_other, grad_u, loss),
        (sums, partial, jax.ShapeDtypeStruct((rows, width + 128), BF16)),
        "fifth_block",
        (),
    )
    last = send(for_partner, CORE_SWAP)
    done_u, loss = compute(
        u_kernel,
        (pltpu.with_memory_space_constraint(slot4, pltpu.VMEM), z_pair, grad_u, loss, unit_u, inverse_u),
        (block, partial),
        "finish_u",
        (),
        10**10,
    )
    image_grad, text_grad, loss_rows = call(
        w_kernel,
        [VMEM] * 4,
        (last, part_w, loss, done_u),
        [ANY, ANY, VMEM],
        (block, block, line),
        "finish_w",
        (raw, copies),
    )
    return loss_rows, image_grad, text_grad


def solution(mesh):
    in_specs = (P(AXES, None), P(AXES, None), P(), P())
    out_specs = (P(AXES), P(AXES, None), P(AXES, None))
    return jax.shard_map(local, mesh=mesh, in_specs=in_specs, out_specs=out_specs, check_vma=False)
```

```python
import jax
import jax.numpy as jnp
from jax import lax
from jax.experimental import pallas as pl
from jax.experimental.pallas import tpu as pltpu
from jax.sharding import PartitionSpec as P

SPAN = 4
GROUP = 4
AXES = ("blk", "inner")
F32 = jnp.float32
BF16 = jnp.bfloat16
VMEM_LIMIT = 28 * 1024 * 1024

X_SWAP = {0: (1, 0), 1: (0, 0), 2: (3, 0), 3: (2, 0)}
CORE_SWAP = {0: (2, 0), 1: (3, 0), 2: (0, 0), 3: (1, 0)}
GROUP_SHIFT = {0: (2, -1), 1: (3, -1), 2: (0, 1), 3: (1, 1)}


def send(value, moves):
    count = lax.axis_size(AXES)
    groups = count // GROUP
    pairs = [
        (g * GROUP + role, (g + step) % groups * GROUP + to)
        for g in range(groups)
        for role, (to, step) in moves.items()
    ]
    return lax.ppermute(value, AXES, pairs)


def unit_rows(raw):
    values = raw.astype(F32)
    inverse = 1.0 / jnp.sqrt(jnp.sum(values * values, axis=1, keepdims=True) + 1e-06)
    return values * inverse, inverse


def sigmoid_of(p):
    whole = 1.0 + p
    guess = pl.reciprocal(whole, approx=True)
    guess = guess * (2.0 - whole * guess)
    return p * (guess * (2.0 - whole * guess))


def log1p_of(p):
    below = p * (1.0 - p * (0.5 - p * (1.0 / 3.0)))
    return jnp.where(p < 0.015625, below, jnp.log(1.0 + p))


def softplus_lanes(p):
    total = None
    parts = [p[:, start : start + 128] for start in range(0, p.shape[1], 128)]
    for first in range(0, len(parts), 3):
        joint = parts[first]
        for part in parts[first + 1 : first + 3]:
            joint = joint + part + joint * part
        value = log1p_of(joint)
        total = value if total is None else total + value
    return total


def dot_nt(a, b):
    return lax.dot_general(a, b, (((1,), (1,)), ((), ())), preferred_element_type=F32)


def dot_nn(a, b):
    return lax.dot_general(a, b, (((1,), (0,)), ((), ())), preferred_element_type=F32)


def dot_tn(a, b):
    return lax.dot_general(a, b, (((0,), (0,)), ((), ())), preferred_element_type=F32)


def pair_step(own, blocks, scale, shift, work):
    rows = blocks[0].shape[0]
    for place, raw in enumerate(blocks):
        work[place * rows : (place + 1) * rows] = unit_rows(raw)[0].astype(BF16)
    return terms(own, work[: len(blocks) * rows], scale, shift)


def terms(own, others, scale, shift):
    half = own.shape[0] // 2
    scores = [dot_nt(own[:half], others), dot_nt(own[half:], others)]
    products, losses = [], []
    for score in scores:
        p = jnp.exp(scale * score + shift)
        coef = (sigmoid_of(p) * scale).astype(BF16)
        products.append(dot_nn(coef, others))
        losses.append(softplus_lanes(p))
    return jnp.concatenate(products), jnp.concatenate(losses)


def raw_terms(own, raw, scale, shift):
    values = raw.astype(F32)
    inverse = 1.0 / jnp.sqrt(jnp.sum(values * values, axis=1, keepdims=True) + 1e-06)
    factor = scale * jnp.transpose(jnp.broadcast_to(inverse, (raw.shape[0], 128)))[:1]
    size = own.shape[0] // 2
    chunks = [slice(start, start + size) for start in range(0, own.shape[0], size)]
    score = dot_nt(own[chunks[0]], raw)
    for place, chunk in enumerate(chunks):
        p = jnp.exp(factor * score + shift)
        if place + 1 < len(chunks):
            score = dot_nt(own[chunks[place + 1]], raw)
        yield chunk, dot_nn((sigmoid_of(p) * factor).astype(BF16), raw), softplus_lanes(p)


def project(unit, inverse, grad):
    return (grad - unit * jnp.sum(unit * grad, axis=1, keepdims=True)) * inverse


def row_parts(rows, wanted):
    count = wanted if rows % (16 * wanted) == 0 else 1
    return [pl.ds(place * (rows // count), rows // count) for place in range(count)]


def scalar_pair(scalars):
    return scalars[0:1, 0:1], scalars[1:2, 0:1]


def image_is_u():
    return lax.rem(lax.axis_index("blk"), 2) == 0


def is_outer():
    return lax.rem(lax.axis_index("blk"), 2) == lax.axis_index("inner")


def sort_kernel(image, text, u, w, sems):
    def move(image_to, text_to):
        copies = []
        for source, target in ((image, image_to), (text, text_to)):
            for part in row_parts(image.shape[0], 3):
                sem = sems.at[len(copies)]
                copies.append(pltpu.make_async_copy(source.at[part], target.at[part], sem))
        for copy in copies:
            copy.start()
        for copy in copies:
            copy.wait()

    u_is_image = image_is_u()

    @pl.when(u_is_image)
    def _():
        move(u, w)

    @pl.when(jnp.logical_not(u_is_image))
    def _():
        move(w, u)


def pick_kernel(when_outer, when_inner, picked, sem):
    @pl.when(is_outer())
    def _():
        pltpu.async_copy(when_outer, picked, sem).wait()

    @pl.when(jnp.logical_not(is_outer()))
    def _():
        pltpu.async_copy(when_inner, picked, sem).wait()


def near_kernel(
    scalars, image, text, b1, b2, b3,
    z_pair, unit_u, unit_other, inverse_u, inverse_other, grad_u, part_w, loss, work, z_w, grad_w, unit_w,
):
    u_is_image = image_is_u()
    u_weight = u_is_image.astype(F32)
    scale, shift = scalar_pair(scalars)
    image_unit, image_inverse = unit_rows(image[...])
    text_unit, text_inverse = unit_rows(text[...])
    unit_u[...] = jnp.where(u_is_image, image_unit, text_unit)
    unit_w[...] = jnp.where(u_is_image, text_unit, image_unit)
    inverse_u[...] = jnp.where(u_is_image, image_inverse, text_inverse)
    inverse_w = jnp.where(u_is_image, text_inverse, image_inverse)
    unit_other[...], inverse_other[...] = unit_rows(b1[...])
    zi = image_unit.astype(BF16)
    zt = text_unit.astype(BF16)
    z_u = jnp.where(u_is_image, zi, zt)
    z_pair[: zi.shape[0]] = z_u
    z_w[...] = jnp.where(u_is_image, zt, zi)
    scores = scale * dot_nt(zi, zt) + shift
    rows = lax.broadcasted_iota(jnp.int32, scores.shape, 0)
    columns = lax.broadcasted_iota(jnp.int32, scores.shape, 1)
    sign = jnp.where(rows == columns, F32(-1.0), F32(1.0))
    p = jnp.exp(sign * scores)
    coef = (sign * sigmoid_of(p) * scale).astype(BF16)
    total = softplus_lanes(p)
    grad_image = dot_nn(coef, zt)
    grad_text = dot_tn(coef, zi)
    grad_u[...] = jnp.where(u_is_image, grad_image, grad_text)
    grad_w[...] = jnp.where(u_is_image, grad_text, grad_image)
    term, row_loss = pair_step(z_u, (b2[...],), scale, shift, work)
    grad_u[...] += term
    total = total + u_weight * row_loss
    term, row_loss = pair_step(z_w[...], (b1[...], b3[...]), scale, shift, work)
    z_pair[zi.shape[0] :] = work[: zi.shape[0]]
    part_w[...] = project(unit_w[...], inverse_w, grad_w[...] + term)
    loss[...] = total + (1.0 - u_weight) * row_loss


def fifth_kernel(
    scalars, b5, z_pair, unit_other, inverse_other, grad_in, loss_in, grad_u, loss, for_partner
):
    rows, width = b5.shape
    weight = image_is_u().astype(F32)
    for chunk, term, row_loss in raw_terms(z_pair, b5[...], *scalar_pair(scalars)):
        if chunk.start < rows:
            grad_u[chunk] = grad_in[chunk] + term
            loss[chunk] = loss_in[chunk] + weight * row_loss
        else:
            part = slice(chunk.start - rows, chunk.stop - rows)
            projected = project(unit_other[part], inverse_other[part], term)
            for_partner[part, :width] = projected.astype(BF16)
            for_partner[part, width:] = row_loss.astype(BF16)


def u_kernel(scalars, b4, z_pair, grad_u, loss_in, unit, inverse, done_u, loss):
    weight = image_is_u().astype(F32)
    own = z_pair.at[pl.ds(0, done_u.shape[0])]
    for chunk, term, row_loss in raw_terms(own, b4[...], *scalar_pair(scalars)):
        loss[chunk] = loss_in[chunk] + weight * row_loss
        done_u[chunk] = project(unit[chunk], inverse[chunk], grad_u[chunk] + term).astype(BF16)


def w_kernel(
    last, part_w, loss_in, done_u, image_grad, text_grad, loss_rows, done_w, sems
):
    u_is_image = image_is_u()
    parts = row_parts(done_w.shape[0], 6)

    def output(action, source, part, to_image, sem):
        @pl.when(to_image)
        def _():
            action(pltpu.make_async_copy(source.at[part], image_grad.at[part], sem))

        @pl.when(jnp.logical_not(to_image))
        def _():
            action(pltpu.make_async_copy(source.at[part], text_grad.at[part], sem))

    whole = pl.ds(0, done_w.shape[0])
    output(lambda copy: copy.start(), done_u, whole, u_is_image, sems.at[0])
    width = done_w.shape[1]
    for place, part in enumerate(parts):
        done_w[part] = (part_w[part] + last[part, :width].astype(F32)).astype(BF16)
        output(lambda copy: copy.start(), done_w, part, jnp.logical_not(u_is_image), sems.at[1 + place])
    total = loss_in[...] + (1.0 - u_is_image.astype(F32)) * last[:, width:].astype(F32)
    loss_rows[...] = jnp.sum(jnp.transpose(total), axis=0) / (SPAN * total.shape[0])
    output(lambda copy: copy.wait(), done_u, whole, u_is_image, sems.at[0])
    for place, part in enumerate(parts):
        output(lambda copy: copy.wait(), done_w, part, jnp.logical_not(u_is_image), sems.at[1 + place])


VMEM = pl.BlockSpec(memory_space=pltpu.VMEM)
ANY = pl.BlockSpec(memory_space=pl.ANY)


def call(kernel, in_specs, args, out_specs, outs, name, scratch=(), flops=1):
    return pl.pallas_call(
        kernel,
        out_shape=outs,
        in_specs=in_specs,
        out_specs=out_specs,
        scratch_shapes=list(scratch),
        name=name,
        cost_estimate=pl.CostEstimate(flops=flops, bytes_accessed=1, transcendentals=0),
        compiler_params=pltpu.CompilerParams(vmem_limit_bytes=VMEM_LIMIT),
    )(*args)


def local(image, text, score_scaling, score_shift):
    rows, width = image.shape
    block = jax.ShapeDtypeStruct((rows, width), BF16)
    pair = jax.ShapeDtypeStruct((2 * rows, width), BF16)
    sums = jax.ShapeDtypeStruct((rows, width), F32)
    column = jax.ShapeDtypeStruct((rows, 1), F32)
    partial = jax.ShapeDtypeStruct((rows, 128), F32)
    line = jax.ShapeDtypeStruct((rows,), F32)
    raw = pltpu.VMEM((rows, width), BF16)
    copies = pltpu.SemaphoreType.DMA((7,))

    def in_hbm(*arrays):
        return [pltpu.with_memory_space_constraint(x, pltpu.HBM) for x in arrays]


    def pick(when_outer, when_inner, out):
        sem = pltpu.SemaphoreType.DMA
        return call(
            pick_kernel, [ANY] * 2, (when_outer, when_inner), [ANY], (out,), "pick", (sem,)
        )[0]

    def compute(kernel, args, outs, name, scratch, flops=1):
        in_specs = [VMEM] * (1 + len(args))
        out_specs = [VMEM] * len(outs)
        return call(kernel, in_specs, (scalars, *args), out_specs, outs, name, scratch, flops)

    u, w = call(
        sort_kernel, [ANY] * 2, in_hbm(image, text), [VMEM] * 2, (block, block), "sort", (copies,)
    )
    slot1 = send(w, CORE_SWAP)
    slot2 = send(u, GROUP_SHIFT)
    slot3 = send(pick(slot1, u, block), X_SWAP)
    slot4 = send(slot3, GROUP_SHIFT)
    slot5 = send(pick(w, slot2, pltpu.HBM((rows, width), BF16)), X_SWAP)
    slot3, score_scaling, score_shift = lax.optimization_barrier((slot3, score_scaling, score_shift))
    first = lax.broadcasted_iota(jnp.int32, (8, 128), 0) == 0
    scalars = jnp.where(first, score_scaling, score_shift)
    z_pair, unit_u, unit_other, inverse_u, inverse_other, grad_u, part_w, loss = compute(
        near_kernel,
        (*in_hbm(image, text, slot1, slot2), slot3),
        (pair, sums, sums, column, column, sums, sums, partial),
        "near_blocks",
        (pltpu.VMEM((2 * rows, width), BF16), raw) + (pltpu.VMEM((rows, width), F32),) * 2,
    )
    grad_u, loss, for_partner = compute(
        fifth_kernel,
        (pltpu.with_memory_space_constraint(slot5, pltpu.VMEM), z_pair, unit_other, inverse_other, grad_u, loss),
        (sums, partial, jax.ShapeDtypeStruct((rows, width + 128), BF16)),
        "fifth_block",
        (),
    )
    last = send(for_partner, CORE_SWAP)
    done_u, loss = compute(
        u_kernel,
        (pltpu.with_memory_space_constraint(slot4, pltpu.VMEM), z_pair, grad_u, loss, unit_u, inverse_u),
        (block, partial),
        "finish_u",
        (),
        10**10,
    )
    image_grad, text_grad, loss_rows = call(
        w_kernel,
        [VMEM] * 4,
        (last, part_w, loss, done_u),
        [ANY, ANY, VMEM],
        (block, block, line),
        "finish_w",
        (raw, copies),
    )
    return loss_rows, image_grad, text_grad


def solution(mesh):
    in_specs = (P(AXES, None), P(AXES, None), P(), P())
    out_specs = (P(AXES), P(AXES, None), P(AXES, None))
    return jax.shard_map(local, mesh=mesh, in_specs=in_specs, out_specs=out_specs, check_vma=False)
```
